32 devices in a mesh: section: 2 (over y), ctx: 4 (over z), wsh: 4 (over x, core).
Axes of the slice: x: 2, y: 2, z: 4, core: 2. Of those that a mesh axis runs over, the one named last changes fastest.
Arguments:
- x_in: bfloat16 [2, 4, 2048, 1152], P(None, 'wsh', 'ctx'), may hold values from -6 to 6
- cotangent: bfloat16 [2, 4, 2048, 1152], P(None, 'wsh', 'ctx'), may hold values from -6 to 6
- w_qkv: bfloat16 [2, 1152, 1920], P('section', 'wsh'), may hold values from -0.1875 to 0.1875
- w_out: bfloat16 [2, 1152, 1152], P('section', None, 'wsh'), may hold values from -0.5 to 0.5
- w_gate_up: bfloat16 [2, 1152, 6144], P('section', 'wsh'), may hold values from -0.1875 to 0.1875
- w_down: bfloat16 [2, 3072, 1152], P('section', None, 'wsh'), may hold values from -0.109375 to 0.109375
- gains: bfloat16 [2, 2, 1152], P('section', None, 'wsh'), may hold values from 0.5 to 1.5
- order: int32 [2, 4], replicated, may hold values from 0 to 3, as said below
- visible: int32 [4, 4], replicated, may hold values from 0 to 1, as said below
- seq_ids: int32 [2, 4, 2048], P(None, 'wsh'), may hold values from 0 to 1, as said below
Outputs:
- activations: bfloat16 [2, 2, 4, 2048, 1152], P('section', None, 'wsh', 'ctx')
- input_grads: float32 [2, 2, 4, 2048, 1152], P('section', None, 'wsh', 'ctx')
- grad_qkv: float32 [2, 1152, 1920], P('section', ('ctx', 'wsh'))
- grad_out: float32 [2, 1152, 1152], P('section', None, ('ctx', 'wsh'))
- grad_gate_up: float32 [2, 1152, 6144], P('section', ('ctx', 'wsh'))
- grad_down: float32 [2, 3072, 1152], P('section', None, ('ctx', 'wsh'))
- grad_gains: float32 [2, 2, 1152], P('section', None, ('ctx', 'wsh'))
The draws below stay inside these ranges and needn't reach their ends.
Inputs may be any that keep to these rules, and one draw needn't show every extreme that they name: Row m lists every block number of 0 to 3 once: index c of ctx holds block order[m, c] of micro-batch m. Indices 0, 2 and 3 hold three blocks that one sequence of every stream reaches into. visible[i, i] is 1 and visible[i, j] is 0 for j > i; an earlier block j < i is visible to block i only where the table says so. `seq_ids`: taken in order of position, each micro-batch of each stream is 0 up to a cut and 1 from it on; each of the two sequences holds 512 tokens or more.
All inputs are finite; a program needn't handle non-finite values.
Results may differ from the reference program's by a relative error of at most 0.022.
Values may be sent and summed in bfloat16 or wider, within the bound.
A program may use at most 384 MiB of HBM per device.

```python
import jax
import jax.numpy as jnp
from jax import lax

D = 1152
H = 18
KV = 6
HD = 64
FF = 3072
MB = 2
LEN = 2048
BLOCK = 512
GROUPS = 4
QD = 1152
QKV = 1920
N_CTX = 4


def shared_side(key):
    side_key = jax.random.fold_in(key, 11)
    return jax.random.randint(side_key, (MB,), 0, 2).astype(jnp.int32)


def shared_order(key):
    side = shared_side(key)
    perm_key = jax.random.fold_in(key, 13)
    streams = jax.random.split(perm_key, MB)
    blocks = jnp.arange(N_CTX, dtype=jnp.int32)
    special_slot = (blocks == 0) | (blocks == N_CTX // 2) | (blocks == N_CTX - 1)
    slots = jnp.argsort(jnp.where(special_slot, 0, 1) * N_CTX + blocks, stable=True).astype(jnp.int32)

    def one_row(stream, long_first):
        scores = jax.random.permutation(stream, N_CTX).astype(jnp.int32)
        early_target = blocks < 3
        late_target = blocks >= N_CTX - 3
        target = jnp.where(long_first == 1, early_target, late_target)
        listing = jnp.argsort(jnp.where(target, 0, 1) * N_CTX + scores, stable=True).astype(jnp.int32)
        return jnp.zeros((N_CTX,), jnp.int32).at[slots].set(listing)
    return jax.vmap(one_row)(streams, side).astype(jnp.int32)


def draw_order(key, part):
    order = shared_order(key)
    return order.astype(jnp.int32)


def draw_seq_ids(key, part):
    order = shared_order(key)
    side = shared_side(key)
    key = jax.random.fold_in(key, 7)
    raw = jax.random.randint(key, (MB, GROUPS), 0, LEN // 4 + 1).astype(jnp.int32)
    low_cut = LEN // 4 + jnp.minimum(raw, LEN // 4 - 1)
    high_cut = LEN // 2 + 1 + jnp.minimum(raw, LEN // 4 - 1)
    cut_points = jnp.where(side[:, None] == 1, high_cut, low_cut)
    offsets = jnp.arange(LEN, dtype=jnp.int32)
    initial = order[:, offsets // BLOCK] * BLOCK + (offsets % BLOCK)[None, :]
    return (initial[:, None, :] >= cut_points[:, :, None]).astype(jnp.int32)


def draw_visible(key, part):
    key = jax.random.fold_in(key, 29)
    row_keys = jax.random.split(key, N_CTX)

    def one_row(row_key):
        return jax.random.permutation(row_key, N_CTX).astype(jnp.int32) % 2
    coin_flips = jax.vmap(one_row)(row_keys).astype(jnp.int32)
    row_index = jnp.arange(N_CTX, dtype=jnp.int32)[:, None]
    col_index = jnp.arange(N_CTX, dtype=jnp.int32)[None, :]
    lower = (col_index < row_index) & (coin_flips > 0)
    return jnp.where(row_index == col_index, 1, jnp.where(lower, 1, 0)).astype(jnp.int32)


def levels(key, dims, shards, smallest, high):
    factor_of = 1.0
    for position, blocks in shards:
        draws = jax.random.uniform(jax.random.fold_in(jax.random.fold_in(key, 6), position), (blocks,), jnp.float32, smallest / len(shards), high / len(shards))
        factor_of = factor_of * jnp.repeat(jnp.exp(draws), dims[position] // blocks).reshape((-1,) + (1,) * (len(dims) - 1 - position))
    return factor_of


def scatter_about(own_key, dims, deviation, reach, cuts=(), kind=jnp.bfloat16):
    gain = levels(own_key, dims, cuts, -0.22, 0.18) if cuts else 1.0
    values = jax.random.normal(own_key, dims, jnp.float32) * deviation * gain
    return jnp.minimum(jnp.maximum(values, -reach), reach).astype(kind)


def setup_inputs(seed: int = 0) -> dict:
    splits = jax.random.split(jax.random.key(seed), 11)
    x_in = scatter_about(splits[0], (MB, GROUPS, LEN, D), 1.0, 6.0, ((1, 4), (2, 4)))
    cotangent = scatter_about(splits[1], (MB, GROUPS, LEN, D), 1.0, 6.0, ((1, 4), (2, 4)))
    w_qkv = scatter_about(splits[2], (2, D, QKV), D ** -0.5, 0.1875, ((0, 2), (1, 4)))
    w_out = scatter_about(splits[3], (2, QD, D), (QD // 8) ** -0.5, 0.5, ((0, 2), (2, 4)))
    w_gate_up = scatter_about(splits[4], (2, D, 2 * FF), D ** -0.5, 0.1875, ((0, 2), (1, 4)))
    w_down = scatter_about(splits[5], (2, FF, D), FF ** -0.5, 0.109375, ((0, 2), (2, 4)))
    gains = jnp.clip(1.0 + 0.1 * jax.random.normal(splits[6], (2, 2, D), jnp.float32), 0.5, 1.5).astype(jnp.bfloat16)
    order = draw_order(jax.random.fold_in(splits[10], 71), 0)
    visible = draw_visible(jax.random.fold_in(splits[10], 71), 0)
    seq_ids = draw_seq_ids(jax.random.fold_in(splits[10], 71), 0)
    return {"x_in": x_in, "cotangent": cotangent, "w_qkv": w_qkv, "w_out": w_out, "w_gate_up": w_gate_up, "w_down": w_down, "gains": gains, "order": order, "visible": visible, "seq_ids": seq_ids}


NEG = -1e+30
EPS = 1e-05
HIGH = lax.Precision.HIGHEST

@jax.custom_vjp
def low(v):
    return lax.optimization_barrier(v.astype(jnp.bfloat16)).astype(jnp.float32)

@jax.custom_vjp
def low_back(v):
    return v

def low_keep(v):
    return (low(v), None)

def low_pass(kept, grad):
    return (grad,)

def back_keep(v):
    return (v, None)

def back_low(kept, grad):
    return (low(grad),)
low.defvjp(low_keep, low_pass)
low_back.defvjp(back_keep, back_low)

def rms_norm(hidden, gain_row):
    inverse = lax.rsqrt(lax.optimization_barrier(jnp.mean(hidden * hidden, axis=-1, keepdims=True)) + EPS)
    return hidden * inverse * gain_row

def rotation(positions):
    frequency = 10000.0 ** (-(jnp.arange(HD // 2, dtype=jnp.float32) * 2.0 / HD))
    angles = positions.astype(jnp.float32)[:, None] * frequency[None, :]
    return (jnp.cos(angles), jnp.sin(angles))

def rotate(vectors, cosine, sine):
    half_width = vectors.shape[-1] // 2
    first_half = vectors[..., :half_width]
    second_half = vectors[..., half_width:]
    cos_rows = cosine[:, None, :]
    sin_rows = sine[:, None, :]
    return jnp.concatenate([first_half * cos_rows - second_half * sin_rows, first_half * sin_rows + second_half * cos_rows], axis=-1)

def attend(queries, key_rows, value_rows, blocks, sequences, visible):
    length = queries.shape[0]
    step_rows = 512 if length % 512 == 0 else length
    count = length // step_rows
    query_blocks = queries.reshape(count, step_rows, KV, H // KV, HD)
    block_ids = blocks.reshape(count, step_rows)
    seq_blocks = sequences.reshape(count, step_rows)
    scale = HD ** (-0.5)

    def one_block(item):
        query_part, block_part, seq_part = item
        scores = jnp.einsum('nkgd,mkd->kgnm', query_part, key_rows, precision=HIGH) * scale
        scores = low_back(scores)
        allowed = (visible[block_part[:, None], blocks[None, :]] == 1) & (seq_part[:, None] == sequences[None, :])
        scores = jnp.where(allowed[None, None], scores, NEG)
        weights = low(jax.nn.softmax(scores, axis=-1))
        return jnp.einsum('kgnm,mkd->nkgd', weights, value_rows, precision=HIGH)
    result = lax.map(jax.checkpoint(one_block), (query_blocks, block_ids, seq_blocks))
    return result.reshape(length, H * HD)

def layer(hidden, positions, blocks, sequences, visible, weights):
    w_qkv, w_out, w_gate_up, w_down, gains = weights
    length = hidden.shape[0]
    query_width = H * HD
    key_width = KV * HD
    normed = low(rms_norm(hidden, gains[0]))
    mixed = low_back(jnp.dot(normed, w_qkv, precision=HIGH))
    cosine, sine = rotation(positions)
    queries = low(rotate(mixed[:, :query_width].reshape(length, H, HD), cosine, sine)).reshape(length, KV, H // KV, HD)
    key_rows = low(rotate(mixed[:, query_width:query_width + key_width].reshape(length, KV, HD), cosine, sine))
    value_rows = low(mixed[:, query_width + key_width:].reshape(length, KV, HD))
    attended = low_back(low(attend(queries, key_rows, value_rows, blocks, sequences, visible)))
    middle = hidden + low_back(jnp.dot(attended, w_out, precision=HIGH))
    normed_two = low(rms_norm(middle, gains[1]))
    gate_up = low_back(jnp.dot(normed_two, w_gate_up, precision=HIGH))
    gate_part = gate_up[:, :FF]
    up_part = gate_up[:, FF:]
    units = low(jax.nn.silu(gate_part) * up_part)
    return middle + low_back(jnp.dot(units, w_down, precision=HIGH))

def reference(x_in, cotangent, w_qkv, w_out, w_gate_up, w_down, gains, order, visible, seq_ids):
    groups = MB * GROUPS
    offsets = jnp.arange(LEN, dtype=jnp.int32)
    blocks = order[:, offsets // BLOCK].astype(jnp.int32)
    blocks = jnp.broadcast_to(blocks[:, None, :], (MB, GROUPS, LEN)).reshape(groups, LEN)
    positions = blocks * BLOCK + (offsets % BLOCK)[None, :]
    sequences = seq_ids.reshape(groups, LEN)
    inputs = x_in.astype(jnp.float32).reshape(groups, LEN, D)
    probe = jnp.zeros_like(inputs)
    first = (w_qkv[0].astype(jnp.float32), w_out[0].astype(jnp.float32), w_gate_up[0].astype(jnp.float32), w_down[0].astype(jnp.float32), gains[0].astype(jnp.float32))
    second = (w_qkv[1].astype(jnp.float32), w_out[1].astype(jnp.float32), w_gate_up[1].astype(jnp.float32), w_down[1].astype(jnp.float32), gains[1].astype(jnp.float32))

    def whole(source_rows, probe_rows, first_weights, second_weights):

        def one_group(item):
            source, extra, place, block_row, seq_row = item
            early = layer(source, place, block_row, seq_row, visible, first_weights)
            handed = low(early)
            later = layer(low_back(handed + extra), place, block_row, seq_row, visible, second_weights)
            return (handed, later)
        return lax.map(jax.checkpoint(one_group), (source_rows, probe_rows, positions, blocks, sequences))
    (early_out, later_out), pull = jax.vjp(whole, inputs, probe, first, second)
    grad_in, grad_probe, grad_first, grad_second = pull((jnp.zeros_like(early_out), cotangent.astype(jnp.float32).reshape(groups, LEN, D)))
    shape = (MB, GROUPS, LEN, D)
    activations = jnp.stack([early_out.reshape(shape), later_out.reshape(shape)]).astype(jnp.bfloat16)
    input_grads = jnp.stack([grad_in.reshape(shape), grad_probe.reshape(shape)])
    grad_qkv = jnp.stack([grad_first[0], grad_second[0]])
    grad_out = jnp.stack([grad_first[1], grad_second[1]])
    grad_gate_up = jnp.stack([grad_first[2], grad_second[2]])
    grad_down = jnp.stack([grad_first[3], grad_second[3]])
    grad_gains = jnp.stack([grad_first[4], grad_second[4]])
    return (activations, input_grads, grad_qkv, grad_out, grad_gate_up, grad_down, grad_gains)
```

```python
import jax
import jax.numpy as jnp
from jax import lax
from jax.experimental import pallas as pl
from jax.experimental.pallas import tpu as pltpu
from jax.sharding import PartitionSpec as P

D = 1152
H = 18
KV = 6
HD = 64
FF = 3072


NEG = -1e30
EPS = 1e-05


def shifted(value, axis, by):
    devices = lax.axis_size(axis)
    pairs = [(i, i + by) for i in range(devices) if 0 <= i + by < devices]
    return lax.ppermute(value, axis, pairs)


def rms_forward(hidden, gain_row):
    inverse = lax.rsqrt(jnp.mean(hidden * hidden, axis=-1, keepdims=True) + EPS)
    unit_rows = hidden * inverse
    return (unit_rows * gain_row, unit_rows, inverse)


def rms_backward(grad_rows, unit_rows, inverse, gain_row):
    grad_unit = grad_rows * gain_row
    grad_gain = jnp.sum(grad_rows * unit_rows, axis=0)
    inner = jnp.mean(grad_unit * unit_rows, axis=-1, keepdims=True)
    return (inverse * (grad_unit - unit_rows * inner), grad_gain)


def rotation(positions):
    frequency = 10000.0 ** (-(jnp.arange(HD // 2, dtype=jnp.float32) * 2.0 / HD))
    angles = positions.astype(jnp.float32)[:, None] * frequency[None, :]
    return (jnp.cos(angles), jnp.sin(angles))


def rotate(vectors, cosine, sine):
    half_width = vectors.shape[-1] // 2
    first_half = vectors[..., :half_width]
    second_half = vectors[..., half_width:]
    cos_rows = cosine[:, None, :]
    sin_rows = sine[:, None, :]
    return jnp.concatenate(
        [
            first_half * cos_rows - second_half * sin_rows,
            first_half * sin_rows + second_half * cos_rows,
        ],
        axis=-1,
    )


def stretch_width(rows, n_ctx):
    per_stretch = min(n_ctx, max(1, 512 // rows))
    while n_ctx % per_stretch:
        per_stretch -= 1
    return per_stretch


def sweep(step_fn, init, items, alive):

    def guarded(state, packed):
        item, live = packed
        return step_fn(state, item)

    return lax.scan(guarded, init, (items, alive))


def tables(order, visible, seq_ids, batch_index, column, rows, n_ctx):
    order_row = order[batch_index]
    own_block = order_row[column]
    seq_row = seq_ids[batch_index, 0]
    own_seq = lax.dynamic_slice_in_dim(seq_row, column * rows, rows)
    device_vis = visible[own_block][order_row]
    key_vis = jnp.broadcast_to(device_vis[:, None], (n_ctx, rows)).reshape(n_ctx * rows)
    positions = own_block * rows + jnp.arange(rows, dtype=jnp.int32)
    return ((own_seq, seq_row, key_vis, device_vis), positions)


def key_items(key_rows, value_rows, info, per_stretch, rows):
    own_seq, seq_row, key_vis, device_vis = info
    length = key_rows.shape[0]
    size = per_stretch * rows
    count = length // size
    items = (
        key_rows.reshape(count, size, KV, HD),
        value_rows.reshape(count, size, KV, HD),
        key_vis.reshape(count, size),
        seq_row.reshape(count, size),
    )
    alive = jnp.sum(device_vis.reshape(count, per_stretch), axis=-1) > 0
    return (items, alive, size)


def masked_scores(queries, key_part, vis_part, seq_part, own_seq):
    scores = jnp.einsum(
        "nkgd,mkd->kgnm", queries, key_part, preferred_element_type=jnp.float32
    ) * HD ** (-0.5)
    allowed = (vis_part[None, :] == 1) & (own_seq[:, None] == seq_part[None, :])
    return (jnp.where(allowed[None, None], scores, NEG), allowed)


def attention_forward(queries, key_rows, value_rows, info, per_stretch, rows):
    own_seq = info[0]
    items, alive, size = key_items(key_rows, value_rows, info, per_stretch, rows)
    group = H // KV

    def lse_step(state, item):
        high, total = state
        key_part, value_part, vis_part, seq_part = item
        masked, allowed = masked_scores(queries, key_part, vis_part, seq_part, own_seq)
        top = jnp.maximum(high, jnp.max(masked, axis=-1))
        terms = jnp.where(allowed[None, None], jnp.exp(masked - top[..., None]), 0.0)
        return ((top, total * jnp.exp(high - top) + jnp.sum(terms, axis=-1)), None)

    start_state = (
        jnp.full((KV, group, rows), NEG, jnp.float32),
        jnp.zeros((KV, group, rows), jnp.float32),
    )
    (high, total), unused = sweep(lse_step, start_state, items, alive)
    log_total = high + jnp.log(total)

    def out_step(acc, item):
        key_part, value_part, vis_part, seq_part = item
        masked, allowed = masked_scores(queries, key_part, vis_part, seq_part, own_seq)
        probs = jnp.where(allowed[None, None], jnp.exp(masked - log_total[..., None]), 0.0).astype(
            jnp.bfloat16
        )
        return (
            acc
            + jnp.einsum("kgnm,mkd->nkgd", probs, value_part, preferred_element_type=jnp.float32),
            None,
        )

    attended, unused_two = sweep(
        out_step, jnp.zeros((rows, KV, group, HD), jnp.float32), items, alive
    )
    return (attended, log_total)


def attention_backward(
    queries, key_rows, value_rows, info, per_stretch, rows, log_total, grad_att, delta
):
    own_seq = info[0]
    items, alive, size = key_items(key_rows, value_rows, info, per_stretch, rows)
    group = H // KV

    def back_step(grad_query, item):
        key_part, value_part, vis_part, seq_part = item
        masked, allowed = masked_scores(queries, key_part, vis_part, seq_part, own_seq)
        probs = jnp.where(allowed[None, None], jnp.exp(masked - log_total[..., None]), 0.0)
        probs_low = probs.astype(jnp.bfloat16)
        grad_probs = jnp.einsum(
            "nkgd,mkd->kgnm", grad_att, value_part, preferred_element_type=jnp.float32
        )
        grad_scores = (probs * (grad_probs - delta[..., None])).astype(jnp.bfloat16)
        grad_query = grad_query + jnp.einsum(
            "kgnm,mkd->nkgd", grad_scores, key_part, preferred_element_type=jnp.float32
        ) * HD ** (-0.5)
        grad_keys = jnp.einsum(
            "kgnm,nkgd->mkd", grad_scores, queries, preferred_element_type=jnp.float32
        ) * HD ** (-0.5)
        grad_values = jnp.einsum(
            "kgnm,nkgd->mkd", probs_low, grad_att, preferred_element_type=jnp.float32
        )
        return (grad_query, (grad_keys, grad_values))

    grad_query, (grad_keys, grad_values) = sweep(
        back_step, jnp.zeros((rows, KV, group, HD), jnp.float32), items, alive
    )
    length = key_rows.shape[0]
    return (grad_query, grad_keys.reshape(length, KV, HD), grad_values.reshape(length, KV, HD))


def layer_forward(hidden, weights, info, positions, per_stretch, rows):
    w_qkv, w_out, w_gate_up, w_down, gains = weights
    query_width = H * HD
    key_width = KV * HD
    gain_attn = gains[0].astype(jnp.float32)
    gain_ffn = gains[1].astype(jnp.float32)
    normed, unit_one, inverse_one = rms_forward(hidden, gain_attn)
    normed_low = normed.astype(jnp.bfloat16)
    mixed = jnp.dot(normed_low, w_qkv, preferred_element_type=jnp.float32)
    cosine, sine = rotation(positions)
    queries = (
        rotate(mixed[:, :query_width].reshape(rows, H, HD), cosine, sine)
        .astype(jnp.bfloat16)
        .reshape(rows, KV, H // KV, HD)
    )
    key_own = rotate(
        mixed[:, query_width : query_width + key_width].reshape(rows, KV, HD), cosine, sine
    ).astype(jnp.bfloat16)
    value_own = mixed[:, query_width + key_width :].reshape(rows, KV, HD).astype(jnp.bfloat16)
    key_rows, value_rows = (
        lax.all_gather(key_own, "ctx", axis=0, tiled=True),
        lax.all_gather(value_own, "ctx", axis=0, tiled=True),
    )
    attended, log_total = attention_forward(queries, key_rows, value_rows, info, per_stretch, rows)
    attended_low = attended.reshape(rows, query_width).astype(jnp.bfloat16)
    middle = hidden + jnp.dot(attended_low, w_out, preferred_element_type=jnp.float32)
    normed_two, unit_two, inverse_two = rms_forward(middle, gain_ffn)
    normed_two_low = normed_two.astype(jnp.bfloat16)
    gate_up = jnp.dot(normed_two_low, w_gate_up, preferred_element_type=jnp.float32)
    gate_part = gate_up[:, :FF]
    up_part = gate_up[:, FF:]
    units_low = (jax.nn.silu(gate_part) * up_part).astype(jnp.bfloat16)
    result = middle + jnp.dot(units_low, w_down, preferred_element_type=jnp.float32)
    saved = {
        "unit_one": unit_one,
        "inverse_one": inverse_one,
        "normed_low": normed_low,
        "cosine": cosine,
        "sine": sine,
        "queries": queries,
        "key_rows": key_rows,
        "value_rows": value_rows,
        "attended": attended,
        "log_total": log_total,
        "attended_low": attended_low,
        "unit_two": unit_two,
        "inverse_two": inverse_two,
        "normed_two_low": normed_two_low,
        "gate_part": gate_part,
        "up_part": up_part,
        "units_low": units_low,
    }
    return (result, saved)


def layer_backward(grad_rows, weights, saved, info, per_stretch, rows):
    w_qkv, w_out, w_gate_up, w_down, gains = weights
    query_width = H * HD
    gain_attn = gains[0].astype(jnp.float32)
    gain_ffn = gains[1].astype(jnp.float32)
    gate_part = saved["gate_part"]
    grad_low = grad_rows.astype(jnp.bfloat16)
    grad_units = jnp.dot(grad_low, w_down.T, preferred_element_type=jnp.float32)
    sigmoid = jax.nn.sigmoid(gate_part)
    grad_gate = grad_units * saved["up_part"] * sigmoid * (1.0 + gate_part * (1.0 - sigmoid))
    grad_up = grad_units * gate_part * sigmoid
    grad_mix_low = jnp.concatenate([grad_gate, grad_up], axis=-1).astype(jnp.bfloat16)
    grad_normed_two = jnp.dot(grad_mix_low, w_gate_up.T, preferred_element_type=jnp.float32)
    grad_mid_norm, grad_gain_two = rms_backward(
        grad_normed_two, saved["unit_two"], saved["inverse_two"], gain_ffn
    )
    grad_middle = grad_rows + grad_mid_norm
    grad_branch_low = grad_middle.astype(jnp.bfloat16)
    grad_att = (
        jnp.dot(grad_branch_low, w_out.T, preferred_element_type=jnp.float32)
        .astype(jnp.bfloat16)
        .reshape(rows, KV, H // KV, HD)
    )
    delta = jnp.einsum("nkgd,nkgd->kgn", grad_att.astype(jnp.float32), saved["attended"])
    grad_query, grad_keys, grad_values = attention_backward(
        saved["queries"],
        saved["key_rows"],
        saved["value_rows"],
        info,
        per_stretch,
        rows,
        saved["log_total"],
        grad_att,
        delta,
    )
    key_total, value_total = (
        lax.psum_scatter(
            grad_keys.astype(jnp.bfloat16), "ctx", scatter_dimension=0, tiled=True
        ).astype(jnp.float32),
        lax.psum_scatter(
            grad_values.astype(jnp.bfloat16), "ctx", scatter_dimension=0, tiled=True
        ).astype(jnp.float32),
    )
    cosine = saved["cosine"]
    back_sine = -saved["sine"]
    grad_q = rotate(grad_query.reshape(rows, H, HD), cosine, back_sine).reshape(rows, query_width)
    grad_k = rotate(key_total, cosine, back_sine).reshape(rows, KV * HD)
    grad_v = value_total.reshape(rows, KV * HD)
    grad_qkv_low = jnp.concatenate([grad_q, grad_k, grad_v], axis=-1).astype(jnp.bfloat16)
    grad_normed = jnp.dot(grad_qkv_low, w_qkv.T, preferred_element_type=jnp.float32)
    grad_in_norm, grad_gain_one = rms_backward(
        grad_normed, saved["unit_one"], saved["inverse_one"], gain_attn
    )
    grad_hidden = grad_middle + grad_in_norm
    pairs = (
        saved["normed_low"],
        grad_qkv_low,
        saved["attended_low"],
        grad_branch_low,
        saved["normed_two_low"],
        grad_mix_low,
        saved["units_low"],
        grad_low,
        grad_gain_one,
        grad_gain_two,
    )
    return (grad_hidden, pairs)


def weight_terms(pairs):
    (
        normed_low,
        grad_qkv_low,
        attended_low,
        grad_branch_low,
        normed_two_low,
        grad_mix_low,
        units_low,
        grad_low,
        grad_gain_one,
        grad_gain_two,
    ) = pairs
    return (
        jnp.dot(normed_low.T, grad_qkv_low, preferred_element_type=jnp.float32),
        jnp.dot(attended_low.T, grad_branch_low, preferred_element_type=jnp.float32),
        jnp.dot(normed_two_low.T, grad_mix_low, preferred_element_type=jnp.float32),
        jnp.dot(units_low.T, grad_low, preferred_element_type=jnp.float32),
        jnp.stack([grad_gain_one, grad_gain_two]),
    )


def on_device_general(x_in, cotangent, w_qkv, w_out, w_gate_up, w_down, gains, order, visible, seq_ids):
    section = lax.axis_index("section")
    column = lax.axis_index("ctx")
    n_ctx = lax.axis_size("ctx")
    batches = x_in.shape[0]
    rows = x_in.shape[2]
    per_stretch = stretch_width(rows, n_ctx)
    first_section = section == 0
    weights = (
        lax.all_gather(w_qkv[0], "wsh", axis=0, tiled=True),
        lax.all_gather(w_out[0], "wsh", axis=1, tiled=True),
        lax.all_gather(w_gate_up[0], "wsh", axis=0, tiled=True),
        lax.all_gather(w_down[0], "wsh", axis=1, tiled=True),
        lax.all_gather(gains[0], "wsh", axis=1, tiled=True),
    )
    incoming = jnp.zeros((rows, D), jnp.bfloat16)
    section_inputs = []
    section_outputs = []
    for tick_now in range(batches + 1):
        batch_index = jnp.clip(tick_now - section, 0, batches - 1)
        info, positions = tables(order, visible, seq_ids, batch_index, column, rows, n_ctx)
        source = jnp.where(first_section, x_in[batch_index, 0], incoming)
        result, unused = layer_forward(
            source.astype(jnp.float32), weights, info, positions, per_stretch, rows
        )
        result_low = result.astype(jnp.bfloat16)
        section_inputs.append(source)
        section_outputs.append(result_low)
        if tick_now < batches:
            incoming = shifted(result_low, "section", 1)
    activations = jnp.stack(
        [
            jnp.where(first_section, section_outputs[batch], section_outputs[batch + 1])
            for batch in range(batches)
        ]
    )
    back_weights = (
        lax.all_gather(w_qkv[0], "wsh", axis=0, tiled=True),
        lax.all_gather(w_out[0], "wsh", axis=1, tiled=True),
        lax.all_gather(w_gate_up[0], "wsh", axis=0, tiled=True),
        lax.all_gather(w_down[0], "wsh", axis=1, tiled=True),
        lax.all_gather(gains[0], "wsh", axis=1, tiled=True),
    )
    returned = jnp.zeros((rows, D), jnp.bfloat16)
    grad_list = []
    totals = None
    for tick_now in range(batches + 1):
        raw_index = tick_now - 1 + section
        valid = (raw_index >= 0) & (raw_index < batches)
        batch_index = jnp.clip(raw_index, 0, batches - 1)
        info, positions = tables(order, visible, seq_ids, batch_index, column, rows, n_ctx)
        source = jnp.where(
            first_section,
            section_inputs[max(tick_now - 1, 0)],
            section_inputs[min(tick_now + 1, batches)],
        )
        unused, saved = layer_forward(
            source.astype(jnp.float32), back_weights, info, positions, per_stretch, rows
        )
        grad_rows = jnp.where(first_section, returned, cotangent[batch_index, 0]).astype(
            jnp.float32
        ) * valid.astype(jnp.float32)
        grad_hidden, pairs = layer_backward(grad_rows, back_weights, saved, info, per_stretch, rows)
        grad_hidden_low = grad_hidden.astype(jnp.bfloat16)
        grad_list.append((grad_hidden, grad_hidden_low))
        if tick_now < batches:
            returned = shifted(grad_hidden_low, "section", -1)
        terms = weight_terms(pairs)
        totals = terms if totals is None else jax.tree.map(jnp.add, totals, terms)
    input_grads = jnp.stack(
        [
            jnp.where(
                first_section, grad_list[batch + 1][0], grad_list[batch][1].astype(jnp.float32)
            )
            for batch in range(batches)
        ]
    )
    term_qkv, term_out, term_gate_up, term_down, term_gains = totals
    shares = (
        lax.psum_scatter(term_qkv, ("ctx", "wsh"), scatter_dimension=0, tiled=True),
        lax.psum_scatter(term_out, ("ctx", "wsh"), scatter_dimension=1, tiled=True),
        lax.psum_scatter(term_gate_up, ("ctx", "wsh"), scatter_dimension=0, tiled=True),
        lax.psum_scatter(term_down, ("ctx", "wsh"), scatter_dimension=1, tiled=True),
        lax.psum_scatter(term_gains, ("ctx", "wsh"), scatter_dimension=1, tiled=True),
    )
    return (
        activations[None, :, None],
        input_grads[None, :, None],
        shares[0][None],
        shares[1][None],
        shares[2][None],
        shares[3][None],
        shares[4][None],
    )


GROUP = H // KV
QD = H * HD
KD = KV * HD
QKV = QD + 2 * KD
SIDE = 128
LOW = jnp.bfloat16


def fits_pairs(mesh):
    return mesh.shape["section"] == 2 and mesh.shape["ctx"] == 4 and mesh.shape["wsh"] == 4


def contract(left, right, left_dim, right_dim):
    return lax.dot_general(
        left,
        right,
        (((left_dim,), (right_dim,)), ((), ())),
        preferred_element_type=jnp.float32,
    )


def swap(value, axis, bit):
    return lax.ppermute(value, axis, [(i, i ^ bit) for i in range(lax.axis_size(axis))])


def after(value, *others):
    return lax.optimization_barrier((value, *others))[0]


def fill_bias(bias_ref, kseq_ref, qseq_ref):
    @pl.when(pl.program_id(0) == 0)
    def _():
        for slot in range(bias_ref.shape[0]):
            bias_ref[slot] = jnp.where(kseq_ref[slot][:, :1] == qseq_ref[...], 0.0, NEG)


def forward_kernel(live_ref, q_ref, k_ref, v_ref, kseq_ref, qseq_ref, o_ref, lse_ref, bias_ref):
    fill_bias(bias_ref, kseq_ref, qseq_ref)
    rows = q_ref.shape[1]
    queries = [q_ref[pl.ds(j * HD, HD), :] for j in range(GROUP)]

    def step(i, states):
        slot = live_ref[1 + i]
        key_t = k_ref[slot, 0]
        value_t = v_ref[slot, 0]
        new_states = []
        for j in range(GROUP):
            high, total, acc = states[j]
            scores = contract(key_t, queries[j], 0, 0) + bias_ref[slot]
            top = jnp.maximum(high, jnp.max(scores, axis=0, keepdims=True))
            terms = jnp.exp(scores - top)
            scale = jnp.exp(high - top)
            total = total * scale + jnp.sum(terms, axis=0, keepdims=True)
            acc = acc * scale + contract(value_t, terms.astype(LOW), 1, 0)
            new_states.append((top, total, acc))
        return tuple(new_states)

    start = (
        jnp.full((1, rows), NEG, jnp.float32),
        jnp.zeros((1, rows), jnp.float32),
        jnp.zeros((HD, rows), jnp.float32),
    )
    states = lax.fori_loop(0, live_ref[0], step, (start,) * GROUP)
    for j in range(GROUP):
        high, total, acc = states[j]
        o_ref[pl.ds(j * HD, HD), :] = (acc / total).astype(o_ref.dtype)
        lse_ref[0, pl.ds(j, 1), :] = high + jnp.log(total)


def backward_kernel(
    live_ref,
    q_ref,
    do_ref,
    o_ref,
    lse_ref,
    k_ref,
    v_ref,
    kseq_ref,
    qseq_ref,
    dq_ref,
    dk_ref,
    dv_ref,
    bias_ref,
    acc_ref,
):
    fill_bias(bias_ref, kseq_ref, qseq_ref)
    keys = bias_ref.shape[1]
    acc_ref[...] = jnp.zeros_like(acc_ref)
    dk_ref[...] = jnp.zeros_like(dk_ref)
    dv_ref[...] = jnp.zeros_like(dv_ref)
    deltas = []
    for j in range(GROUP):
        part = pl.ds(j * HD, HD)
        both = do_ref[part, :].astype(jnp.float32) * o_ref[part, :].astype(jnp.float32)
        deltas.append(jnp.sum(both, axis=0, keepdims=True))

    def step(i, carry):
        slot = live_ref[1 + i]
        key_t = k_ref[slot, 0]
        value_t = v_ref[slot, 0]
        grad_k = jnp.zeros((keys, HD), jnp.float32)
        grad_v = jnp.zeros((keys, HD), jnp.float32)
        for j in range(GROUP):
            part = pl.ds(j * HD, HD)
            query_t = q_ref[part, :]
            grad_t = do_ref[part, :]
            scores = contract(key_t, query_t, 0, 0) + bias_ref[slot]
            probs = jnp.exp(scores - lse_ref[0, pl.ds(j, 1), :])
            grad_probs = contract(value_t, grad_t, 0, 0)
            grad_scores = (probs * (grad_probs - deltas[j])).astype(LOW)
            grad_v = grad_v + contract(probs.astype(LOW), grad_t, 1, 1)
            grad_k = grad_k + contract(grad_scores, query_t, 1, 1)
            acc_ref[part, :] += contract(key_t, grad_scores, 1, 0)
        dk_ref[slot, 0] = jnp.transpose(grad_k).astype(LOW)
        dv_ref[slot, 0] = jnp.transpose(grad_v).astype(LOW)
        return carry

    lax.fori_loop(0, live_ref[0], step, 0)
    dq_ref[...] = acc_ref[...] * HD ** (-0.5)


def kernel_cost(scores, matmuls):
    return pl.CostEstimate(
        flops=scores * matmuls * HD * 2 * 4, bytes_accessed=12 * 2**20, transcendentals=scores
    )


def pair_attention_forward(info, q_t, kv_t):
    live, key_seq, own_seq = info
    slots, keys = kv_t.shape[0], kv_t.shape[3]
    rows = q_t.shape[1]
    return pl.pallas_call(
        forward_kernel,
        grid_spec=pltpu.PrefetchScalarGridSpec(
            num_scalar_prefetch=1,
            grid=(KV,),
            in_specs=[
                pl.BlockSpec((GROUP * HD, rows), lambda g, l: (g, 0)),
                pl.BlockSpec((slots, 1, HD, keys), lambda g, l: (0, g, 0, 0)),
                pl.BlockSpec((slots, 1, HD, keys), lambda g, l: (0, KV + g, 0, 0)),
                pl.BlockSpec((slots, keys, SIDE), lambda g, l: (0, 0, 0)),
                pl.BlockSpec((1, rows), lambda g, l: (0, 0)),
            ],
            out_specs=[
                pl.BlockSpec((GROUP * HD, rows), lambda g, l: (g, 0)),
                pl.BlockSpec((1, GROUP, rows), lambda g, l: (g, 0, 0)),
            ],
            scratch_shapes=[pltpu.VMEM((slots, keys, rows), jnp.float32)],
        ),
        out_shape=[
            jax.ShapeDtypeStruct(q_t.shape, LOW),
            jax.ShapeDtypeStruct((KV, GROUP, rows), jnp.float32),
        ],
        compiler_params=pltpu.CompilerParams(vmem_limit_bytes=48 * 2**20),
        cost_estimate=kernel_cost(H * rows * slots * keys, 2),
    )(live, q_t, kv_t, kv_t, key_seq, own_seq)


def pair_attention_backward(info, q_t, do_t, o_t, lse, kv_t):
    live, key_seq, own_seq = info
    slots, keys = kv_t.shape[0], kv_t.shape[3]
    rows = q_t.shape[1]
    q_spec = pl.BlockSpec((GROUP * HD, rows), lambda g, l: (g, 0))
    part_spec = pl.BlockSpec((slots, 1, HD, keys), lambda g, l: (0, g, 0, 0))
    part_shape = jax.ShapeDtypeStruct((slots, KV, HD, keys), LOW)
    return pl.pallas_call(
        backward_kernel,
        grid_spec=pltpu.PrefetchScalarGridSpec(
            num_scalar_prefetch=1,
            grid=(KV,),
            in_specs=[
                q_spec,
                q_spec,
                q_spec,
                pl.BlockSpec((1, GROUP, rows), lambda g, l: (g, 0, 0)),
                part_spec,
                pl.BlockSpec((slots, 1, HD, keys), lambda g, l: (0, KV + g, 0, 0)),
                pl.BlockSpec((slots, keys, SIDE), lambda g, l: (0, 0, 0)),
                pl.BlockSpec((1, rows), lambda g, l: (0, 0)),
            ],
            out_specs=[q_spec, part_spec, part_spec],
            scratch_shapes=[
                pltpu.VMEM((slots, keys, rows), jnp.float32),
                pltpu.VMEM((GROUP * HD, rows), jnp.float32),
            ],
        ),
        out_shape=[jax.ShapeDtypeStruct(q_t.shape, jnp.float32), part_shape, part_shape],
        compiler_params=pltpu.CompilerParams(vmem_limit_bytes=48 * 2**20),
        cost_estimate=kernel_cost(H * rows * slots * keys, 5),
    )(live, q_t, do_t, o_t, lse, kv_t, kv_t, key_seq, own_seq)


def turn(heads, cosine, sine):
    half = HD // 2
    first, second = heads[:, :half], heads[:, half:]
    return jnp.concatenate(
        [first * cosine - second * sine, first * sine + second * cosine], axis=1
    )


def one_hot(index, size):
    return (index[:, None] == jnp.arange(size, dtype=jnp.int32)[None, :]).astype(LOW)


def pair_tables(order, visible, seq_ids, batch, slot, rows):
    order_row = order[batch]
    order_slots = [order_row[slot ^ step] for step in (0, 2, 1, 3)]
    own_block = order_slots[0]
    seqs = [
        lax.dynamic_slice_in_dim(seq_ids, (slot ^ step) * rows, rows) for step in (0, 2, 1, 3)
    ]
    has = [(jnp.any(s == 0), jnp.any(s == 1)) for s in seqs]
    alive = []
    for block, (zero, one) in zip(order_slots, has):
        shares = (zero & has[0][0]) | (one & has[0][1])
        alive.append((visible[own_block, block] == 1) & shares)
    alive[0] = jnp.bool_(True)
    alive = jnp.stack(alive).astype(jnp.int32)
    place = jnp.cumsum(alive) - 1
    ids = jnp.arange(4, dtype=jnp.int32)
    listed = jnp.sum(
        jnp.where((place[None, :] == ids[:, None]) & (alive[None, :] == 1), ids[None, :], 0),
        axis=1,
    )
    live = jnp.concatenate([jnp.sum(alive, keepdims=True), listed]).astype(jnp.int32)
    key_seq = jnp.broadcast_to(
        jnp.stack(seqs).astype(jnp.float32)[:, :, None], (4, rows, SIDE)
    )
    own_seq = seqs[0].astype(jnp.float32)[None]
    positions = own_block * rows + jnp.arange(rows, dtype=jnp.int32)
    frequency = 10000.0 ** (-(jnp.arange(HD // 2, dtype=jnp.float32) * 2.0 / HD))
    angles = frequency[:, None] * positions.astype(jnp.float32)[None, :]
    return (live, key_seq, own_seq), (jnp.cos(angles), jnp.sin(angles))


def gather_both(shards, section, half):
    own_side, other_side = [], []
    sent = []
    for step, own in enumerate(shards):
        if step >= 2:
            own = after(own, sent[step - 2])
        near = swap(own, "wsh", 2)
        sent.append(near)
        rows, width = own.shape
        if step < 2:
            other = swap(own, "section", 1)
            if step == 0:
                far = swap(after(other, near), "wsh", 2)
            else:
                far = swap(near, "section", 1)
        else:
            both = jnp.stack([own, near]).reshape(2, 2, rows // 2, width)
            mine = lax.dynamic_index_in_dim(both, half, 1, keepdims=False)
            crossed = swap(mine, "section", 1)
            passed = swap(crossed, "ctx", 1)
            crossed_two = swap(crossed, "wsh", 1)
            passed_two = swap(passed, "wsh", 1)
            first = half == 0

            def joined(a, b):
                return jnp.concatenate([jnp.where(first, a, b), jnp.where(first, b, a)], axis=0)

            other, far = joined(crossed[0], passed[0]), joined(crossed[1], passed[1])
            other_two = joined(crossed_two[0], passed_two[0])
            far_two = joined(crossed_two[1], passed_two[1])
        if step < 2:
            other_two, far_two = swap(other, "wsh", 1), swap(far, "wsh", 1)
        own_side.append(
            jnp.concatenate([own, swap(own, "wsh", 1), near, swap(near, "wsh", 1)], axis=0)
        )
        other_side.append(jnp.concatenate([other, other_two, far, far_two], axis=0))
    first_section = section == 0
    return [
        [
            jnp.where(first_section, a, b) if layer == 0 else jnp.where(first_section, b, a)
            for a, b in zip(own_side, other_side)
        ]
        for layer in range(2)
    ]


def unpack(weights):
    w_in, w_out_t, w_gate, w_up, w_down_t = weights
    gain_one = w_in[:, QKV].astype(jnp.float32)
    gain_two = w_in[:, QKV + 1].astype(jnp.float32)
    return w_in, w_out_t, w_gate, w_up, w_down_t, gain_one, gain_two


def pair_forward(hidden, weights, info, angles):
    w_in, w_out_t, w_gate, w_up, w_down_t, gain_one, gain_two = unpack(weights)
    rows = hidden.shape[0]
    cosine, sine = angles
    normed, unused, inverse_one = rms_forward(hidden, gain_one)
    normed = normed.astype(LOW)
    kv = contract(w_in[:, QD:QKV], normed, 0, 1).reshape(2 * KV, HD, rows)
    kv_own = jnp.concatenate([turn(kv[:KV], cosine, sine), kv[KV:]], axis=0).astype(LOW)
    kv_far = swap(kv_own, "ctx", 1)
    kv_near = swap(kv_own, "wsh", 1)
    kv_last = swap(kv_far, "wsh", 1)
    q = contract(w_in[:, :QD], normed, 0, 1).reshape(H, HD, rows)
    q_t = (turn(q, cosine, sine).astype(LOW) * HD ** (-0.5)).reshape(QD, rows)
    kv_t = jnp.stack([kv_own, kv_near, kv_far, kv_last])
    o_t, lse = pair_attention_forward(info, q_t, kv_t)
    middle = hidden + contract(o_t, w_out_t, 0, 1)
    normed_two, unused, inverse_two = rms_forward(middle, gain_two)
    normed_two = normed_two.astype(LOW)
    gate = contract(normed_two, w_gate, 1, 0).astype(LOW)
    up = contract(normed_two, w_up, 1, 0).astype(LOW)
    gate_wide = gate.astype(jnp.float32)
    units = (jax.nn.silu(gate_wide) * up.astype(jnp.float32)).astype(LOW)
    result = (middle + contract(units, w_down_t, 1, 1)).astype(LOW)
    saved = (hidden, inverse_one, normed, q_t, kv_t, o_t, lse, middle, inverse_two, normed_two)
    return result, saved + (gate, up, units)


def spread(layer, lhs_t, rhs, rhs_dim, extra=None):
    half = lhs_t.shape[0] // 2
    given = contract(lhs_t[:half], rhs, 1, rhs_dim)
    kept = contract(lhs_t[half:], rhs, 1, rhs_dim)
    if extra is not None:
        given = jnp.concatenate([given, extra[:half]], axis=1)
        kept = jnp.concatenate([kept, extra[half:]], axis=1)
    width = given.shape[1]
    kept = (kept + swap(given.astype(LOW), "wsh", 1).astype(jnp.float32)).astype(LOW)
    quarter = half // 2
    got = swap(kept[:quarter], "wsh", 2).astype(jnp.float32)
    parts = (kept[quarter:].astype(jnp.float32) + got).reshape(4, quarter // 4, width)
    sent = [swap(parts[k].astype(LOW), "ctx", k).astype(jnp.float32) for k in range(1, 4)]
    own = (parts[0] + sent[0] + sent[1] + sent[2]).astype(LOW)
    return own, lax.ppermute(own, "section", [(1 - layer, layer)])


def pair_backward(layer, grad_low, weights, saved, info, angles, arrange):
    w_in, w_out_t, w_gate, w_up, w_down_t, gain_one, gain_two = unpack(weights)
    (
        hidden,
        inverse_one,
        normed,
        q_t,
        kv_t,
        o_t,
        lse,
        middle,
        inverse_two,
        normed_two,
        gate,
        up,
        units,
    ) = saved
    rows = hidden.shape[0]
    cosine, sine = angles

    def arranged(value):
        return contract(arrange, value, 1, 1).astype(LOW)

    shares = {}
    shares["down"] = spread(layer, arranged(grad_low), units, 0)
    grad_units = contract(grad_low, w_down_t, 1, 0)
    gate_wide = gate.astype(jnp.float32)
    sigmoid = jax.nn.sigmoid(gate_wide)
    grad_gate = (
        grad_units * up.astype(jnp.float32) * sigmoid * (1.0 + gate_wide * (1.0 - sigmoid))
    ).astype(LOW)
    grad_up = (grad_units * gate_wide * sigmoid).astype(LOW)
    lhs_two = arranged(normed_two)
    shares["gate"] = spread(layer, lhs_two, grad_gate, 0)
    shares["up"] = spread(layer, lhs_two, grad_up, 0)
    grad_normed_two = contract(grad_gate, w_gate, 1, 1) + contract(grad_up, w_up, 1, 1)
    grad_mid_norm, grad_gain_two = rms_backward(
        grad_normed_two, middle * inverse_two, inverse_two, gain_two
    )
    grad_middle = grad_low.astype(jnp.float32) + grad_mid_norm
    grad_branch = grad_middle.astype(LOW)
    do_t = contract(w_out_t, grad_branch, 0, 1).astype(LOW)
    dq_t, dk_t, dv_t = pair_attention_backward(info, q_t, do_t, o_t, lse, kv_t)
    grad_kv = jnp.concatenate([dk_t, dv_t], axis=1)
    crossed = swap(jnp.stack([grad_kv[1], grad_kv[3]]), "wsh", 1).astype(jnp.float32)
    far = (grad_kv[2].astype(jnp.float32) + crossed[1]).astype(LOW)
    grad_kv = (
        grad_kv[0].astype(jnp.float32) + crossed[0] + swap(far, "ctx", 1).astype(jnp.float32)
    )
    grad_q = turn(dq_t.reshape(H, HD, rows), cosine, -sine).reshape(QD, rows)
    grad_k = turn(grad_kv[:KV], cosine, -sine).reshape(KD, rows)
    grad_v = grad_kv[KV:].reshape(KD, rows)
    grad_mixed = jnp.concatenate([grad_q, grad_k, grad_v], axis=0).astype(LOW)
    grad_normed = contract(grad_mixed, w_in[:, :QKV], 0, 1)
    grad_in_norm, grad_gain_one = rms_backward(
        grad_normed, hidden * inverse_one, inverse_one, gain_one
    )
    grad_hidden = (grad_middle + grad_in_norm).astype(LOW)
    shares["out"] = spread(layer, arranged(grad_branch), o_t, 1)
    gain_rows = jnp.zeros((SIDE, D), LOW)
    gain_rows = gain_rows.at[0].set(grad_gain_one.astype(LOW)).at[1].set(grad_gain_two.astype(LOW))
    shares["in"] = spread(layer, arranged(normed), grad_mixed, 1, arranged(gain_rows))
    return grad_hidden, shares


def on_device_pairs(
    x_in, cotangent, w_qkv, w_out, w_gate_up, w_down, gains, order, visible, seq_ids
):
    section = lax.axis_index("section")
    column = lax.axis_index("ctx")
    place = lax.axis_index("wsh")
    core = place % 2
    side = place // 2
    rows = x_in.shape[2]
    quarter = D // 4
    share = quarter // 4
    slot = column % 2 + 2 * core
    first_section = section == 0

    def partner(index):
        z, w = index // 4, index % 4
        if (z < 2) == (w % 2 == 1):
            return ((z + 2) % 4) * 4 + (w ^ 1)
        return index

    moves = [(i, partner(i)) for i in range(16)]

    def moved(value):
        return lax.ppermute(value, ("ctx", "wsh"), moves)

    ids = jnp.arange(D, dtype=jnp.int32)
    natural = one_hot((place ^ (ids // quarter)) * quarter + ids % quarter, D)
    given, block, shard = ids // (D // 2), (ids % quarter) // share, ids % share
    to_core = jnp.where(given == 0, 1 - core, core)
    to_side = jnp.where((ids % (D // 2)) // quarter == 0, 1 - side, side)
    to_place = place ^ column ^ block
    arrange = one_hot(to_place * quarter + (2 * to_side + to_core) * share + shard, D)

    seq_both = jnp.stack([seq_ids[:, 0], swap(seq_ids[:, 0], "wsh", 1)])
    seq_row = jnp.where(core == column // 2, seq_both[0, section], seq_both[1, section])
    info, angles = pair_tables(order, visible, seq_row, section, slot, rows)

    gain_columns = jnp.concatenate(
        [gains[0].T, jnp.zeros((quarter, SIDE - gains.shape[1]), LOW)], axis=1
    )
    shards = [
        jnp.concatenate([w_qkv[0], gain_columns], axis=1),
        w_out[0].T,
        w_gate_up[0][:, :FF],
        w_gate_up[0][:, FF:],
        w_down[0].T,
    ]
    hidden = contract(moved(x_in[section, 0]), natural, 1, 1)
    weights = gather_both(shards, section, column % 2)
    result_one, saved_one = pair_forward(hidden, weights[0], info, angles)
    result_two, saved_two = pair_forward(
        result_one.astype(jnp.float32), weights[1], info, angles
    )

    def placed(own_one, own_two):
        mine = jnp.where(first_section, own_one, own_two)
        other = swap(jnp.where(first_section, own_two, own_one), "section", 1)
        both = jnp.concatenate(
            [jnp.where(first_section, mine, other), jnp.where(first_section, other, mine)], axis=0
        )
        both = contract(both, natural, 1, 0).astype(LOW)
        return moved(both).reshape(2, rows, D)

    activations = placed(result_one, result_two)
    grad_low = contract(moved(cotangent[section, 0]), natural, 1, 1).astype(LOW)
    grad_two, shares_two = pair_backward(
        1, grad_low, weights[1], saved_two, info, angles, arrange
    )
    grad_one, shares_one = pair_backward(
        0, grad_two, weights[0], saved_one, info, angles, arrange
    )
    input_grads = placed(grad_one, grad_two).astype(jnp.float32)

    def total(name):
        one, two = shares_one[name], shares_two[name]
        return jnp.where(
            first_section,
            one[0].astype(jnp.float32) + one[1].astype(jnp.float32),
            two[0].astype(jnp.float32) + two[1].astype(jnp.float32),
        )

    term_in = total("in")
    return (
        activations[None, :, None],
        input_grads[None, :, None],
        term_in[None, :, :QKV],
        total("out").T[None],
        jnp.concatenate([total("gate"), total("up")], axis=1)[None],
        total("down").T[None],
        term_in[:, QKV : QKV + 2].T[None],
    )


def solution(mesh):
    in_specs = (
        P(None, "wsh", "ctx", None),
        P(None, "wsh", "ctx", None),
        P("section", "wsh", None),
        P("section", None, "wsh"),
        P("section", "wsh", None),
        P("section", None, "wsh"),
        P("section", None, "wsh"),
        P(),
        P(),
        P(None, "wsh", None),
    )
    out_specs = (
        P("section", None, "wsh", "ctx", None),
        P("section", None, "wsh", "ctx", None),
        P("section", ("ctx", "wsh"), None),
        P("section", None, ("ctx", "wsh")),
        P("section", ("ctx", "wsh"), None),
        P("section", None, ("ctx", "wsh")),
        P("section", None, ("ctx", "wsh")),
    )
    body = on_device_pairs if fits_pairs(mesh) else on_device_general
    return jax.shard_map(
        body, mesh=mesh, in_specs=in_specs, out_specs=out_specs, check_vma=False
    )
```

```python
import jax
import jax.numpy as jnp
from jax import lax
from jax.experimental import pallas as pl
from jax.experimental.pallas import tpu as pltpu
from jax.sharding import PartitionSpec as P

D = 1152
H = 18
KV = 6
HD = 64
FF = 3072


NEG = -1e30
EPS = 1e-05


def shifted(value, axis, by):
    devices = lax.axis_size(axis)
    pairs = [(i, i + by) for i in range(devices) if 0 <= i + by < devices]
    return lax.ppermute(value, axis, pairs)


def rms_forward(hidden, gain_row):
    inverse = lax.rsqrt(jnp.mean(hidden * hidden, axis=-1, keepdims=True) + EPS)
    unit_rows = hidden * inverse
    return (unit_rows * gain_row, unit_rows, inverse)


def rms_backward(grad_rows, unit_rows, inverse, gain_row):
    grad_unit = grad_rows * gain_row
    grad_gain = jnp.sum(grad_rows * unit_rows, axis=0)
    inner = jnp.mean(grad_unit * unit_rows, axis=-1, keepdims=True)
    return (inverse * (grad_unit - unit_rows * inner), grad_gain)


def rotation(positions):
    frequency = 10000.0 ** (-(jnp.arange(HD // 2, dtype=jnp.float32) * 2.0 / HD))
    angles = positions.astype(jnp.float32)[:, None] * frequency[None, :]
    return (jnp.cos(angles), jnp.sin(angles))


def rotate(vectors, cosine, sine):
    half_width = vectors.shape[-1] // 2
    first_half = vectors[..., :half_width]
    second_half = vectors[..., half_width:]
    cos_rows = cosine[:, None, :]
    sin_rows = sine[:, None, :]
    return jnp.concatenate(
        [
            first_half * cos_rows - second_half * sin_rows,
            first_half * sin_rows + second_half * cos_rows,
        ],
        axis=-1,
    )


def stretch_width(rows, n_ctx):
    per_stretch = min(n_ctx, max(1, 512 // rows))
    while n_ctx % per_stretch:
        per_stretch -= 1
    return per_stretch


def sweep(step_fn, init, items, alive):

    def guarded(state, packed):
        item, live = packed
        return step_fn(state, item)

    return lax.scan(guarded, init, (items, alive))


def tables(order, visible, seq_ids, batch_index, column, rows, n_ctx):
    order_row = order[batch_index]
    own_block = order_row[column]
    seq_row = seq_ids[batch_index, 0]
    own_seq = lax.dynamic_slice_in_dim(seq_row, column * rows, rows)
    device_vis = visible[own_block][order_row]
    key_vis = jnp.broadcast_to(device_vis[:, None], (n_ctx, rows)).reshape(n_ctx * rows)
    positions = own_block * rows + jnp.arange(rows, dtype=jnp.int32)
    return ((own_seq, seq_row, key_vis, device_vis), positions)


def key_items(key_rows, value_rows, info, per_stretch, rows):
    own_seq, seq_row, key_vis, device_vis = info
    length = key_rows.shape[0]
    size = per_stretch * rows
    count = length // size
    items = (
        key_rows.reshape(count, size, KV, HD),
        value_rows.reshape(count, size, KV, HD),
        key_vis.reshape(count, size),
        seq_row.reshape(count, size),
    )
    alive = jnp.sum(device_vis.reshape(count, per_stretch), axis=-1) > 0
    return (items, alive, size)


def masked_scores(queries, key_part, vis_part, seq_part, own_seq):
    scores = jnp.einsum(
        "nkgd,mkd->kgnm", queries, key_part, preferred_element_type=jnp.float32
    ) * HD ** (-0.5)
    allowed = (vis_part[None, :] == 1) & (own_seq[:, None] == seq_part[None, :])
    return (jnp.where(allowed[None, None], scores, NEG), allowed)


def attention_forward(queries, key_rows, value_rows, info, per_stretch, rows):
    own_seq = info[0]
    items, alive, size = key_items(key_rows, value_rows, info, per_stretch, rows)
    group = H // KV

    def lse_step(state, item):
        high, total = state
        key_part, value_part, vis_part, seq_part = item
        masked, allowed = masked_scores(queries, key_part, vis_part, seq_part, own_seq)
        top = jnp.maximum(high, jnp.max(masked, axis=-1))
        terms = jnp.where(allowed[None, None], jnp.exp(masked - top[..., None]), 0.0)
        return ((top, total * jnp.exp(high - top) + jnp.sum(terms, axis=-1)), None)

    start_state = (
        jnp.full((KV, group, rows), NEG, jnp.float32),
        jnp.zeros((KV, group, rows), jnp.float32),
    )
    (high, total), unused = sweep(lse_step, start_state, items, alive)
    log_total = high + jnp.log(total)

    def out_step(acc, item):
        key_part, value_part, vis_part, seq_part = item
        masked, allowed = masked_scores(queries, key_part, vis_part, seq_part, own_seq)
        probs = jnp.where(allowed[None, None], jnp.exp(masked - log_total[..., None]), 0.0).astype(
            jnp.bfloat16
        )
        return (
            acc
            + jnp.einsum("kgnm,mkd->nkgd", probs, value_part, preferred_element_type=jnp.float32),
            None,
        )

    attended, unused_two = sweep(
        out_step, jnp.zeros((rows, KV, group, HD), jnp.float32), items, alive
    )
    return (attended, log_total)


def attention_backward(
    queries, key_rows, value_rows, info, per_stretch, rows, log_total, grad_att, delta
):
    own_seq = info[0]
    items, alive, size = key_items(key_rows, value_rows, info, per_stretch, rows)
    group = H // KV

    def back_step(grad_query, item):
        key_part, value_part, vis_part, seq_part = item
        masked, allowed = masked_scores(queries, key_part, vis_part, seq_part, own_seq)
        probs = jnp.where(allowed[None, None], jnp.exp(masked - log_total[..., None]), 0.0)
        probs_low = probs.astype(jnp.bfloat16)
        grad_probs = jnp.einsum(
            "nkgd,mkd->kgnm", grad_att, value_part, preferred_element_type=jnp.float32
        )
        grad_scores = (probs * (grad_probs - delta[..., None])).astype(jnp.bfloat16)
        grad_query = grad_query + jnp.einsum(
            "kgnm,mkd->nkgd", grad_scores, key_part, preferred_element_type=jnp.float32
        ) * HD ** (-0.5)
        grad_keys = jnp.einsum(
            "kgnm,nkgd->mkd", grad_scores, queries, preferred_element_type=jnp.float32
        ) * HD ** (-0.5)
        grad_values = jnp.einsum(
            "kgnm,nkgd->mkd", probs_low, grad_att, preferred_element_type=jnp.float32
        )
        return (grad_query, (grad_keys, grad_values))

    grad_query, (grad_keys, grad_values) = sweep(
        back_step, jnp.zeros((rows, KV, group, HD), jnp.float32), items, alive
    )
    length = key_rows.shape[0]
    return (grad_query, grad_keys.reshape(length, KV, HD), grad_values.reshape(length, KV, HD))


def layer_forward(hidden, weights, info, positions, per_stretch, rows):
    w_qkv, w_out, w_gate_up, w_down, gains = weights
    query_width = H * HD
    key_width = KV * HD
    gain_attn = gains[0].astype(jnp.float32)
    gain_ffn = gains[1].astype(jnp.float32)
    normed, unit_one, inverse_one = rms_forward(hidden, gain_attn)
    normed_low = normed.astype(jnp.bfloat16)
    mixed = jnp.dot(normed_low, w_qkv, preferred_element_type=jnp.float32)
    cosine, sine = rotation(positions)
    queries = (
        rotate(mixed[:, :query_width].reshape(rows, H, HD), cosine, sine)
        .astype(jnp.bfloat16)
        .reshape(rows, KV, H // KV, HD)
    )
    key_own = rotate(
        mixed[:, query_width : query_width + key_width].reshape(rows, KV, HD), cosine, sine
    ).astype(jnp.bfloat16)
    value_own = mixed[:, query_width + key_width :].reshape(rows, KV, HD).astype(jnp.bfloat16)
    key_rows, value_rows = (
        lax.all_gather(key_own, "ctx", axis=0, tiled=True),
        lax.all_gather(value_own, "ctx", axis=0, tiled=True),
    )
    attended, log_total = attention_forward(queries, key_rows, value_rows, info, per_stretch, rows)
    attended_low = attended.reshape(rows, query_width).astype(jnp.bfloat16)
    middle = hidden + jnp.dot(attended_low, w_out, preferred_element_type=jnp.float32)
    normed_two, unit_two, inverse_two = rms_forward(middle, gain_ffn)
    normed_two_low = normed_two.astype(jnp.bfloat16)
    gate_up = jnp.dot(normed_two_low, w_gate_up, preferred_element_type=jnp.float32)
    gate_part = gate_up[:, :FF]
    up_part = gate_up[:, FF:]
    units_low = (jax.nn.silu(gate_part) * up_part).astype(jnp.bfloat16)
    result = middle + jnp.dot(units_low, w_down, preferred_element_type=jnp.float32)
    saved = {
        "unit_one": unit_one,
        "inverse_one": inverse_one,
        "normed_low": normed_low,
        "cosine": cosine,
        "sine": sine,
        "queries": queries,
        "key_rows": key_rows,
        "value_rows": value_rows,
        "attended": attended,
        "log_total": log_total,
        "attended_low": attended_low,
        "unit_two": unit_two,
        "inverse_two": inverse_two,
        "normed_two_low": normed_two_low,
        "gate_part": gate_part,
        "up_part": up_part,
        "units_low": units_low,
    }
    return (result, saved)


def layer_backward(grad_rows, weights, saved, info, per_stretch, rows):
    w_qkv, w_out, w_gate_up, w_down, gains = weights
    query_width = H * HD
    gain_attn = gains[0].astype(jnp.float32)
    gain_ffn = gains[1].astype(jnp.float32)
    gate_part = saved["gate_part"]
    grad_low = grad_rows.astype(jnp.bfloat16)
    grad_units = jnp.dot(grad_low, w_down.T, preferred_element_type=jnp.float32)
    sigmoid = jax.nn.sigmoid(gate_part)
    grad_gate = grad_units * saved["up_part"] * sigmoid * (1.0 + gate_part * (1.0 - sigmoid))
    grad_up = grad_units * gate_part * sigmoid
    grad_mix_low = jnp.concatenate([grad_gate, grad_up], axis=-1).astype(jnp.bfloat16)
    grad_normed_two = jnp.dot(grad_mix_low, w_gate_up.T, preferred_element_type=jnp.float32)
    grad_mid_norm, grad_gain_two = rms_backward(
        grad_normed_two, saved["unit_two"], saved["inverse_two"], gain_ffn
    )
    grad_middle = grad_rows + grad_mid_norm
    grad_branch_low = grad_middle.astype(jnp.bfloat16)
    grad_att = (
        jnp.dot(grad_branch_low, w_out.T, preferred_element_type=jnp.float32)
        .astype(jnp.bfloat16)
        .reshape(rows, KV, H // KV, HD)
    )
    delta = jnp.einsum("nkgd,nkgd->kgn", grad_att.astype(jnp.float32), saved["attended"])
    grad_query, grad_keys, grad_values = attention_backward(
        saved["queries"],
        saved["key_rows"],
        saved["value_rows"],
        info,
        per_stretch,
        rows,
        saved["log_total"],
        grad_att,
        delta,
    )
    key_total, value_total = (
        lax.psum_scatter(
            grad_keys.astype(jnp.bfloat16), "ctx", scatter_dimension=0, tiled=True
        ).astype(jnp.float32),
        lax.psum_scatter(
            grad_values.astype(jnp.bfloat16), "ctx", scatter_dimension=0, tiled=True
        ).astype(jnp.float32),
    )
    cosine = saved["cosine"]
    back_sine = -saved["sine"]
    grad_q = rotate(grad_query.reshape(rows, H, HD), cosine, back_sine).reshape(rows, query_width)
    grad_k = rotate(key_total, cosine, back_sine).reshape(rows, KV * HD)
    grad_v = value_total.reshape(rows, KV * HD)
    grad_qkv_low = jnp.concatenate([grad_q, grad_k, grad_v], axis=-1).astype(jnp.bfloat16)
    grad_normed = jnp.dot(grad_qkv_low, w_qkv.T, preferred_element_type=jnp.float32)
    grad_in_norm, grad_gain_one = rms_backward(
        grad_normed, saved["unit_one"], saved["inverse_one"], gain_attn
    )
    grad_hidden = grad_middle + grad_in_norm
    pairs = (
        saved["normed_low"],
        grad_qkv_low,
        saved["attended_low"],
        grad_branch_low,
        saved["normed_two_low"],
        grad_mix_low,
        saved["units_low"],
        grad_low,
        grad_gain_one,
        grad_gain_two,
    )
    return (grad_hidden, pairs)


def weight_terms(pairs):
    (
        normed_low,
        grad_qkv_low,
        attended_low,
        grad_branch_low,
        normed_two_low,
        grad_mix_low,
        units_low,
        grad_low,
        grad_gain_one,
        grad_gain_two,
    ) = pairs
    return (
        jnp.dot(normed_low.T, grad_qkv_low, preferred_element_type=jnp.float32),
        jnp.dot(attended_low.T, grad_branch_low, preferred_element_type=jnp.float32),
        jnp.dot(normed_two_low.T, grad_mix_low, preferred_element_type=jnp.float32),
        jnp.dot(units_low.T, grad_low, preferred_element_type=jnp.float32),
        jnp.stack([grad_gain_one, grad_gain_two]),
    )


def on_device_general(x_in, cotangent, w_qkv, w_out, w_gate_up, w_down, gains, order, visible, seq_ids):
    section = lax.axis_index("section")
    column = lax.axis_index("ctx")
    n_ctx = lax.axis_size("ctx")
    batches = x_in.shape[0]
    rows = x_in.shape[2]
    per_stretch = stretch_width(rows, n_ctx)
    first_section = section == 0
    weights = (
        lax.all_gather(w_qkv[0], "wsh", axis=0, tiled=True),
        lax.all_gather(w_out[0], "wsh", axis=1, tiled=True),
        lax.all_gather(w_gate_up[0], "wsh", axis=0, tiled=True),
        lax.all_gather(w_down[0], "wsh", axis=1, tiled=True),
        lax.all_gather(gains[0], "wsh", axis=1, tiled=True),
    )
    incoming = jnp.zeros((rows, D), jnp.bfloat16)
    section_inputs = []
    section_outputs = []
    for tick_now in range(batches + 1):
        batch_index = jnp.clip(tick_now - section, 0, batches - 1)
        info, positions = tables(order, visible, seq_ids, batch_index, column, rows, n_ctx)
        source = jnp.where(first_section, x_in[batch_index, 0], incoming)
        result, unused = layer_forward(
            source.astype(jnp.float32), weights, info, positions, per_stretch, rows
        )
        result_low = result.astype(jnp.bfloat16)
        section_inputs.append(source)
        section_outputs.append(result_low)
        if tick_now < batches:
            incoming = shifted(result_low, "section", 1)
    activations = jnp.stack(
        [
            jnp.where(first_section, section_outputs[batch], section_outputs[batch + 1])
            for batch in range(batches)
        ]
    )
    back_weights = (
        lax.all_gather(w_qkv[0], "wsh", axis=0, tiled=True),
        lax.all_gather(w_out[0], "wsh", axis=1, tiled=True),
        lax.all_gather(w_gate_up[0], "wsh", axis=0, tiled=True),
        lax.all_gather(w_down[0], "wsh", axis=1, tiled=True),
        lax.all_gather(gains[0], "wsh", axis=1, tiled=True),
    )
    returned = jnp.zeros((rows, D), jnp.bfloat16)
    grad_list = []
    totals = None
    for tick_now in range(batches + 1):
        raw_index = tick_now - 1 + section
        valid = (raw_index >= 0) & (raw_index < batches)
        batch_index = jnp.clip(raw_index, 0, batches - 1)
        info, positions = tables(order, visible, seq_ids, batch_index, column, rows, n_ctx)
        source = jnp.where(
            first_section,
            section_inputs[max(tick_now - 1, 0)],
            section_inputs[min(tick_now + 1, batches)],
        )
        unused, saved = layer_forward(
            source.astype(jnp.float32), back_weights, info, positions, per_stretch, rows
        )
        grad_rows = jnp.where(first_section, returned, cotangent[batch_index, 0]).astype(
            jnp.float32
        ) * valid.astype(jnp.float32)
        grad_hidden, pairs = layer_backward(grad_rows, back_weights, saved, info, per_stretch, rows)
        grad_hidden_low = grad_hidden.astype(jnp.bfloat16)
        grad_list.append((grad_hidden, grad_hidden_low))
        if tick_now < batches:
            returned = shifted(grad_hidden_low, "section", -1)
        terms = weight_terms(pairs)
        totals = terms if totals is None else jax.tree.map(jnp.add, totals, terms)
    input_grads = jnp.stack(
        [
            jnp.where(
                first_section, grad_list[batch + 1][0], grad_list[batch][1].astype(jnp.float32)
            )
            for batch in range(batches)
        ]
    )
    term_qkv, term_out, term_gate_up, term_down, term_gains = totals
    shares = (
        lax.psum_scatter(term_qkv, ("ctx", "wsh"), scatter_dimension=0, tiled=True),
        lax.psum_scatter(term_out, ("ctx", "wsh"), scatter_dimension=1, tiled=True),
        lax.psum_scatter(term_gate_up, ("ctx", "wsh"), scatter_dimension=0, tiled=True),
        lax.psum_scatter(term_down, ("ctx", "wsh"), scatter_dimension=1, tiled=True),
        lax.psum_scatter(term_gains, ("ctx", "wsh"), scatter_dimension=1, tiled=True),
    )
    return (
        activations[None, :, None],
        input_grads[None, :, None],
        shares[0][None],
        shares[1][None],
        shares[2][None],
        shares[3][None],
        shares[4][None],
    )


GROUP = H // KV
QD = H * HD
KD = KV * HD
QKV = QD + 2 * KD
SIDE = 128
LOW = jnp.bfloat16


def fits_pairs(mesh):
    return mesh.shape["section"] == 2 and mesh.shape["ctx"] == 4 and mesh.shape["wsh"] == 4


def contract(left, right, left_dim, right_dim):
    return lax.dot_general(
        left,
        right,
        (((left_dim,), (right_dim,)), ((), ())),
        preferred_element_type=jnp.float32,
    )


def swap(value, axis, bit):
    return lax.ppermute(value, axis, [(i, i ^ bit) for i in range(lax.axis_size(axis))])


def after(value, *others):
    return lax.optimization_barrier((value, *others))[0]


def fill_bias(bias_ref, kseq_ref, qseq_ref):
    @pl.when(pl.program_id(0) == 0)
    def _():
        for slot in range(bias_ref.shape[0]):
            bias_ref[slot] = jnp.where(kseq_ref[slot][:, :1] == qseq_ref[...], 0.0, NEG)


def forward_kernel(live_ref, q_ref, k_ref, v_ref, kseq_ref, qseq_ref, o_ref, lse_ref, bias_ref):
    fill_bias(bias_ref, kseq_ref, qseq_ref)
    rows = q_ref.shape[1]
    queries = [q_ref[pl.ds(j * HD, HD), :] for j in range(GROUP)]

    def step(i, states):
        slot = live_ref[1 + i]
        key_t = k_ref[slot, 0]
        value_t = v_ref[slot, 0]
        new_states = []
        for j in range(GROUP):
            high, total, acc = states[j]
            scores = contract(key_t, queries[j], 0, 0) + bias_ref[slot]
            top = jnp.maximum(high, jnp.max(scores, axis=0, keepdims=True))
            terms = jnp.exp(scores - top)
            scale = jnp.exp(high - top)
            total = total * scale + jnp.sum(terms, axis=0, keepdims=True)
            acc = acc * scale + contract(value_t, terms.astype(LOW), 1, 0)
            new_states.append((top, total, acc))
        return tuple(new_states)

    start = (
        jnp.full((1, rows), NEG, jnp.float32),
        jnp.zeros((1, rows), jnp.float32),
        jnp.zeros((HD, rows), jnp.float32),
    )
    states = lax.fori_loop(0, live_ref[0], step, (start,) * GROUP)
    for j in range(GROUP):
        high, total, acc = states[j]
        o_ref[pl.ds(j * HD, HD), :] = (acc / total).astype(o_ref.dtype)
        lse_ref[0, pl.ds(j, 1), :] = high + jnp.log(total)


def backward_kernel(
    live_ref,
    q_ref,
    do_ref,
    o_ref,
    lse_ref,
    k_ref,
    v_ref,
    kseq_ref,
    qseq_ref,
    dq_ref,
    dk_ref,
    dv_ref,
    bias_ref,
    acc_ref,
):
    fill_bias(bias_ref, kseq_ref, qseq_ref)
    keys = bias_ref.shape[1]
    acc_ref[...] = jnp.zeros_like(acc_ref)
    dk_ref[...] = jnp.zeros_like(dk_ref)
    dv_ref[...] = jnp.zeros_like(dv_ref)
    deltas = []
    for j in range(GROUP):
        part = pl.ds(j * HD, HD)
        both = do_ref[part, :].astype(jnp.float32) * o_ref[part, :].astype(jnp.float32)
        deltas.append(jnp.sum(both, axis=0, keepdims=True))

    def step(i, carry):
        slot = live_ref[1 + i]
        key_t = k_ref[slot, 0]
        value_t = v_ref[slot, 0]
        grad_k = jnp.zeros((keys, HD), jnp.float32)
        grad_v = jnp.zeros((keys, HD), jnp.float32)
        for j in range(GROUP):
            part = pl.ds(j * HD, HD)
            query_t = q_ref[part, :]
            grad_t = do_ref[part, :]
            scores = contract(key_t, query_t, 0, 0) + bias_ref[slot]
            probs = jnp.exp(scores - lse_ref[0, pl.ds(j, 1), :])
            grad_probs = contract(value_t, grad_t, 0, 0)
            grad_scores = (probs * (grad_probs - deltas[j])).astype(LOW)
            grad_v = grad_v + contract(probs.astype(LOW), grad_t, 1, 1)
            grad_k = grad_k + contract(grad_scores, query_t, 1, 1)
            acc_ref[part, :] += contract(key_t, grad_scores, 1, 0)
        dk_ref[slot, 0] = jnp.transpose(grad_k).astype(LOW)
        dv_ref[slot, 0] = jnp.transpose(grad_v).astype(LOW)
        return carry

    lax.fori_loop(0, live_ref[0], step, 0)
    dq_ref[...] = acc_ref[...] * HD ** (-0.5)


def kernel_cost(scores, matmuls):
    return pl.CostEstimate(
        flops=scores * matmuls * HD * 2 * 4, bytes_accessed=12 * 2**20, transcendentals=scores
    )


def pair_attention_forward(info, q_t, kv_t):
    live, key_seq, own_seq = info
    slots, keys = kv_t.shape[0], kv_t.shape[3]
    rows = q_t.shape[1]
    return pl.pallas_call(
        forward_kernel,
        grid_spec=pltpu.PrefetchScalarGridSpec(
            num_scalar_prefetch=1,
            grid=(KV,),
            in_specs=[
                pl.BlockSpec((GROUP * HD, rows), lambda g, l: (g, 0)),
                pl.BlockSpec((slots, 1, HD, keys), lambda g, l: (0, g, 0, 0)),
                pl.BlockSpec((slots, 1, HD, keys), lambda g, l: (0, KV + g, 0, 0)),
                pl.BlockSpec((slots, keys, SIDE), lambda g, l: (0, 0, 0)),
                pl.BlockSpec((1, rows), lambda g, l: (0, 0)),
            ],
            out_specs=[
                pl.BlockSpec((GROUP * HD, rows), lambda g, l: (g, 0)),
                pl.BlockSpec((1, GROUP, rows), lambda g, l: (g, 0, 0)),
            ],
            scratch_shapes=[pltpu.VMEM((slots, keys, rows), jnp.float32)],
        ),
        out_shape=[
            jax.ShapeDtypeStruct(q_t.shape, LOW),
            jax.ShapeDtypeStruct((KV, GROUP, rows), jnp.float32),
        ],
        compiler_params=pltpu.CompilerParams(vmem_limit_bytes=48 * 2**20),
        cost_estimate=kernel_cost(H * rows * slots * keys, 2),
    )(live, q_t, kv_t, kv_t, key_seq, own_seq)


def pair_attention_backward(info, q_t, do_t, o_t, lse, kv_t):
    live, key_seq, own_seq = info
    slots, keys = kv_t.shape[0], kv_t.shape[3]
    rows = q_t.shape[1]
    q_spec = pl.BlockSpec((GROUP * HD, rows), lambda g, l: (g, 0))
    part_spec = pl.BlockSpec((slots, 1, HD, keys), lambda g, l: (0, g, 0, 0))
    part_shape = jax.ShapeDtypeStruct((slots, KV, HD, keys), LOW)
    return pl.pallas_call(
        backward_kernel,
        grid_spec=pltpu.PrefetchScalarGridSpec(
            num_scalar_prefetch=1,
            grid=(KV,),
            in_specs=[
                q_spec,
                q_spec,
                q_spec,
                pl.BlockSpec((1, GROUP, rows), lambda g, l: (g, 0, 0)),
                part_spec,
                pl.BlockSpec((slots, 1, HD, keys), lambda g, l: (0, KV + g, 0, 0)),
                pl.BlockSpec((slots, keys, SIDE), lambda g, l: (0, 0, 0)),
                pl.BlockSpec((1, rows), lambda g, l: (0, 0)),
            ],
            out_specs=[q_spec, part_spec, part_spec],
            scratch_shapes=[
                pltpu.VMEM((slots, keys, rows), jnp.float32),
                pltpu.VMEM((GROUP * HD, rows), jnp.float32),
            ],
        ),
        out_shape=[jax.ShapeDtypeStruct(q_t.shape, jnp.float32), part_shape, part_shape],
        compiler_params=pltpu.CompilerParams(vmem_limit_bytes=48 * 2**20),
        cost_estimate=kernel_cost(H * rows * slots * keys, 5),
    )(live, q_t, do_t, o_t, lse, kv_t, kv_t, key_seq, own_seq)


def turn(heads, cosine, sine):
    half = HD // 2
    first, second = heads[:, :half], heads[:, half:]
    return jnp.concatenate(
        [first * cosine - second * sine, first * sine + second * cosine], axis=1
    )


def one_hot(index, size):
    return (index[:, None] == jnp.arange(size, dtype=jnp.int32)[None, :]).astype(LOW)


def pair_tables(order, visible, seq_ids, batch, slot, rows):
    order_row = order[batch]
    order_slots = [order_row[slot ^ step] for step in (0, 2, 1, 3)]
    own_block = order_slots[0]
    seqs = [
        lax.dynamic_slice_in_dim(seq_ids, (slot ^ step) * rows, rows) for step in (0, 2, 1, 3)
    ]
    has = [(jnp.any(s == 0), jnp.any(s == 1)) for s in seqs]
    alive = []
    for block, (zero, one) in zip(order_slots, has):
        shares = (zero & has[0][0]) | (one & has[0][1])
        alive.append((visible[own_block, block] == 1) & shares)
    alive[0] = jnp.bool_(True)
    alive = jnp.stack(alive).astype(jnp.int32)
    place = jnp.cumsum(alive) - 1
    ids = jnp.arange(4, dtype=jnp.int32)
    listed = jnp.sum(
        jnp.where((place[None, :] == ids[:, None]) & (alive[None, :] == 1), ids[None, :], 0),
        axis=1,
    )
    live = jnp.concatenate([jnp.sum(alive, keepdims=True), listed]).astype(jnp.int32)
    key_seq = jnp.broadcast_to(
        jnp.stack(seqs).astype(jnp.float32)[:, :, None], (4, rows, SIDE)
    )
    own_seq = seqs[0].astype(jnp.float32)[None]
    positions = own_block * rows + jnp.arange(rows, dtype=jnp.int32)
    frequency = 10000.0 ** (-(jnp.arange(HD // 2, dtype=jnp.float32) * 2.0 / HD))
    angles = frequency[:, None] * positions.astype(jnp.float32)[None, :]
    return (live, key_seq, own_seq), (jnp.cos(angles), jnp.sin(angles))


MESH_ID = pl.DeviceIdType.MESH
PIECE = 1024


def stream_partner(column, place):
    core = place % 2
    moving = (column < 2) == (core == 1)
    return moving, lax.rem(column + 2, 4), place + 1 - 2 * core


def gather_kernel(*refs):
    rows_refs, shard_refs = refs[:2], refs[2:6]
    full_refs, moved_refs = refs[6:11], refs[11:13]
    send_sem, recv_sem, local_sem = refs[13:16]
    held_refs, held_rows = refs[16:20], refs[20:22]
    section = lax.axis_index("section")
    column = lax.axis_index("ctx")
    place = lax.axis_index("wsh")
    half = lax.rem(column, 2)
    over_x = (section, column, lax.rem(place + 2, 4))
    over_y = (1 - section, column, place)
    over_z = (section, column + 1 - 2 * half, place)
    over_core = (section, column, place + 1 - 2 * lax.rem(place, 2))
    moving, partner_column, partner_place = stream_partner(column, place)
    partner = (section, partner_column, partner_place)

    barrier = pltpu.get_barrier_semaphore()
    for target in (over_x, over_y, over_z, over_core):
        pl.semaphore_signal(barrier, inc=1, device_id=target, device_id_type=MESH_ID)

    @pl.when(moving)
    def _():
        pl.semaphore_signal(barrier, inc=1, device_id=partner, device_id_type=MESH_ID)
        pl.semaphore_wait(barrier, 5)

    @pl.when(jnp.logical_not(moving))
    def _():
        pl.semaphore_wait(barrier, 4)

    in_ref, out_ref, gate_up_ref, down_ref = shard_refs
    sources = [
        (in_ref, 0, full_refs[0]),
        (out_ref, 0, full_refs[1]),
        (gate_up_ref, 0, full_refs[2]),
        (gate_up_ref, FF, full_refs[3]),
        (down_ref, 0, full_refs[4]),
    ]
    pieces = []
    for shard_ref, offset, full_ref in sources:
        width = full_ref.shape[3]
        step = PIECE if width % PIECE == 0 else width
        for first in range(0, width, step):
            pieces.append((shard_ref, offset + first, full_ref, first, step))
    count = len(pieces)
    quarter = shard_refs[0].shape[0]
    mid = quarter // 2

    def own(k):
        shard_ref, offset, full_ref, first, step = pieces[k]
        return shard_ref.at[:, pl.ds(offset, step)]

    def own_half(k):
        shard_ref, offset, full_ref, first, step = pieces[k]
        return shard_ref.at[pl.ds(half * mid, mid), pl.ds(offset, step)]

    def full(k, layer, block):
        shard_ref, offset, full_ref, first, step = pieces[k]
        return full_ref.at[layer, block, :, pl.ds(first, step)]

    def full_half(k, layer, block, which):
        shard_ref, offset, full_ref, first, step = pieces[k]
        return full_ref.at[layer, block, pl.ds(which * mid, mid), pl.ds(first, step)]

    started = {}

    def send(kind, k, source, target, device):
        copy = pltpu.make_async_remote_copy(
            src_ref=source,
            dst_ref=target,
            send_sem=send_sem.at[kind, k],
            recv_sem=recv_sem.at[kind, k],
            device_id=device,
            device_id_type=MESH_ID,
        )
        copy.start()
        started[kind, k] = copy

    other = 1 - section

    def start_near(k):
        send(0, k, own(k), full(k, section, 2), over_x)

    def start_cross(k):
        send(1, k, own_half(k), full_half(k, section, 0, half), over_y)

    def row_copies():
        return [
            pltpu.make_async_remote_copy(
                src_ref=rows_refs[i].at[section, 0],
                dst_ref=moved_refs[i],
                send_sem=send_sem.at[11, i],
                recv_sem=recv_sem.at[11, i],
                device_id=partner,
                device_id_type=MESH_ID,
            )
            for i in range(2)
        ]

    loads = [
        pltpu.make_async_copy(shard_refs[i], held_refs[i], local_sem.at[count + i])
        for i in range(4)
    ]
    row_loads = [
        pltpu.make_async_copy(
            rows_refs[i].at[section, 0], held_rows[i], local_sem.at[count + 4 + i]
        )
        for i in range(2)
    ]
    row_stores = [
        pltpu.make_async_copy(held_rows[i], moved_refs[i], local_sem.at[count + 4 + i])
        for i in range(2)
    ]
    for copy in loads:
        copy.start()

    for k in range(2):
        start_near(k)
        start_cross(k)

    @pl.when(moving)
    def _():
        for copy in row_copies():
            copy.start()

    @pl.when(jnp.logical_not(moving))
    def _():
        for copy in row_loads:
            copy.start()
        for copy, store in zip(row_loads, row_stores):
            copy.wait()
            store.start()

    for copy in loads:
        copy.wait()
    stores = []
    for k in range(count):
        shard_ref, offset, full_ref, first, step = pieces[k]
        held_ref = held_refs[[i for i in range(4) if shard_refs[i] is shard_ref][0]]
        copy = pltpu.make_async_copy(
            held_ref.at[:, pl.ds(offset, step)], full(k, section, 0), local_sem.at[k]
        )
        copy.start()
        stores.append(copy)
        send(5, k, own(k), full(k, section, 1), over_core)

    for k in range(count + 2):
        if k < count:
            started[0, k].wait_recv()
            send(
                2,
                k,
                full_half(k, section, 2, half),
                full_half(k, section, 2, half),
                over_y,
            )
            send(6, k, full(k, section, 2), full(k, section, 3), over_core)
            if k + 2 < count:
                start_near(k + 2)
            started[1, k].wait_recv()
            send(
                3, k, full_half(k, other, 0, half), full_half(k, other, 0, half), over_z
            )
            send(
                7, k, full_half(k, other, 0, half), full_half(k, other, 1, half), over_core
            )
            if k + 2 < count:
                start_cross(k + 2)
        j = k - 1
        if 0 <= j < count:
            started[2, j].wait_recv()
            send(
                4, j, full_half(j, other, 2, half), full_half(j, other, 2, half), over_z
            )
            send(
                8, j, full_half(j, other, 2, half), full_half(j, other, 3, half), over_core
            )
            started[3, j].wait_recv()
            send(
                9,
                j,
                full_half(j, other, 0, 1 - half),
                full_half(j, other, 1, 1 - half),
                over_core,
            )
        j = k - 2
        if 0 <= j < count:
            started[4, j].wait_recv()
            send(
                10,
                j,
                full_half(j, other, 2, 1 - half),
                full_half(j, other, 3, 1 - half),
                over_core,
            )
    for (kind, k), copy in started.items():
        if kind >= 5:
            copy.wait_recv()
        copy.wait_send()
    for copy in stores:
        copy.wait()

    @pl.when(moving)
    def _():
        for copy in row_copies():
            copy.wait()

    @pl.when(jnp.logical_not(moving))
    def _():
        for copy in row_stores:
            copy.wait()


def gather_all(rows_in, shards):
    widths = [shards[0].shape[1], shards[1].shape[1], FF, FF, shards[3].shape[1]]
    quarter = shards[0].shape[0]
    batch_rows = rows_in[0].shape[2:]
    anywhere = pl.BlockSpec(memory_space=pl.ANY)
    count = sum(w // PIECE if w % PIECE == 0 else 1 for w in widths)
    outs = pl.pallas_call(
        gather_kernel,
        out_shape=[jax.ShapeDtypeStruct((2, 4, quarter, w), LOW) for w in widths]
        + [jax.ShapeDtypeStruct(batch_rows, LOW)] * 2,
        in_specs=[anywhere] * 6,
        out_specs=[anywhere] * 7,
        scratch_shapes=[
            pltpu.SemaphoreType.DMA((12, count)),
            pltpu.SemaphoreType.DMA((12, count)),
            pltpu.SemaphoreType.DMA((count + 6,)),
        ]
        + [pltpu.VMEM(shard.shape, LOW) for shard in shards]
        + [pltpu.VMEM(batch_rows, LOW)] * 2,
        compiler_params=pltpu.CompilerParams(collective_id=1, has_side_effects=True),
    )(*rows_in, *shards)
    full = outs[:5]
    weights = [[w[layer].reshape(4 * quarter, -1) for w in full] for layer in range(2)]
    return weights, outs[5], outs[6]


def unpack(weights):
    w_in, w_out_t, w_gate, w_up, w_down_t = weights
    gain_one = w_in[:, QKV].astype(jnp.float32)
    gain_two = w_in[:, QKV + 1].astype(jnp.float32)
    return w_in, w_out_t, w_gate, w_up, w_down_t, gain_one, gain_two


def pair_forward(hidden, weights, info, angles):
    w_in, w_out_t, w_gate, w_up, w_down_t, gain_one, gain_two = unpack(weights)
    rows = hidden.shape[0]
    cosine, sine = angles
    normed, unused, inverse_one = rms_forward(hidden, gain_one)
    normed = normed.astype(LOW)
    kv = contract(w_in[:, QD:QKV], normed, 0, 1).reshape(2 * KV, HD, rows)
    kv_own = jnp.concatenate([turn(kv[:KV], cosine, sine), kv[KV:]], axis=0).astype(LOW)
    kv_far = swap(kv_own, "ctx", 1)
    kv_near = swap(kv_own, "wsh", 1)
    kv_last = swap(kv_far, "wsh", 1)
    q = contract(w_in[:, :QD], normed, 0, 1).reshape(H, HD, rows)
    q_t = (turn(q, cosine, sine).astype(LOW) * HD ** (-0.5)).reshape(QD, rows)
    kv_t = jnp.stack([kv_own, kv_near, kv_far, kv_last])
    o_t, lse = pair_attention_forward(info, q_t, kv_t)
    middle = hidden + contract(o_t, w_out_t, 0, 1)
    normed_two, unused, inverse_two = rms_forward(middle, gain_two)
    normed_two = normed_two.astype(LOW)
    gate = contract(normed_two, w_gate, 1, 0).astype(LOW)
    up = contract(normed_two, w_up, 1, 0).astype(LOW)
    gate_wide = gate.astype(jnp.float32)
    units = (jax.nn.silu(gate_wide) * up.astype(jnp.float32)).astype(LOW)
    result = (middle + contract(units, w_down_t, 1, 1)).astype(LOW)
    saved = (hidden, inverse_one, normed, q_t, kv_t, o_t, lse, middle, inverse_two, normed_two)
    return result, saved + (gate, up, units)


TILE = 384
CROSSED = 22
PLANE = 11


def spread_kernel(
    lhs_all,
    rhs_all,
    out_ref,
    rhs_peer,
    lhs_ref,
    rhs_ref,
    given_ref,
    sum_ref,
    side_ref,
    block_ref,
    last_given,
    last_ref,
    lhs_sem,
    peer_send,
    peer_recv,
    load_sem,
    given_send,
    given_recv,
    side_send,
    side_recv,
    block_send,
    block_recv,
    last_send,
    last_recv,
):
    section = lax.axis_index("section")
    column = lax.axis_index("ctx")
    place = lax.axis_index("wsh")
    other = 1 - section
    over_x = (section, column, lax.rem(place + 2, 4))
    over_y = (other, column, place)
    over_core = (section, column, place + 1 - 2 * lax.rem(place, 2))
    flip_low = column + 1 - 2 * lax.rem(column, 2)
    flip_high = lax.rem(column + 2, 4)
    flip_both = lax.rem(flip_low + 2, 4)
    over_z = [(section, c, place) for c in (flip_low, flip_high, flip_both)]

    barrier = pltpu.get_barrier_semaphore()
    for target in (over_x, over_y, over_core, *over_z):
        pl.semaphore_signal(barrier, inc=1, device_id=target, device_id_type=MESH_ID)
    pl.semaphore_wait(barrier, 6)

    half = lhs_all.shape[2] // 2
    tokens = lhs_all.shape[3]
    quarter = half // 2
    share = quarter // 4
    layers = (section, other)

    def remote(source, target, send_sem, recv_sem, device):
        return pltpu.make_async_remote_copy(
            src_ref=source,
            dst_ref=target,
            send_sem=send_sem,
            recv_sem=recv_sem,
            device_id=device,
            device_id_type=MESH_ID,
        )

    def lhs_copies():
        copies = []
        for which in range(2):
            copies.append(
                pltpu.make_async_copy(
                    lhs_all.at[layers[which], :, pl.ds(half, half), :],
                    lhs_ref.at[which, :, :, pl.ds(0, tokens)],
                    lhs_sem.at[which],
                )
            )
            copies.append(
                remote(
                    lhs_all.at[layers[which], :, pl.ds(0, half), :],
                    lhs_ref.at[which, :, :, pl.ds(tokens, tokens)],
                    lhs_sem.at[2 + which],
                    lhs_sem.at[4 + which],
                    over_core,
                )
            )
        return copies

    def peer_copy(which, tile):
        return remote(
            rhs_all.at[layers[which], tile],
            rhs_peer.at[layers[which], tile],
            peer_send.at[which, tile],
            peer_recv.at[which, tile],
            over_core,
        )

    def peer_starts(i):
        for tile in (2 * i, 2 * i + 1, CROSSED + i):
            for which in range(2):
                peer_copy(1 - which, tile).start()

    def loads(slot, which, tile):
        return (
            pltpu.make_async_copy(
                rhs_all.at[layers[which], tile],
                rhs_ref.at[slot, pl.ds(0, tokens)],
                load_sem.at[slot, 0],
            ),
            pltpu.make_async_copy(
                rhs_peer.at[layers[which], tile],
                rhs_ref.at[slot, pl.ds(tokens, tokens)],
                load_sem.at[slot, 1],
            ),
        )

    def load_start(slot, which, tile):
        own, peer = loads(slot, which, tile)
        own.start()
        peer_copy(which, tile).wait_recv()
        peer.start()

    def product(slot, which, tile, kind):
        for copy in loads(slot, which, tile):
            copy.wait()
        return jnp.dot(
            lhs_ref[which, kind], rhs_ref[slot], preferred_element_type=jnp.float32
        )

    def crossed_kind(tile):
        return jnp.where(tile < 16, 0, jnp.where(tile < 21, 1, 2))

    def plane_kind(i):
        return jnp.where(i < 8, 3, 4)

    def given_copy(tile):
        slot = lax.rem(tile, 4)
        return remote(
            given_ref.at[slot],
            sum_ref.at[tile],
            given_send.at[slot],
            given_recv.at[tile],
            over_y,
        )

    def side_copy(unit):
        return remote(
            sum_ref.at[unit, pl.ds(0, quarter)],
            side_ref.at[unit // 2, pl.ds(lax.rem(unit, 2) * quarter, quarter)],
            side_send.at[unit],
            side_recv.at[unit],
            over_x,
        )

    def block_copy(pair, k):
        return remote(
            side_ref.at[pair, pl.ds((k + 1) * 2 * share, 2 * share)],
            block_ref.at[pair, k],
            block_send.at[pair, k],
            block_recv.at[pair, k],
            over_z[k],
        )

    def last_copy(i):
        return remote(
            last_given.at[i], last_ref.at[i], last_send.at[i], last_recv.at[i], over_y
        )

    def combine(pair):
        parts = []
        for e in range(2):
            unit = 2 * pair + e
            side_copy(unit).wait_recv()
            kept = sum_ref[unit, pl.ds(quarter, quarter)].astype(jnp.float32)
            got = side_ref[pair, pl.ds(e * quarter, quarter)].astype(jnp.float32)
            parts.append((kept + got).reshape(4, share, TILE))
        both = jnp.concatenate(parts, axis=1).reshape(8 * share, TILE)
        side_ref[pair] = both.astype(LOW)
        for k in range(3):
            block_copy(pair, k).start()

    def settle(pair):
        total = side_ref[pair, pl.ds(0, 2 * share)].astype(jnp.float32)
        for k in range(3):
            block_copy(pair, k).wait_recv()
            total = total + block_ref[pair, k].astype(jnp.float32)
        return total[:share], total[share:]

    for copy in lhs_copies():
        copy.start()
    peer_starts(0)
    for copy in lhs_copies():
        copy.wait()

    def within(i, low=0):
        return (i >= low) & (i < low + PLANE)

    def step(i, carry):
        @pl.when(i + 1 < PLANE)
        def _():
            peer_starts(i + 1)

        @pl.when(i < PLANE)
        def _():
            load_start(0, 1, 2 * i)
            load_start(1, 1, 2 * i + 1)
            for e in range(2):
                tile = 2 * i + e
                value = product(e, 1, tile, crossed_kind(tile))
                if e == 0:
                    load_start(2, 1, CROSSED + i)
                else:
                    load_start(0, 0, CROSSED + i)

                @pl.when(i >= 2)
                def _():
                    given_copy(tile - 4).wait_send()

                given_ref[lax.rem(tile, 4)] = value.astype(LOW)
                given_copy(tile).start()
            for e in range(2):
                unit = CROSSED + 2 * i + e
                value = product(2 - 2 * e, 1 - e, CROSSED + i, plane_kind(i))
                sum_ref[unit] = value.astype(LOW)
                side_copy(unit).start()

        @pl.when(within(i, 1))
        def _():
            load_start(1, 0, 2 * i - 2)
            load_start(2, 0, 2 * i - 1)
            combine(PLANE + i - 1)
            for e in range(2):
                tile = 2 * i - 2 + e
                value = product(1 + e, 0, tile, crossed_kind(tile))
                given_copy(tile).wait_recv()
                sum_ref[tile] = (value + sum_ref[tile].astype(jnp.float32)).astype(LOW)
                side_copy(tile).start()

        @pl.when(within(i, 2))
        def _():
            j = i - 2
            given, kept = settle(PLANE + j)
            out_ref[CROSSED + j] = kept
            last_given[j] = jnp.concatenate(
                [given, jnp.zeros((last_given.shape[1] - share, TILE), jnp.float32)], axis=0
            ).astype(LOW)
            last_copy(j).start()
            combine(j)

        @pl.when(within(i, 3))
        def _():
            j = i - 3
            first, second = settle(j)
            out_ref[2 * j] = first
            out_ref[2 * j + 1] = second
            last_copy(j).wait_recv()
            out_ref[CROSSED + j] += last_ref[j].astype(jnp.float32)[:share]

        return carry

    lax.fori_loop(0, PLANE + 3, step, 0)

    def drain(i, carry):
        for e in range(4):
            side_copy(4 * i + e).wait_send()
        for e in range(2):
            for k in range(3):
                block_copy(2 * i + e, k).wait_send()
        last_copy(i).wait_send()
        for tile in (2 * i, 2 * i + 1, CROSSED + i):
            for which in range(2):
                peer_copy(which, tile).wait_send()
        return carry

    lax.fori_loop(0, PLANE, drain, 0)
    for e in range(4):
        given_copy(2 * PLANE - 4 + e).wait_send()


def spread_all(lhs, rhs):
    tiles = rhs.shape[1]
    half = lhs.shape[2] // 2
    share = half // 8
    tokens = lhs.shape[3]
    dma = pltpu.SemaphoreType.DMA
    anywhere = pl.BlockSpec(memory_space=pl.ANY)
    return pl.pallas_call(
        spread_kernel,
        out_shape=[
            jax.ShapeDtypeStruct((tiles, share, TILE), jnp.float32),
            jax.ShapeDtypeStruct(rhs.shape, LOW),
        ],
        in_specs=[anywhere, anywhere],
        out_specs=[pl.BlockSpec(memory_space=pltpu.VMEM), anywhere],
        scratch_shapes=[
            pltpu.VMEM((2, lhs.shape[1], half, 2 * tokens), LOW),
            pltpu.VMEM((3, 2 * tokens, TILE), LOW),
            pltpu.VMEM((4, half, TILE), LOW),
            pltpu.VMEM((4 * PLANE, half, TILE), LOW),
            pltpu.VMEM((2 * PLANE, half, TILE), LOW),
            pltpu.VMEM((2 * PLANE, 3, 2 * share, TILE), LOW),
            pltpu.VMEM((PLANE, share + 8, TILE), LOW),
            pltpu.VMEM((PLANE, share + 8, TILE), LOW),
            dma((6,)),
            dma((2, tiles)),
            dma((2, tiles)),
            dma((3, 2)),
            dma((4,)),
            dma((CROSSED,)),
            dma((4 * PLANE,)),
            dma((4 * PLANE,)),
            dma((2 * PLANE, 3)),
            dma((2 * PLANE, 3)),
            dma((PLANE,)),
            dma((PLANE,)),
        ],
        compiler_params=pltpu.CompilerParams(
            collective_id=2, has_side_effects=True, vmem_limit_bytes=62 * 2**20
        ),
    )(lhs, rhs)[0]


def tiled(value):
    rows, width = value.shape
    return value.reshape(rows, width // TILE, TILE).transpose(1, 0, 2)


def pair_backward(grad_low, weights, saved, info, angles, arrange):
    w_in, w_out_t, w_gate, w_up, w_down_t, gain_one, gain_two = unpack(weights)
    (
        hidden,
        inverse_one,
        normed,
        q_t,
        kv_t,
        o_t,
        lse,
        middle,
        inverse_two,
        normed_two,
        gate,
        up,
        units,
    ) = saved
    rows = hidden.shape[0]
    cosine, sine = angles

    def arranged(value):
        return contract(arrange, value, 1, 1).astype(LOW)

    grad_units = contract(grad_low, w_down_t, 1, 0)
    gate_wide = gate.astype(jnp.float32)
    sigmoid = jax.nn.sigmoid(gate_wide)
    grad_gate = (
        grad_units * up.astype(jnp.float32) * sigmoid * (1.0 + gate_wide * (1.0 - sigmoid))
    ).astype(LOW)
    grad_up = (grad_units * gate_wide * sigmoid).astype(LOW)
    grad_normed_two = contract(grad_gate, w_gate, 1, 1) + contract(grad_up, w_up, 1, 1)
    grad_mid_norm, grad_gain_two = rms_backward(
        grad_normed_two, middle * inverse_two, inverse_two, gain_two
    )
    grad_middle = grad_low.astype(jnp.float32) + grad_mid_norm
    grad_branch = grad_middle.astype(LOW)
    do_t = contract(w_out_t, grad_branch, 0, 1).astype(LOW)
    dq_t, dk_t, dv_t = pair_attention_backward(info, q_t, do_t, o_t, lse, kv_t)
    grad_kv = jnp.concatenate([dk_t, dv_t], axis=1)
    crossed = swap(jnp.stack([grad_kv[1], grad_kv[3]]), "wsh", 1).astype(jnp.float32)
    far = (grad_kv[2].astype(jnp.float32) + crossed[1]).astype(LOW)
    grad_kv = (
        grad_kv[0].astype(jnp.float32) + crossed[0] + swap(far, "ctx", 1).astype(jnp.float32)
    )
    grad_q = turn(dq_t.reshape(H, HD, rows), cosine, -sine).reshape(QD, rows)
    grad_k = turn(grad_kv[:KV], cosine, -sine).reshape(KD, rows)
    grad_v = grad_kv[KV:].reshape(KD, rows)
    grad_mixed = jnp.concatenate([grad_q, grad_k, grad_v], axis=0).astype(LOW)
    grad_normed = contract(grad_mixed, w_in[:, :QKV], 0, 1)
    grad_in_norm, grad_gain_one = rms_backward(
        grad_normed, hidden * inverse_one, inverse_one, gain_one
    )
    grad_hidden = (grad_middle + grad_in_norm).astype(LOW)
    gain_rows = jnp.zeros((rows, D), LOW)
    gain_rows = gain_rows.at[0].set(grad_gain_one.astype(LOW)).at[1].set(grad_gain_two.astype(LOW))
    lhs = jnp.stack(
        [arranged(v) for v in (normed_two, normed, gain_rows, grad_low, grad_branch)]
    )
    rhs = jnp.concatenate(
        [
            tiled(grad_gate),
            tiled(grad_up),
            tiled(grad_mixed.T),
            jnp.eye(rows, TILE, dtype=LOW)[None],
            tiled(units),
            tiled(o_t.T),
        ],
        axis=0,
    )
    return grad_hidden, lhs, rhs


def on_device_pairs(
    x_in, cotangent, w_qkv, w_out, w_gate_up, w_down, gains, order, visible, seq_ids
):
    section = lax.axis_index("section")
    column = lax.axis_index("ctx")
    place = lax.axis_index("wsh")
    core = place % 2
    side = place // 2
    rows = x_in.shape[2]
    quarter = D // 4
    share = quarter // 4
    slot = column % 2 + 2 * core
    first_section = section == 0

    def partner(index):
        z, w = index // 4, index % 4
        if (z < 2) == (w % 2 == 1):
            return ((z + 2) % 4) * 4 + (w ^ 1)
        return index

    moves = [(i, partner(i)) for i in range(16)]

    def moved(value):
        return lax.ppermute(value, ("ctx", "wsh"), moves)

    ids = jnp.arange(D, dtype=jnp.int32)
    natural = one_hot((place ^ (ids // quarter)) * quarter + ids % quarter, D)
    given, block, shard = ids // (D // 2), (ids % quarter) // share, ids % share
    to_core = jnp.where(given == 0, 1 - core, core)
    to_side = jnp.where((ids % (D // 2)) // quarter == 0, 1 - side, side)
    to_place = place ^ column ^ block
    arrange = one_hot(to_place * quarter + (2 * to_side + to_core) * share + shard, D)

    seq_both = jnp.stack([seq_ids[:, 0], swap(seq_ids[:, 0], "wsh", 1)])
    seq_row = jnp.where(core == column // 2, seq_both[0, section], seq_both[1, section])
    info, angles = pair_tables(order, visible, seq_row, section, slot, rows)

    gain_columns = jnp.concatenate(
        [gains[0].T, jnp.zeros((quarter, SIDE - gains.shape[1]), LOW)], axis=1
    )
    shards = [
        jnp.concatenate([w_qkv[0], gain_columns], axis=1),
        w_out[0].T,
        w_gate_up[0],
        w_down[0].T,
    ]
    weights, source, upstream = gather_all([x_in, cotangent], shards)
    hidden = contract(source, natural, 1, 1)
    result_one, saved_one = pair_forward(hidden, weights[0], info, angles)
    result_two, saved_two = pair_forward(
        result_one.astype(jnp.float32), weights[1], info, angles
    )

    def placed(own_one, own_two):
        mine = jnp.where(first_section, own_one, own_two)
        other = swap(jnp.where(first_section, own_two, own_one), "section", 1)
        both = jnp.concatenate(
            [jnp.where(first_section, mine, other), jnp.where(first_section, other, mine)], axis=0
        )
        both = contract(both, natural, 1, 0).astype(LOW)
        return moved(both).reshape(2, rows, D)

    activations = placed(result_one, result_two)
    grad_low = contract(upstream, natural, 1, 1).astype(LOW)
    grad_two, lhs_two, rhs_two = pair_backward(
        grad_low, weights[1], saved_two, info, angles, arrange
    )
    grad_one, lhs_one, rhs_one = pair_backward(
        grad_two, weights[0], saved_one, info, angles, arrange
    )
    shares = spread_all(jnp.stack([lhs_one, lhs_two]), jnp.stack([rhs_one, rhs_two]))
    input_grads = placed(grad_one, grad_two).astype(jnp.float32)

    def joined(first, count):
        return shares[first : first + count].transpose(1, 0, 2).reshape(share, count * TILE)

    def joined_t(first, count):
        return shares[first : first + count].transpose(0, 2, 1).reshape(count * TILE, share)

    return (
        activations[None, :, None],
        input_grads[None, :, None],
        joined(16, 5)[None],
        joined_t(30, 3)[None],
        joined(0, 16)[None],
        joined_t(22, 8)[None],
        shares[21, :, :2].T[None],
    )


def solution(mesh):
    in_specs = (
        P(None, "wsh", "ctx", None),
        P(None, "wsh", "ctx", None),
        P("section", "wsh", None),
        P("section", None, "wsh"),
        P("section", "wsh", None),
        P("section", None, "wsh"),
        P("section", None, "wsh"),
        P(),
        P(),
        P(None, "wsh", None),
    )
    out_specs = (
        P("section", None, "wsh", "ctx", None),
        P("section", None, "wsh", "ctx", None),
        P("section", ("ctx", "wsh"), None),
        P("section", None, ("ctx", "wsh")),
        P("section", ("ctx", "wsh"), None),
        P("section", None, ("ctx", "wsh")),
        P("section", None, ("ctx", "wsh")),
    )
    body = on_device_pairs if fits_pairs(mesh) else on_device_general
    return jax.shard_map(
        body, mesh=mesh, in_specs=in_specs, out_specs=out_specs, check_vma=False
    )
```

```python
import functools

import jax
import jax.numpy as jnp
from jax import lax
from jax.experimental import pallas as pl
from jax.experimental.pallas import tpu as pltpu
from jax.sharding import PartitionSpec as P

D = 1152
H = 18
KV = 6
HD = 64
FF = 3072
SECTION, CTX, WSH = "section", "ctx", "wsh"


NEG = -1e30
EPS = 1e-05


def shifted(value, axis, by):
    devices = lax.axis_size(axis)
    pairs = [(i, i + by) for i in range(devices) if 0 <= i + by < devices]
    return lax.ppermute(value, axis, pairs)


def rms_forward(hidden, gain_row):
    inverse = lax.rsqrt(jnp.mean(hidden * hidden, axis=-1, keepdims=True) + EPS)
    unit_rows = hidden * inverse
    return (unit_rows * gain_row, unit_rows, inverse)


def rms_backward(grad_rows, unit_rows, inverse, gain_row):
    grad_unit = grad_rows * gain_row
    grad_gain = jnp.sum(grad_rows * unit_rows, axis=0)
    inner = jnp.mean(grad_unit * unit_rows, axis=-1, keepdims=True)
    return (inverse * (grad_unit - unit_rows * inner), grad_gain)


def rotation(positions):
    frequency = 10000.0 ** (-(jnp.arange(HD // 2, dtype=jnp.float32) * 2.0 / HD))
    angles = positions.astype(jnp.float32)[:, None] * frequency[None, :]
    return (jnp.cos(angles), jnp.sin(angles))


def rotate(vectors, cosine, sine):
    half_width = vectors.shape[-1] // 2
    first_half = vectors[..., :half_width]
    second_half = vectors[..., half_width:]
    cos_rows = cosine[:, None, :]
    sin_rows = sine[:, None, :]
    return jnp.concatenate(
        [
            first_half * cos_rows - second_half * sin_rows,
            first_half * sin_rows + second_half * cos_rows,
        ],
        axis=-1,
    )


def stretch_width(rows, n_ctx):
    per_stretch = min(n_ctx, max(1, 512 // rows))
    while n_ctx % per_stretch:
        per_stretch -= 1
    return per_stretch


def sweep(step_fn, init, items, alive):

    def guarded(state, packed):
        item, live = packed
        return step_fn(state, item)

    return lax.scan(guarded, init, (items, alive))


def tables(order, visible, seq_ids, batch_index, column, rows, n_ctx):
    order_row = order[batch_index]
    own_block = order_row[column]
    seq_row = seq_ids[batch_index, 0]
    own_seq = lax.dynamic_slice_in_dim(seq_row, column * rows, rows)
    device_vis = visible[own_block][order_row]
    key_vis = jnp.broadcast_to(device_vis[:, None], (n_ctx, rows)).reshape(n_ctx * rows)
    positions = own_block * rows + jnp.arange(rows, dtype=jnp.int32)
    return ((own_seq, seq_row, key_vis, device_vis), positions)


def key_items(key_rows, value_rows, info, per_stretch, rows):
    own_seq, seq_row, key_vis, device_vis = info
    length = key_rows.shape[0]
    size = per_stretch * rows
    count = length // size
    items = (
        key_rows.reshape(count, size, KV, HD),
        value_rows.reshape(count, size, KV, HD),
        key_vis.reshape(count, size),
        seq_row.reshape(count, size),
    )
    alive = jnp.sum(device_vis.reshape(count, per_stretch), axis=-1) > 0
    return (items, alive, size)


def masked_scores(queries, key_part, vis_part, seq_part, own_seq):
    scores = jnp.einsum(
        "nkgd,mkd->kgnm", queries, key_part, preferred_element_type=jnp.float32
    ) * HD ** (-0.5)
    allowed = (vis_part[None, :] == 1) & (own_seq[:, None] == seq_part[None, :])
    return (jnp.where(allowed[None, None], scores, NEG), allowed)


def attention_forward(queries, key_rows, value_rows, info, per_stretch, rows):
    own_seq = info[0]
    items, alive, size = key_items(key_rows, value_rows, info, per_stretch, rows)
    group = H // KV

    def lse_step(state, item):
        high, total = state
        key_part, value_part, vis_part, seq_part = item
        masked, allowed = masked_scores(queries, key_part, vis_part, seq_part, own_seq)
        top = jnp.maximum(high, jnp.max(masked, axis=-1))
        terms = jnp.where(allowed[None, None], jnp.exp(masked - top[..., None]), 0.0)
        return ((top, total * jnp.exp(high - top) + jnp.sum(terms, axis=-1)), None)

    start_state = (
        jnp.full((KV, group, rows), NEG, jnp.float32),
        jnp.zeros((KV, group, rows), jnp.float32),
    )
    (high, total), unused = sweep(lse_step, start_state, items, alive)
    log_total = high + jnp.log(total)

    def out_step(acc, item):
        key_part, value_part, vis_part, seq_part = item
        masked, allowed = masked_scores(queries, key_part, vis_part, seq_part, own_seq)
        probs = jnp.where(allowed[None, None], jnp.exp(masked - log_total[..., None]), 0.0).astype(
            jnp.bfloat16
        )
        return (
            acc
            + jnp.einsum("kgnm,mkd->nkgd", probs, value_part, preferred_element_type=jnp.float32),
            None,
        )

    attended, unused_two = sweep(
        out_step, jnp.zeros((rows, KV, group, HD), jnp.float32), items, alive
    )
    return (attended, log_total)


def attention_backward(
    queries, key_rows, value_rows, info, per_stretch, rows, log_total, grad_att, delta
):
    own_seq = info[0]
    items, alive, size = key_items(key_rows, value_rows, info, per_stretch, rows)
    group = H // KV

    def back_step(grad_query, item):
        key_part, value_part, vis_part, seq_part = item
        masked, allowed = masked_scores(queries, key_part, vis_part, seq_part, own_seq)
        probs = jnp.where(allowed[None, None], jnp.exp(masked - log_total[..., None]), 0.0)
        probs_low = probs.astype(jnp.bfloat16)
        grad_probs = jnp.einsum(
            "nkgd,mkd->kgnm", grad_att, value_part, preferred_element_type=jnp.float32
        )
        grad_scores = (probs * (grad_probs - delta[..., None])).astype(jnp.bfloat16)
        grad_query = grad_query + jnp.einsum(
            "kgnm,mkd->nkgd", grad_scores, key_part, preferred_element_type=jnp.float32
        ) * HD ** (-0.5)
        grad_keys = jnp.einsum(
            "kgnm,nkgd->mkd", grad_scores, queries, preferred_element_type=jnp.float32
        ) * HD ** (-0.5)
        grad_values = jnp.einsum(
            "kgnm,nkgd->mkd", probs_low, grad_att, preferred_element_type=jnp.float32
        )
        return (grad_query, (grad_keys, grad_values))

    grad_query, (grad_keys, grad_values) = sweep(
        back_step, jnp.zeros((rows, KV, group, HD), jnp.float32), items, alive
    )
    length = key_rows.shape[0]
    return (grad_query, grad_keys.reshape(length, KV, HD), grad_values.reshape(length, KV, HD))


def layer_forward(hidden, weights, info, positions, per_stretch, rows):
    w_qkv, w_out, w_gate_up, w_down, gains = weights
    query_width = H * HD
    key_width = KV * HD
    gain_attn = gains[0].astype(jnp.float32)
    gain_ffn = gains[1].astype(jnp.float32)
    normed, unit_one, inverse_one = rms_forward(hidden, gain_attn)
    normed_low = normed.astype(jnp.bfloat16)
    mixed = jnp.dot(normed_low, w_qkv, preferred_element_type=jnp.float32)
    cosine, sine = rotation(positions)
    queries = (
        rotate(mixed[:, :query_width].reshape(rows, H, HD), cosine, sine)
        .astype(jnp.bfloat16)
        .reshape(rows, KV, H // KV, HD)
    )
    key_own = rotate(
        mixed[:, query_width : query_width + key_width].reshape(rows, KV, HD), cosine, sine
    ).astype(jnp.bfloat16)
    value_own = mixed[:, query_width + key_width :].reshape(rows, KV, HD).astype(jnp.bfloat16)
    key_rows, value_rows = (
        lax.all_gather(key_own, "ctx", axis=0, tiled=True),
        lax.all_gather(value_own, "ctx", axis=0, tiled=True),
    )
    attended, log_total = attention_forward(queries, key_rows, value_rows, info, per_stretch, rows)
    attended_low = attended.reshape(rows, query_width).astype(jnp.bfloat16)
    middle = hidden + jnp.dot(attended_low, w_out, preferred_element_type=jnp.float32)
    normed_two, unit_two, inverse_two = rms_forward(middle, gain_ffn)
    normed_two_low = normed_two.astype(jnp.bfloat16)
    gate_up = jnp.dot(normed_two_low, w_gate_up, preferred_element_type=jnp.float32)
    gate_part = gate_up[:, :FF]
    up_part = gate_up[:, FF:]
    units_low = (jax.nn.silu(gate_part) * up_part).astype(jnp.bfloat16)
    result = middle + jnp.dot(units_low, w_down, preferred_element_type=jnp.float32)
    saved = {
        "unit_one": unit_one,
        "inverse_one": inverse_one,
        "normed_low": normed_low,
        "cosine": cosine,
        "sine": sine,
        "queries": queries,
        "key_rows": key_rows,
        "value_rows": value_rows,
        "attended": attended,
        "log_total": log_total,
        "attended_low": attended_low,
        "unit_two": unit_two,
        "inverse_two": inverse_two,
        "normed_two_low": normed_two_low,
        "gate_part": gate_part,
        "up_part": up_part,
        "units_low": units_low,
    }
    return (result, saved)


def layer_backward(grad_rows, weights, saved, info, per_stretch, rows):
    w_qkv, w_out, w_gate_up, w_down, gains = weights
    query_width = H * HD
    gain_attn = gains[0].astype(jnp.float32)
    gain_ffn = gains[1].astype(jnp.float32)
    gate_part = saved["gate_part"]
    grad_low = grad_rows.astype(jnp.bfloat16)
    grad_units = jnp.dot(grad_low, w_down.T, preferred_element_type=jnp.float32)
    sigmoid = jax.nn.sigmoid(gate_part)
    grad_gate = grad_units * saved["up_part"] * sigmoid * (1.0 + gate_part * (1.0 - sigmoid))
    grad_up = grad_units * gate_part * sigmoid
    grad_mix_low = jnp.concatenate([grad_gate, grad_up], axis=-1).astype(jnp.bfloat16)
    grad_normed_two = jnp.dot(grad_mix_low, w_gate_up.T, preferred_element_type=jnp.float32)
    grad_mid_norm, grad_gain_two = rms_backward(
        grad_normed_two, saved["unit_two"], saved["inverse_two"], gain_ffn
    )
    grad_middle = grad_rows + grad_mid_norm
    grad_branch_low = grad_middle.astype(jnp.bfloat16)
    grad_att = (
        jnp.dot(grad_branch_low, w_out.T, preferred_element_type=jnp.float32)
        .astype(jnp.bfloat16)
        .reshape(rows, KV, H // KV, HD)
    )
    delta = jnp.einsum("nkgd,nkgd->kgn", grad_att.astype(jnp.float32), saved["attended"])
    grad_query, grad_keys, grad_values = attention_backward(
        saved["queries"],
        saved["key_rows"],
        saved["value_rows"],
        info,
        per_stretch,
        rows,
        saved["log_total"],
        grad_att,
        delta,
    )
    key_total, value_total = (
        lax.psum_scatter(
            grad_keys.astype(jnp.bfloat16), "ctx", scatter_dimension=0, tiled=True
        ).astype(jnp.float32),
        lax.psum_scatter(
            grad_values.astype(jnp.bfloat16), "ctx", scatter_dimension=0, tiled=True
        ).astype(jnp.float32),
    )
    cosine = saved["cosine"]
    back_sine = -saved["sine"]
    grad_q = rotate(grad_query.reshape(rows, H, HD), cosine, back_sine).reshape(rows, query_width)
    grad_k = rotate(key_total, cosine, back_sine).reshape(rows, KV * HD)
    grad_v = value_total.reshape(rows, KV * HD)
    grad_qkv_low = jnp.concatenate([grad_q, grad_k, grad_v], axis=-1).astype(jnp.bfloat16)
    grad_normed = jnp.dot(grad_qkv_low, w_qkv.T, preferred_element_type=jnp.float32)
    grad_in_norm, grad_gain_one = rms_backward(
        grad_normed, saved["unit_one"], saved["inverse_one"], gain_attn
    )
    grad_hidden = grad_middle + grad_in_norm
    pairs = (
        saved["normed_low"],
        grad_qkv_low,
        saved["attended_low"],
        grad_branch_low,
        saved["normed_two_low"],
        grad_mix_low,
        saved["units_low"],
        grad_low,
        grad_gain_one,
        grad_gain_two,
    )
    return (grad_hidden, pairs)


def weight_terms(pairs):
    (
        normed_low,
        grad_qkv_low,
        attended_low,
        grad_branch_low,
        normed_two_low,
        grad_mix_low,
        units_low,
        grad_low,
        grad_gain_one,
        grad_gain_two,
    ) = pairs
    return (
        jnp.dot(normed_low.T, grad_qkv_low, preferred_element_type=jnp.float32),
        jnp.dot(attended_low.T, grad_branch_low, preferred_element_type=jnp.float32),
        jnp.dot(normed_two_low.T, grad_mix_low, preferred_element_type=jnp.float32),
        jnp.dot(units_low.T, grad_low, preferred_element_type=jnp.float32),
        jnp.stack([grad_gain_one, grad_gain_two]),
    )


def on_device_general(x_in, cotangent, w_qkv, w_out, w_gate_up, w_down, gains, order, visible, seq_ids):
    section = lax.axis_index("section")
    column = lax.axis_index("ctx")
    n_ctx = lax.axis_size("ctx")
    batches = x_in.shape[0]
    rows = x_in.shape[2]
    per_stretch = stretch_width(rows, n_ctx)
    first_section = section == 0
    weights = (
        lax.all_gather(w_qkv[0], "wsh", axis=0, tiled=True),
        lax.all_gather(w_out[0], "wsh", axis=1, tiled=True),
        lax.all_gather(w_gate_up[0], "wsh", axis=0, tiled=True),
        lax.all_gather(w_down[0], "wsh", axis=1, tiled=True),
        lax.all_gather(gains[0], "wsh", axis=1, tiled=True),
    )
    incoming = jnp.zeros((rows, D), jnp.bfloat16)
    section_inputs = []
    section_outputs = []
    for tick_now in range(batches + 1):
        batch_index = jnp.clip(tick_now - section, 0, batches - 1)
        info, positions = tables(order, visible, seq_ids, batch_index, column, rows, n_ctx)
        source = jnp.where(first_section, x_in[batch_index, 0], incoming)
        result, unused = layer_forward(
            source.astype(jnp.float32), weights, info, positions, per_stretch, rows
        )
        result_low = result.astype(jnp.bfloat16)
        section_inputs.append(source)
        section_outputs.append(result_low)
        if tick_now < batches:
            incoming = shifted(result_low, "section", 1)
    activations = jnp.stack(
        [
            jnp.where(first_section, section_outputs[batch], section_outputs[batch + 1])
            for batch in range(batches)
        ]
    )
    back_weights = (
        lax.all_gather(w_qkv[0], "wsh", axis=0, tiled=True),
        lax.all_gather(w_out[0], "wsh", axis=1, tiled=True),
        lax.all_gather(w_gate_up[0], "wsh", axis=0, tiled=True),
        lax.all_gather(w_down[0], "wsh", axis=1, tiled=True),
        lax.all_gather(gains[0], "wsh", axis=1, tiled=True),
    )
    returned = jnp.zeros((rows, D), jnp.bfloat16)
    grad_list = []
    totals = None
    for tick_now in range(batches + 1):
        raw_index = tick_now - 1 + section
        valid = (raw_index >= 0) & (raw_index < batches)
        batch_index = jnp.clip(raw_index, 0, batches - 1)
        info, positions = tables(order, visible, seq_ids, batch_index, column, rows, n_ctx)
        source = jnp.where(
            first_section,
            section_inputs[max(tick_now - 1, 0)],
            section_inputs[min(tick_now + 1, batches)],
        )
        unused, saved = layer_forward(
            source.astype(jnp.float32), back_weights, info, positions, per_stretch, rows
        )
        grad_rows = jnp.where(first_section, returned, cotangent[batch_index, 0]).astype(
            jnp.float32
        ) * valid.astype(jnp.float32)
        grad_hidden, pairs = layer_backward(grad_rows, back_weights, saved, info, per_stretch, rows)
        grad_hidden_low = grad_hidden.astype(jnp.bfloat16)
        grad_list.append((grad_hidden, grad_hidden_low))
        if tick_now < batches:
            returned = shifted(grad_hidden_low, "section", -1)
        terms = weight_terms(pairs)
        totals = terms if totals is None else jax.tree.map(jnp.add, totals, terms)
    input_grads = jnp.stack(
        [
            jnp.where(
                first_section, grad_list[batch + 1][0], grad_list[batch][1].astype(jnp.float32)
            )
            for batch in range(batches)
        ]
    )
    term_qkv, term_out, term_gate_up, term_down, term_gains = totals
    shares = (
        lax.psum_scatter(term_qkv, ("ctx", "wsh"), scatter_dimension=0, tiled=True),
        lax.psum_scatter(term_out, ("ctx", "wsh"), scatter_dimension=1, tiled=True),
        lax.psum_scatter(term_gate_up, ("ctx", "wsh"), scatter_dimension=0, tiled=True),
        lax.psum_scatter(term_down, ("ctx", "wsh"), scatter_dimension=1, tiled=True),
        lax.psum_scatter(term_gains, ("ctx", "wsh"), scatter_dimension=1, tiled=True),
    )
    return (
        activations[None, :, None],
        input_grads[None, :, None],
        shares[0][None],
        shares[1][None],
        shares[2][None],
        shares[3][None],
        shares[4][None],
    )


GROUP = H // KV
QD = H * HD
KD = KV * HD
QKV = QD + 2 * KD
SIDE = 128
LOW = jnp.bfloat16


def fits_pairs(mesh):
    return mesh.shape[SECTION] == 2 and mesh.shape[CTX] == 4 and mesh.shape[WSH] == 4


def contract(left, right, left_dim, right_dim):
    return lax.dot_general(
        left,
        right,
        (((left_dim,), (right_dim,)), ((), ())),
        preferred_element_type=jnp.float32,
    )


def swap(value, axis, bit):
    return lax.ppermute(value, axis, [(i, i ^ bit) for i in range(lax.axis_size(axis))])


def after(value, *others):
    return lax.optimization_barrier((value, *others))[0]


def masked_pair(first, second):
    return jnp.concatenate([first, second], axis=0)


def attend(queries, masks, keys_of, values_of, key_mask_of, first, last, slot_of):
    rows = masks.shape[1]
    query = masked_pair(
        jnp.concatenate(queries, axis=1), jnp.concatenate([masks] * GROUP, axis=1)
    )

    def step(i, state):
        high, acc = state
        slot = slot_of(i)
        value_t = values_of(slot)
        ones = jnp.ones((1, value_t.shape[1]), jnp.float32)
        ones = jnp.concatenate([ones, jnp.zeros((15, value_t.shape[1]), jnp.float32)], axis=0)
        scores = contract(masked_pair(keys_of(slot), key_mask_of(slot)), query, 0, 0)
        top = jnp.maximum(high, jnp.max(scores, axis=0, keepdims=True))
        terms = jnp.exp(scores - top).astype(LOW)
        fresh = contract(masked_pair(value_t, ones.astype(LOW)), terms, 1, 0)
        return top, acc * jnp.exp(high - top) + fresh

    start = (
        jnp.full((1, GROUP * rows), NEG, jnp.float32),
        jnp.zeros((HD + 16, GROUP * rows), jnp.float32),
    )
    high, acc = lax.fori_loop(first, last, step, start)
    total = acc[HD : HD + 1]
    out = (acc[:HD] / total).astype(LOW)
    log_total = high + jnp.log(total)
    cuts = [slice(j * rows, (j + 1) * rows) for j in range(GROUP)]
    return [out[:, c] for c in cuts], [log_total[:, c] for c in cuts]


def forward_kernel(live_ref, q_ref, k_ref, v_ref, key_mask_ref, mask_ref, o_ref, lse_ref):
    out, log_total = attend(
        [q_ref[pl.ds(j * HD, HD), :] for j in range(GROUP)],
        mask_ref[...],
        lambda slot: k_ref[slot, 0],
        lambda slot: v_ref[slot, 0],
        lambda slot: key_mask_ref[slot],
        0,
        live_ref[0],
        lambda i: live_ref[1 + i],
    )
    for j in range(GROUP):
        o_ref[pl.ds(j * HD, HD), :] = out[j]
        lse_ref[0, pl.ds(j, 1), :] = log_total[j]


def backward_kernel(
    live_ref,
    q_ref,
    do_ref,
    o_ref,
    lse_ref,
    k_ref,
    v_ref,
    key_mask_ref,
    mask_ref,
    dq_ref,
    dk_ref,
    dv_ref,
    acc_ref,
):
    rows = q_ref.shape[1]
    acc_ref[...] = jnp.zeros_like(acc_ref)
    dk_ref[...] = jnp.zeros_like(dk_ref)
    dv_ref[...] = jnp.zeros_like(dv_ref)
    parts = [pl.ds(j * HD, HD) for j in range(GROUP)]
    query_t = jnp.concatenate([q_ref[part, :] for part in parts], axis=1)
    grad_t = jnp.concatenate([do_ref[part, :] for part in parts], axis=1)
    out_t = jnp.concatenate([o_ref[part, :] for part in parts], axis=1)
    log_total = jnp.concatenate([lse_ref[0, pl.ds(j, 1), :] for j in range(GROUP)], axis=1)
    both = grad_t.astype(jnp.float32) * out_t.astype(jnp.float32)
    delta = jnp.sum(both, axis=0, keepdims=True)
    query = masked_pair(query_t, jnp.concatenate([mask_ref[...]] * GROUP, axis=1))

    def step(i, carry):
        slot = live_ref[1 + i]
        key_t = k_ref[slot, 0]
        scores = contract(masked_pair(key_t, key_mask_ref[slot]), query, 0, 0)
        probs = jnp.exp(scores - log_total)
        grad_probs = contract(v_ref[slot, 0], grad_t, 0, 0)
        grad_scores = (probs * (grad_probs - delta)).astype(LOW)
        grad_v = contract(probs.astype(LOW), grad_t, 1, 1)
        grad_k = contract(grad_scores, query_t, 1, 1)
        acc_ref[...] += contract(key_t, grad_scores, 1, 0)
        dk_ref[slot, 0] = jnp.transpose(grad_k).astype(LOW)
        dv_ref[slot, 0] = jnp.transpose(grad_v).astype(LOW)
        return carry

    lax.fori_loop(0, live_ref[0], step, 0)
    for j in range(GROUP):
        cut = slice(j * rows, (j + 1) * rows)
        dq_ref[parts[j], :] = acc_ref[:, cut] * HD ** (-0.5)


def long_cost(microseconds):
    return pl.CostEstimate(
        flops=microseconds * 10**9, bytes_accessed=2**20, transcendentals=0
    )


def kernel_cost(scores, matmuls):
    return pl.CostEstimate(
        flops=scores * matmuls * HD * 2 * 4, bytes_accessed=12 * 2**20, transcendentals=scores
    )


def pair_attention_forward(info, q_t, kv_t):
    live, key_masks, masks = info
    slots, keys = kv_t.shape[0], kv_t.shape[3]
    rows = q_t.shape[1]
    return pl.pallas_call(
        forward_kernel,
        grid_spec=pltpu.PrefetchScalarGridSpec(
            num_scalar_prefetch=1,
            grid=(KV,),
            in_specs=[
                pl.BlockSpec((GROUP * HD, rows), lambda g, l: (g, 0)),
                pl.BlockSpec((slots, 1, HD, keys), lambda g, l: (0, g, 0, 0)),
                pl.BlockSpec((slots, 1, HD, keys), lambda g, l: (0, KV + g, 0, 0)),
                pl.BlockSpec((slots, 16, keys), lambda g, l: (0, 0, 0)),
                pl.BlockSpec((16, rows), lambda g, l: (0, 0)),
            ],
            out_specs=[
                pl.BlockSpec((GROUP * HD, rows), lambda g, l: (g, 0)),
                pl.BlockSpec((1, GROUP, rows), lambda g, l: (g, 0, 0)),
            ],
        ),
        out_shape=[
            jax.ShapeDtypeStruct(q_t.shape, LOW),
            jax.ShapeDtypeStruct((KV, GROUP, rows), jnp.float32),
        ],
        compiler_params=pltpu.CompilerParams(vmem_limit_bytes=62 * 2**20),
        cost_estimate=kernel_cost(H * rows * slots * keys, 2),
    )(live, q_t, kv_t, kv_t, key_masks, masks)


def pair_attention_backward(info, q_t, do_t, o_t, lse, kv_t):
    live, key_masks, masks = info
    slots, keys = kv_t.shape[0], kv_t.shape[3]
    rows = q_t.shape[1]
    q_spec = pl.BlockSpec((GROUP * HD, rows), lambda g, l: (g, 0))
    part_spec = pl.BlockSpec((slots, 1, HD, keys), lambda g, l: (0, g, 0, 0))
    part_shape = jax.ShapeDtypeStruct((slots, KV, HD, keys), LOW)
    return pl.pallas_call(
        backward_kernel,
        grid_spec=pltpu.PrefetchScalarGridSpec(
            num_scalar_prefetch=1,
            grid=(KV,),
            in_specs=[
                q_spec,
                q_spec,
                q_spec,
                pl.BlockSpec((1, GROUP, rows), lambda g, l: (g, 0, 0)),
                part_spec,
                pl.BlockSpec((slots, 1, HD, keys), lambda g, l: (0, KV + g, 0, 0)),
                pl.BlockSpec((slots, 16, keys), lambda g, l: (0, 0, 0)),
                pl.BlockSpec((16, rows), lambda g, l: (0, 0)),
            ],
            out_specs=[q_spec, part_spec, part_spec],
            scratch_shapes=[pltpu.VMEM((HD, GROUP * rows), jnp.float32)],
        ),
        out_shape=[jax.ShapeDtypeStruct(q_t.shape, jnp.float32), part_shape, part_shape],
        compiler_params=pltpu.CompilerParams(vmem_limit_bytes=62 * 2**20),
        cost_estimate=kernel_cost(H * rows * slots * keys, 5),
    )(live, q_t, do_t, o_t, lse, kv_t, kv_t, key_masks, masks)


def turn(heads, cosine, sine):
    half = HD // 2
    first, second = heads[:, :half], heads[:, half:]
    return jnp.concatenate(
        [first * cosine - second * sine, first * sine + second * cosine], axis=1
    )


def pair_angles(own_block, rows):
    positions = own_block * rows + jnp.arange(rows, dtype=jnp.int32)
    frequency = 10000.0 ** (-(jnp.arange(HD // 2, dtype=jnp.float32) * 2.0 / HD))
    angles = frequency[:, None] * positions.astype(jnp.float32)[None, :]
    return jnp.cos(angles), jnp.sin(angles)


MESH_ID = pl.DeviceIdType.MESH


def stream_partner(column, place):
    core = place % 2
    moving = (column < 2) == (core == 1)
    return moving, lax.rem(column + 2, 4), place + 1 - 2 * core


def first_kernel(*refs):
    x_ref, shard_refs = refs[0], refs[1:5]
    seq_all_ref, cos_ref, sin_ref, order_ref, visible_ref = refs[5:10]
    full_refs = refs[10:15]
    (
        hidden_ref,
        q_ref,
        kv_out,
        o_ref,
        lse_ref,
        result_ref,
        middle_ref,
        lhs_out,
        attended_out,
        units_out,
        gate_out,
        up_out,
        stream_ref,
        gains_ref,
        next_q_ref,
        next_kv_out,
        natural_out_ref,
        key_mask_out,
        mask_out,
        live_ref,
        natural_ref,
    ) = refs[15:36]
    (
        send_sem,
        recv_sem,
        store_sem,
        hold_sem,
        local_sem,
        ring_ref,
        rows_ref,
        w_in_ref,
        w_out_ref,
        w_mlp_ref,
        w_down_ref,
        units_ref,
        gate_ref,
        up_ref,
        normed_ref,
        turned_ref,
        attended_ref,
        acc_ref,
        kv_ref,
        seq_peer_ref,
        key_mask_ref,
        mask_ref,
        gain_ref,
        next_kv_ref,
        seq_ref,
    ) = refs[36:]
    section = lax.axis_index(SECTION)
    column = lax.axis_index(CTX)
    place = lax.axis_index(WSH)
    half = lax.rem(column, 2)
    core = lax.rem(place, 2)
    other = 1 - section
    over_x = (section, column, lax.rem(place + 2, 4))
    over_y = (other, column, place)
    over_z = (section, column + 1 - 2 * half, place)
    over_core = (section, column, place + 1 - 2 * core)
    moving, partner_column, partner_place = stream_partner(column, place)
    partner = (section, partner_column, partner_place)

    barrier = pltpu.get_barrier_semaphore()
    for target in (over_x, over_y, over_z, over_core):
        pl.semaphore_signal(barrier, inc=1, device_id=target, device_id_type=MESH_ID)

    @pl.when(moving)
    def _():
        pl.semaphore_signal(barrier, inc=1, device_id=partner, device_id_type=MESH_ID)
        pl.semaphore_wait(barrier, 5)

    @pl.when(jnp.logical_not(moving))
    def _():
        pl.semaphore_wait(barrier, 4)

    seq_ref[...] = seq_all_ref[section].astype(jnp.float32)
    in_shard, out_shard, gate_up_shard, down_shard = shard_refs
    sources = [
        (in_shard, 0, full_refs[0], 1024),
        (out_shard, 0, full_refs[1], QD),
        (gate_up_shard, 0, full_refs[2], WIDE),
        (gate_up_shard, FF, full_refs[3], WIDE),
        (down_shard, 0, full_refs[4], WIDE),
    ]
    pieces = []
    for shard_ref, offset, full_ref, step in sources:
        for first in range(0, full_ref.shape[2], step):
            pieces.append((shard_ref, offset + first, full_ref, first, step))
    count = len(pieces)
    direct = (13, 14)
    quarter = in_shard.shape[0]
    mid = quarter // 2
    rows = hidden_ref.shape[0]

    def own(k):
        shard_ref, offset, full_ref, first, step = pieces[k]
        return shard_ref.at[:, pl.ds(offset, step)]

    def own_half(k):
        shard_ref, offset, full_ref, first, step = pieces[k]
        return shard_ref.at[pl.ds(half * mid, mid), pl.ds(offset, step)]

    def full(k, layer, block):
        shard_ref, offset, full_ref, first, step = pieces[k]
        return full_ref.at[layer, pl.ds(block * quarter, quarter), pl.ds(first, step)]

    def full_half(k, layer, block, which):
        shard_ref, offset, full_ref, first, step = pieces[k]
        span = pl.ds(block * quarter + which * mid, mid)
        return full_ref.at[layer, span, pl.ds(first, step)]

    started = {}
    arrived = set()

    def remote(kind, k, source, target, device):
        return pltpu.make_async_remote_copy(
            src_ref=source,
            dst_ref=target,
            send_sem=send_sem.at[kind, k],
            recv_sem=recv_sem.at[kind, k],
            device_id=device,
            device_id_type=MESH_ID,
        )

    def send(kind, k, source, target, device):
        copy = remote(kind, k, source, target, device)
        copy.start()
        started[kind, k] = copy

    def receive(kind, k):
        if (kind, k) not in arrived:
            arrived.add((kind, k))
            started[kind, k].wait_recv()

    def start_near(k):
        if k < count:
            send(0, k, own(k), full(k, section, 2), over_x)

    def start_cross(k):
        if k in direct:
            send(1, k, own(k), full(k, section, 0), over_y)
        elif k < count:
            send(1, k, own_half(k), full_half(k, section, 0, half), over_y)

    def ring(k):
        return ring_ref.at[k % 2, :, pl.ds(0, pieces[k][4])]

    def hold(k):
        return pltpu.make_async_copy(own(k), ring(k), hold_sem.at[k % 2])

    def store(k):
        return pltpu.make_async_copy(ring(k), full(k, section, 0), store_sem.at[k])

    stored_pieces = set()

    def need(k):
        for kind in range(5, 10 if k in direct else 11):
            receive(kind, k)
        if k not in stored_pieces:
            stored_pieces.add(k)
            store(k).wait()

    local_copies = {}

    def begin(name, source, target):
        copy = pltpu.make_async_copy(source, target, local_sem.at[len(local_copies)])
        local_copies[name] = copy
        copy.start()

    def finish(name):
        local_copies[name].wait()

    row_source = x_ref.at[section, 0]
    row_move = remote(11, 0, row_source, rows_ref, partner)
    row_copy = pltpu.make_async_copy(row_source, rows_ref, hold_sem.at[2])

    def move_rows():
        @pl.when(moving)
        def _():
            row_move.wait()

        @pl.when(jnp.logical_not(moving))
        def _():
            row_copy.wait()

        share = quarter // 4
        index = lax.broadcasted_iota(jnp.int32, (D, 1), 0)
        block, inner = index // quarter, index % quarter
        to_core, to_side = inner // (2 * share), inner % (2 * share) // share
        index = (block ^ place) * quarter + (2 * to_side + to_core) * share + inner % share
        lane = lax.broadcasted_iota(jnp.int32, (D, D), 1)
        natural_ref[...] = jnp.where(index == lane, 1.0, 0.0).astype(LOW)
        hidden_ref[...] = contract(rows_ref[...], natural_ref[...], 1, 1).astype(LOW)

    def make_masks():
        receive(11, 1)
        own_stream = jnp.broadcast_to(core == column // 2, seq_ref.shape)
        stream_ref[...] = jnp.where(own_stream, seq_ref[...], seq_peer_ref[...])
        slot = half + 2 * core
        own_block = order_ref[section, slot]
        alive, spans = [], []
        for p, step in enumerate((0, 2, 1, 3)):
            at = slot ^ step
            span = pl.ds(pl.multiple_of(at * rows, rows), rows)
            ids = stream_ref[:, span]
            seen = visible_ref[own_block, order_ref[section, at]].astype(jnp.float32)
            unseen = jnp.full((1, rows), 1.0, jnp.float32) * (1.0 - seen)
            blank = jnp.zeros((13, rows), jnp.float32)
            key_mask = jnp.concatenate([ids, 1.0 - ids, unseen, blank], axis=0) * NEG
            key_mask_ref[p] = key_mask.astype(LOW)
            spans.append((jnp.min(ids), jnp.max(ids)))
            if p == 0:
                ones = jnp.ones((1, rows), jnp.float32)
                mask_ref[...] = jnp.concatenate([1.0 - ids, ids, ones, blank], axis=0).astype(LOW)
                alive.append(jnp.int32(1))
            else:
                shared = (spans[p][0] <= spans[0][1]) & (spans[0][0] <= spans[p][1])
                alive.append(jnp.where(shared & (seen > 0.5), 1, 0).astype(jnp.int32))
        key_mask_out[...] = key_mask_ref[...]
        mask_out[...] = mask_ref[...]
        found = [sum(alive[:p], jnp.int32(0)) for p in range(5)]
        live_ref[0] = found[4]
        for j in range(4):
            live_ref[1 + j] = sum(
                (jnp.where((alive[p] == 1) & (found[p] == j), p, 0) for p in range(1, 4)),
                jnp.int32(0),
            )

    def load_in(layer):
        need(0)
        need(1)
        begin((0, layer), full_refs[0].at[layer], w_in_ref)

    def make_keys(layer, source_ref, keys_ref, first):
        if layer == 0:
            finish((0, 0))
            gain_ref[0] = w_in_ref[:, pl.ds(QKV, SIDE)].astype(jnp.float32).T[:8]
        else:
            finish((1, 0))
        unit_rows, unused = norm_parts(source_ref[...].astype(jnp.float32))
        normed = (unit_rows * gain_ref[layer, :1]).astype(LOW)
        normed_ref[...] = normed
        turned_ref[1] = normed.T
        begin((1, layer), turned_ref.at[1], lhs_out.at[layer, 3])
        for part in range(2):
            cut = pl.ds(QD + part * KD, KD)
            heads = jnp.dot(normed, w_in_ref[:, cut], preferred_element_type=jnp.float32).T
            heads = heads.reshape(KV, HD, rows)
            if part == 0:
                heads = turn(heads, cos_ref[...], sin_ref[...])
            keys_ref[0, pl.ds(part * KV, KV)] = heads.astype(LOW)
        send(11, first, keys_ref.at[0], keys_ref.at[2], over_z)
        send(11, first + 1, keys_ref.at[0], keys_ref.at[1], over_core)

    def make_queries(target_ref):
        normed = normed_ref[...]
        for part in range(QD // KD):
            heads = jnp.dot(
                normed, w_in_ref[:, pl.ds(part * KD, KD)], preferred_element_type=jnp.float32
            ).T
            turned = turn(heads.reshape(KV, HD, rows), cos_ref[...], sin_ref[...])
            turned = turned.astype(LOW).astype(jnp.float32) * HD ** (-0.5)
            target_ref[pl.ds(part * KD, KD), :] = turned.astype(LOW).reshape(KD, rows)

    def take_keys(layer, keys_ref, keys_out, first):
        receive(11, first)
        send(11, first + 2, keys_ref.at[2], keys_ref.at[3], over_core)
        receive(11, first + 1)
        receive(11, first + 2)
        begin((2, layer), keys_ref, keys_out)

    def attention(first, last):
        def one(g, carry):
            spans = [
                pl.ds(pl.multiple_of(g * GROUP * HD + j * HD, HD), HD) for j in range(GROUP)
            ]
            out, log_total = attend(
                [q_ref[span, :] for span in spans],
                mask_ref[...],
                lambda slot: kv_ref[slot, g],
                lambda slot: kv_ref[slot, KV + g],
                lambda slot: key_mask_ref[slot],
                0,
                4,
                lambda i: i,
            )
            for j in range(GROUP):
                o_ref[spans[j], :] = out[j]
            lse_ref[g] = jnp.concatenate(log_total, axis=0)
            return carry

        lax.fori_loop(first, last, one, 0)

    def load_out():
        need(2)
        begin((3, 0), full_refs[1].at[0], w_out_ref)

    def make_middle():
        attended = o_ref[...].T
        for t in range(QD // TILE):
            attended_ref[t] = attended[:, t * TILE : (t + 1) * TILE]
        begin((4, 0), attended_ref, attended_out.at[0])
        finish((3, 0))
        added = jnp.dot(w_out_ref[...], o_ref[...], preferred_element_type=jnp.float32)
        middle = hidden_ref[...].astype(jnp.float32) + added.T
        middle_ref[...] = middle
        acc_ref[...] = jnp.zeros_like(acc_ref)
        unit_rows, unused = norm_parts(middle)
        normed = (unit_rows * gain_ref[0, 1:2]).astype(LOW)
        normed_ref[...] = normed
        turned_ref[0] = normed.T
        begin((5, 0), turned_ref.at[0], lhs_out.at[0, 2])

    per = WIDE // TILE

    def load_mlp(t):
        need(3 + t)
        need(7 + t)
        span = pl.ds(t * WIDE, WIDE)
        begin((6, t), full_refs[2].at[0, :, span], w_mlp_ref.at[t % 2, 0])
        begin((7, t), full_refs[3].at[0, :, span], w_mlp_ref.at[t % 2, 1])

    def make_units(t):
        finish((6, t))
        finish((7, t))
        normed = normed_ref[...]
        gate = jnp.dot(normed, w_mlp_ref[t % 2, 0], preferred_element_type=jnp.float32)
        up = jnp.dot(normed, w_mlp_ref[t % 2, 1], preferred_element_type=jnp.float32)
        units = (gate * sigmoid_of(gate) * up).astype(LOW)
        gate_low, up_low = gate.astype(LOW), up.astype(LOW)
        for i in range(per):
            cut = slice(i * TILE, (i + 1) * TILE)
            gate_ref[per * t + i] = gate_low[:, cut]
            up_ref[per * t + i] = up_low[:, cut]
            units_ref[per * t + i] = units[:, cut]
        span = pl.ds(per * t, per)
        begin((8, t), units_ref.at[span], units_out.at[0, span])
        begin((9, t), gate_ref.at[span], gate_out.at[span])
        begin((10, t), up_ref.at[span], up_out.at[span])

    def load_down(t):
        need(11 + t)
        span = pl.ds(t * WIDE, WIDE)
        begin((11, t), full_refs[4].at[0, :, span], w_down_ref.at[t % 2])

    def add_down(t):
        finish((11, t))
        units = jnp.concatenate([units_ref[per * t + i] for i in range(per)], axis=1)
        acc_ref[...] += jnp.dot(w_down_ref[t % 2], units.T, preferred_element_type=jnp.float32)

    def make_late_gains():
        finish((0, 1))
        gain_ref[1] = w_in_ref[:, pl.ds(QKV, SIDE)].astype(jnp.float32).T[:8]
        gains_ref[...] = gain_ref[...]

    tasks = {
        1: [make_masks],
        2: [move_rows],
        3: [lambda: load_in(0)],
        4: [lambda: make_keys(0, hidden_ref, kv_ref, 2), lambda: make_queries(q_ref)],
        6: [lambda: take_keys(0, kv_ref, kv_out, 2), lambda: attention(0, 1), load_out],
        7: [lambda: attention(1, 2)],
        8: [lambda: attention(2, 3)],
        9: [lambda: attention(3, 4)],
        10: [lambda: attention(4, 5)],
        11: [lambda: attention(5, 6), make_middle, lambda: load_mlp(0), lambda: load_in(1)],
        12: [lambda: load_mlp(1), lambda: make_units(0), make_late_gains],
        13: [lambda: load_mlp(2), lambda: make_units(1)],
        14: [lambda: load_mlp(3), lambda: make_units(2), lambda: load_down(0)],
        15: [lambda: make_units(3)],
        16: [lambda: load_down(1), lambda: add_down(0), lambda: load_down(2), lambda: add_down(1)],
    }

    ahead = 3
    for k in range(ahead):
        start_near(k)
        start_cross(k)

    @pl.when(moving)
    def _():
        row_move.start()

    @pl.when(jnp.logical_not(moving))
    def _():
        row_copy.start()

    send(11, 1, seq_ref, seq_peer_ref, over_core)
    hold(0).start()
    for k in range(count):
        send(5, k, own(k), full(k, section, 1), over_core)

    for k in range(count + 2):
        if k < count:
            hold(k).wait()
            store(k).start()
            if k + 1 < count:
                if k >= 1 and k - 1 not in stored_pieces:
                    stored_pieces.add(k - 1)
                    store(k - 1).wait()
                hold(k + 1).start()
            receive(0, k)
            send(6, k, full(k, section, 2), full(k, section, 3), over_core)
            which = 1 if k in direct else half
            mine = full_half(k, section, 2, which)
            send(2, k, mine, mine, over_y)
            start_near(k + ahead)
            receive(1, k)
            if k in direct:
                send(3, k, full_half(k, other, 0, 0), full_half(k, other, 2, 0), over_x)
                send(7, k, full(k, other, 0), full(k, other, 1), over_core)
            else:
                crossed = full_half(k, other, 0, half)
                send(3, k, crossed, crossed, over_z)
                send(7, k, crossed, full_half(k, other, 1, half), over_core)
            start_cross(k + ahead)
        j = k - 1
        if 0 <= j < count:
            receive(2, j)
            if j in direct:
                send(8, j, full_half(j, other, 2, 1), full_half(j, other, 3, 1), over_core)
                receive(3, j)
                send(9, j, full_half(j, other, 2, 0), full_half(j, other, 3, 0), over_core)
            else:
                crossed = full_half(j, other, 2, half)
                send(4, j, crossed, crossed, over_z)
                send(8, j, crossed, full_half(j, other, 3, half), over_core)
                receive(3, j)
                passed = full_half(j, other, 0, 1 - half)
                send(9, j, passed, full_half(j, other, 1, 1 - half), over_core)
        j = k - 2
        if 0 <= j < count and j not in direct:
            receive(4, j)
            passed = full_half(j, other, 2, 1 - half)
            send(10, j, passed, full_half(j, other, 3, 1 - half), over_core)
        for task in tasks.get(k, []):
            task()
    load_down(3)
    add_down(2)
    add_down(3)
    result_ref[...] = (middle_ref[...] + acc_ref[...].T).astype(LOW)
    make_keys(1, result_ref, next_kv_ref, 5)
    make_queries(next_q_ref)
    turned = jnp.dot(result_ref[...], natural_ref[...], preferred_element_type=jnp.float32)
    natural_out_ref[...] = turned.astype(LOW)
    for k in range(count):
        need(k)
    take_keys(1, next_kv_ref, next_kv_out, 5)
    for copy in started.values():
        copy.wait_send()
    for name in ((1, 1), (2, 0), (2, 1), (4, 0), (5, 0)):
        finish(name)
    for t in range(FF // WIDE):
        for name in (8, 9, 10):
            finish((name, t))


def first_layer(x_in, shards, seq_ids, angles, order, visible):
    rows = x_in.shape[2]
    quarter = shards[0].shape[0]
    widths = [shards[0].shape[1], QD, FF, FF, FF]
    pieces = 15
    tiles, head_tiles = FF // TILE, QD // TILE
    in_vmem = pl.BlockSpec(memory_space=pltpu.VMEM)
    in_smem = pl.BlockSpec(memory_space=pltpu.SMEM)

    def low(*shape):
        return jax.ShapeDtypeStruct(shape, LOW)

    def wide(*shape):
        return jax.ShapeDtypeStruct(shape, jnp.float32)

    dma = pltpu.SemaphoreType.DMA
    outs = pl.pallas_call(
        first_kernel,
        out_shape=[low(2, 4 * quarter, w) for w in widths]
        + [
            low(rows, D),
            low(QD, rows),
            low(4, 2 * KV, HD, rows),
            low(QD, rows),
            wide(KV, GROUP, rows),
            low(rows, D),
            wide(rows, D),
            low(2, 5, D, rows),
            low(2, head_tiles, rows, TILE),
            low(2, tiles, rows, TILE),
            low(tiles, rows, TILE),
            low(tiles, rows, TILE),
            wide(*seq_ids.shape[1:]),
            wide(2, 8, D),
            low(QD, rows),
            low(4, 2 * KV, HD, rows),
            low(rows, D),
            low(4, 16, rows),
            low(16, rows),
            jax.ShapeDtypeStruct((8,), jnp.int32),
            low(D, D),
        ],
        in_specs=[ANYWHERE] * 5 + [in_vmem] * 3 + [in_smem] * 2,
        out_specs=[ANYWHERE] * 5
        + [in_vmem, in_vmem, ANYWHERE, in_vmem, in_vmem, in_vmem, in_vmem]
        + [ANYWHERE] * 5
        + [in_vmem, in_vmem, in_vmem, ANYWHERE, in_vmem, in_vmem, in_vmem, in_smem, in_vmem],
        scratch_shapes=[
            dma((12, pieces)),
            dma((12, pieces)),
            dma((pieces,)),
            dma((3,)),
            dma((40,)),
            pltpu.VMEM((2, quarter, QD), LOW),
            pltpu.VMEM((rows, D), LOW),
            pltpu.VMEM((D, widths[0]), LOW),
            pltpu.VMEM((D, QD), LOW),
            pltpu.VMEM((2, 2, D, WIDE), LOW),
            pltpu.VMEM((2, D, WIDE), LOW),
            pltpu.VMEM((tiles, rows, TILE), LOW),
            pltpu.VMEM((tiles, rows, TILE), LOW),
            pltpu.VMEM((tiles, rows, TILE), LOW),
            pltpu.VMEM((rows, D), LOW),
            pltpu.VMEM((2, D, rows), LOW),
            pltpu.VMEM((head_tiles, rows, TILE), LOW),
            pltpu.VMEM((D, rows), jnp.float32),
            pltpu.VMEM((4, 2 * KV, HD, rows), LOW),
            pltpu.VMEM(seq_ids.shape[1:], jnp.float32),
            pltpu.VMEM((4, 16, rows), LOW),
            pltpu.VMEM((16, rows), LOW),
            pltpu.VMEM((2, 8, D), jnp.float32),
            pltpu.VMEM((4, 2 * KV, HD, rows), LOW),
            pltpu.VMEM(seq_ids.shape[1:], jnp.float32),
        ],
        compiler_params=pltpu.CompilerParams(
            collective_id=1, has_side_effects=True, vmem_limit_bytes=62 * 2**20
        ),
        cost_estimate=long_cost(230),
    )(x_in, *shards, seq_ids, *angles, order, visible)
    names = ("hidden", "q_t", "kv_t", "o_t", "lse", "result", "middle")
    saved = dict(zip(names, outs[5:12]))
    saved.update(gate=outs[15], up=outs[16])
    stores = dict(lhs=outs[12], attended=outs[13], units=outs[14])
    ahead = dict(hidden=outs[10], q_t=outs[19], kv_t=outs[20])
    info = (outs[24], outs[22], outs[23])
    return outs[:5], saved, ahead, stores, info, outs[18], outs[21], outs[25]


ANYWHERE = pl.BlockSpec(memory_space=pl.ANY)
WIDE = 768


def whole(shape, *index):
    return pl.BlockSpec(shape, lambda s: index + (0,) * (len(shape) - len(index)))


def sigmoid_of(value):
    return 0.5 * jnp.tanh(0.5 * value) + 0.5


def norm_parts(value):
    inverse = lax.rsqrt(jnp.mean(value * value, axis=-1, keepdims=True) + EPS)
    return value * inverse, inverse


def norm_back(grad_rows, value, gain_row):
    unit_rows, inverse = norm_parts(value)
    grad_unit = grad_rows * gain_row
    grad_gain = jnp.sum(grad_rows * unit_rows, axis=0, keepdims=True)
    inner = jnp.mean(grad_unit * unit_rows, axis=-1, keepdims=True)
    return inverse * (grad_unit - unit_rows * inner), grad_gain


def stored(stores, name, shape):
    return stores.get(name), jax.ShapeDtypeStruct(shape, LOW)


def copies_of(sem, pairs):
    copies = [pltpu.make_async_copy(x, y, sem.at[i]) for i, (x, y) in enumerate(pairs)]
    for copy in copies:
        copy.start()
    return copies


def mlp_forward_kernel(
    h_ref, o_ref, w_out_ref, w_gate_ref, w_up_ref, w_down_ref, gain_ref, *refs
):
    (
        result_ref,
        middle_ref,
        normed_t_ref,
        attended_ref,
        units_ref,
        gate_ref,
        up_ref,
        acc_ref,
        normed_ref,
    ) = refs[-9:]
    step = pl.program_id(0)

    @pl.when(step == 0)
    def _():
        attended = o_ref[...].T
        for t in range(attended_ref.shape[1]):
            attended_ref[0, t] = attended[:, t * TILE : (t + 1) * TILE]
        added = jnp.dot(w_out_ref[0], o_ref[...], preferred_element_type=jnp.float32)
        middle = h_ref[...].astype(jnp.float32) + added.T
        middle_ref[...] = middle
        acc_ref[...] = jnp.zeros_like(acc_ref)
        unit_rows, unused = norm_parts(middle)
        normed = (unit_rows * gain_ref[0, 1:2]).astype(LOW)
        normed_ref[...] = normed
        normed_t_ref[0, 0] = normed.T

    @pl.when(step > 0)
    def _():
        normed = normed_ref[...]
        gate = jnp.dot(normed, w_gate_ref[0], preferred_element_type=jnp.float32)
        up = jnp.dot(normed, w_up_ref[0], preferred_element_type=jnp.float32)
        units = (gate * sigmoid_of(gate) * up).astype(LOW)
        gate_low, up_low = gate.astype(LOW), up.astype(LOW)
        for t in range(WIDE // TILE):
            cut = slice(t * TILE, (t + 1) * TILE)
            gate_ref[t] = gate_low[:, cut]
            up_ref[t] = up_low[:, cut]
            units_ref[0, t] = units[:, cut]
        acc_ref[...] += jnp.dot(w_down_ref[0], units.T, preferred_element_type=jnp.float32)

    @pl.when(step == pl.num_programs(0) - 1)
    def _():
        result_ref[...] = (middle_ref[...] + acc_ref[...].T).astype(LOW)


def call_mlp_forward(layer, hidden, o_t, weights, gain_rows, stores):
    w_in, w_out_t, w_gate, w_up, w_down_t = weights
    rows = hidden.shape[0]
    steps, per = FF // WIDE, WIDE // TILE
    tiles, head_tiles = FF // TILE, QD // TILE
    names = ("lhs", "attended", "units")
    shapes = ((2, 5, D, rows), (2, head_tiles, rows, TILE), (2, tiles, rows, TILE))
    extra, aliases, store_shapes = [], {}, []
    for place, (name, shape) in enumerate(zip(names, shapes)):
        value, shape = stored(stores, name, shape)
        store_shapes.append(shape)
        if value is not None:
            aliases[7 + len(extra)] = 2 + place
            extra.append(value)

    def behind(s):
        return jnp.maximum(s - 1, 0)

    column = pl.BlockSpec((1, D, WIDE), lambda s: (layer, 0, behind(s)))
    kept = pl.BlockSpec((per, rows, TILE), lambda s: (behind(s), 0, 0))
    result, middle, lhs, attended, units, gate, up = pl.pallas_call(
        mlp_forward_kernel,
        grid=(steps + 1,),
        in_specs=[
            whole((rows, D)),
            whole((QD, rows)),
            whole((1, D, QD), layer),
            column,
            column,
            column,
            whole((1, 8, D), layer),
        ]
        + [ANYWHERE] * len(extra),
        out_specs=[
            whole((rows, D)),
            whole((rows, D)),
            whole((1, 1, D, rows), layer, 2),
            whole((1, head_tiles, rows, TILE), layer),
            pl.BlockSpec((1, per, rows, TILE), lambda s: (layer, behind(s), 0, 0)),
            kept,
            kept,
        ],
        out_shape=[
            jax.ShapeDtypeStruct((rows, D), LOW),
            jax.ShapeDtypeStruct((rows, D), jnp.float32),
            *store_shapes,
            jax.ShapeDtypeStruct((tiles, rows, TILE), LOW),
            jax.ShapeDtypeStruct((tiles, rows, TILE), LOW),
        ],
        scratch_shapes=[pltpu.VMEM((D, rows), jnp.float32), pltpu.VMEM((rows, D), LOW)],
        input_output_aliases=aliases,
        compiler_params=pltpu.CompilerParams(vmem_limit_bytes=62 * 2**20),
        cost_estimate=long_cost(25),
    )(hidden, o_t, w_out_t, w_gate, w_up, w_down_t, gain_rows, *extra)
    stores.update(lhs=lhs, attended=attended, units=units)
    return result, middle, gate, up


def pair_forward(layer, saved, weights, gain_rows, info, stores):
    o_t, lse = pair_attention_forward(info, saved["q_t"], saved["kv_t"])
    result, middle, gate, up = call_mlp_forward(
        layer, saved["hidden"], o_t, weights, gain_rows, stores
    )
    return dict(saved, o_t=o_t, lse=lse, middle=middle, gate=gate, up=up, result=result)


def mlp_backward_kernel(
    layer,
    grad_ref,
    gate_ref,
    up_ref,
    w_gate_ref,
    w_up_ref,
    w_down_ref,
    middle_ref,
    gain_ref,
    w_out_ref,
    *refs,
):
    (
        mlp_ref,
        pair_ref,
        grad_middle_ref,
        do_ref,
        gain_grad_ref,
        acc_ref,
        late_middle,
        late_out,
        late_sem,
    ) = refs[-9:]
    step = pl.program_id(0)
    per = gate_ref.shape[0]
    late = [
        pltpu.make_async_copy(middle_ref, late_middle, late_sem.at[0]),
        pltpu.make_async_copy(w_out_ref.at[layer], late_out, late_sem.at[1]),
    ]

    @pl.when(step == 0)
    def _():
        for copy in late:
            copy.start()

    gate = jnp.concatenate([gate_ref[t] for t in range(per)], axis=1).astype(jnp.float32)
    up = jnp.concatenate([up_ref[t] for t in range(per)], axis=1).astype(jnp.float32)
    grad_units = jnp.dot(grad_ref[...], w_down_ref[0], preferred_element_type=jnp.float32)
    sigmoid = sigmoid_of(gate)
    slope = grad_units * sigmoid
    tilted = slope * gate
    grad_gate = (up * (slope + tilted * (1.0 - sigmoid))).astype(LOW)
    grad_up = tilted.astype(LOW)
    for t in range(per):
        cut = slice(t * TILE, (t + 1) * TILE)
        mlp_ref[0, 2 * t] = grad_gate[:, cut]
        mlp_ref[0, 2 * t + 1] = grad_up[:, cut]
    part = jnp.dot(w_gate_ref[0], grad_gate.T, preferred_element_type=jnp.float32)
    part = part + jnp.dot(w_up_ref[0], grad_up.T, preferred_element_type=jnp.float32)

    @pl.when(step == 0)
    def _():
        acc_ref[...] = part
        pair_ref[0, 0] = grad_ref[...].T

    @pl.when(step > 0)
    def _():
        acc_ref[...] += part

    @pl.when(step == pl.num_programs(0) - 1)
    def _():
        for copy in late:
            copy.wait()
        grad_norm, grad_gain = norm_back(acc_ref[...].T, late_middle[...], gain_ref[0, 1:2])
        gain_grad_ref[...] = jnp.broadcast_to(grad_gain, gain_grad_ref.shape)
        grad_middle = grad_ref[...].astype(jnp.float32) + grad_norm
        grad_middle_ref[...] = grad_middle
        grad_branch = grad_middle.astype(LOW)
        pair_ref[0, 1] = grad_branch.T
        grad_attended = jnp.dot(grad_branch, late_out[...], preferred_element_type=jnp.float32)
        do_ref[...] = grad_attended.astype(LOW).T


def call_mlp_backward(layer, grad_low, saved, weights, gain_rows, stores):
    w_in, w_out_t, w_gate, w_up, w_down_t = weights
    rows = grad_low.shape[0]
    steps, per = FF // WIDE, WIDE // TILE
    mlp, mlp_shape = stored(stores, "mlp", (2, 2 * FF // TILE, rows, TILE))
    extra = [stores["lhs"]] if mlp is None else [stores["lhs"], mlp]
    aliases = {9: 1} if mlp is None else {9: 1, 10: 0}
    column = pl.BlockSpec((1, D, WIDE), lambda s: (layer, 0, s))
    kept = pl.BlockSpec((per, rows, TILE), lambda s: (s, 0, 0))
    mlp, lhs, grad_middle, do_t, grad_gain = pl.pallas_call(
        functools.partial(mlp_backward_kernel, layer),
        grid=(steps,),
        in_specs=[
            whole((rows, D)),
            kept,
            kept,
            column,
            column,
            column,
            ANYWHERE,
            whole((1, 8, D), layer),
            ANYWHERE,
        ]
        + [ANYWHERE] * len(extra),
        out_specs=[
            pl.BlockSpec((1, 2 * per, rows, TILE), lambda s: (layer, s, 0, 0)),
            whole((1, 2, D, rows), layer),
            whole((rows, D)),
            whole((QD, rows)),
            whole((8, D)),
        ],
        out_shape=[
            mlp_shape,
            jax.ShapeDtypeStruct(stores["lhs"].shape, LOW),
            jax.ShapeDtypeStruct((rows, D), jnp.float32),
            jax.ShapeDtypeStruct((QD, rows), LOW),
            jax.ShapeDtypeStruct((8, D), jnp.float32),
        ],
        scratch_shapes=[
            pltpu.VMEM((D, rows), jnp.float32),
            pltpu.VMEM((rows, D), jnp.float32),
            pltpu.VMEM((D, QD), LOW),
            pltpu.SemaphoreType.DMA((2,)),
        ],
        input_output_aliases=aliases,
        compiler_params=pltpu.CompilerParams(vmem_limit_bytes=62 * 2**20),
        cost_estimate=long_cost(25),
    )(
        grad_low,
        saved["gate"],
        saved["up"],
        w_gate,
        w_up,
        w_down_t,
        saved["middle"],
        gain_rows,
        w_out_t,
        *extra,
    )
    stores.update(lhs=lhs, mlp=mlp)
    return grad_middle, do_t, grad_gain


def mixed_backward_kernel(
    layer,
    dk_ref,
    dv_ref,
    gain_ref,
    gain_grad_ref,
    cos_ref,
    sin_ref,
    dq_all,
    h_all,
    grad_middle_all,
    natural_all,
    w_all,
    *refs,
):
    if layer == 0:
        outs = len(refs) - 27
        ahead = (refs[outs - 1], refs[outs + 4], *refs[-7:])
        refs = refs[: outs + 4] + refs[outs + 5 : -7]
    (
        mixed_out,
        lhs_out,
        result_ref,
        natural_out_ref,
        w_ref,
        acc_ref,
        tile_ref,
        gains_ref,
        near_ref,
        far_ref,
        passed_ref,
        dq_ref,
        h_ref,
        grad_middle_ref,
        natural_ref,
        send_sem,
        recv_sem,
        local_sem,
        load_sem,
    ) = refs[-19:]
    section = lax.axis_index(SECTION)
    column = lax.axis_index(CTX)
    place = lax.axis_index(WSH)
    over_z = (section, column + 1 - 2 * lax.rem(column, 2), place)
    over_core = (section, column, place + 1 - 2 * lax.rem(place, 2))
    rows = result_ref.shape[0]
    steps = QKV // TILE
    barrier = pltpu.get_barrier_semaphore()
    over_y = (1 - section, column, place)
    targets = (over_z, over_core, over_y) if layer == 0 else (over_z, over_core)
    for target in targets:
        pl.semaphore_signal(barrier, inc=1, device_id=target, device_id_type=MESH_ID)
    pl.semaphore_wait(barrier, len(targets))

    def remote(index, source, target, device):
        copy = pltpu.make_async_remote_copy(
            src_ref=source,
            dst_ref=target,
            send_sem=send_sem.at[index],
            recv_sem=recv_sem.at[index],
            device_id=device,
            device_id_type=MESH_ID,
        )
        copy.start()
        return copy

    crossed = [
        remote(2 * slot + part, source.at[2 * slot + 1], near_ref.at[slot, part], over_core)
        for slot in (1, 0)
        for part, source in enumerate((dk_ref, dv_ref))
    ]
    loads = copies_of(
        load_sem,
        [
            (w_all.at[layer], w_ref),
            (dq_all, dq_ref),
            (h_all, h_ref),
            (grad_middle_all, grad_middle_ref),
            (natural_all, natural_ref),
        ],
    )
    for copy in crossed[:2]:
        copy.wait_recv()
    for part, source in enumerate((dk_ref, dv_ref)):
        both = source[2].astype(jnp.float32) + near_ref[1, part].astype(jnp.float32)
        far_ref[part] = both.astype(LOW)
    passed = [remote(4 + part, far_ref.at[part], passed_ref.at[part], over_z) for part in range(2)]
    if layer == 0:
        finish = first_crossed(refs[0], ahead, section, place, over_core, over_y)
    for copy in loads:
        copy.wait()

    def add(t, grad_t):
        grad_t = grad_t.astype(LOW)
        tile_ref[t] = grad_t.T
        part = jnp.dot(
            w_ref[:, pl.ds(t * TILE, TILE)], grad_t, preferred_element_type=jnp.float32
        )
        if t == 0:
            acc_ref[...] = part
        else:
            acc_ref[...] += part

    def back(heads):
        return turn(heads, cos_ref[...], -sin_ref[...]).reshape(KD, rows)

    for t in range(QD // KD):
        add(t, back(dq_ref[pl.ds(t * KD, KD), :].reshape(KV, HD, rows)))
    row = lax.broadcasted_iota(jnp.int32, (rows, TILE), 0)
    lane = lax.broadcasted_iota(jnp.int32, (rows, TILE), 1)
    tile_ref[steps] = jnp.where(row == lane, 1.0, 0.0).astype(LOW)
    for copy in crossed[2:]:
        copy.wait_recv()
    for part, source in enumerate((dk_ref, dv_ref)):
        passed[part].wait_recv()
        own = source[0].astype(jnp.float32) + near_ref[0, part].astype(jnp.float32)
        own = own + passed_ref[part].astype(jnp.float32)
        add(QD // KD + part, back(own) if part == 0 else own.reshape(KD, rows))
    tiles = pltpu.make_async_copy(tile_ref, mixed_out.at[layer], local_sem.at[1])
    tiles.start()
    grad_norm, grad_gain = norm_back(
        acc_ref[...].T, h_ref[...].astype(jnp.float32), gain_ref[layer, :1]
    )
    both = jnp.concatenate(
        [grad_gain, gain_grad_ref[:1], jnp.zeros((rows - 2, D), jnp.float32)], axis=0
    )
    gains_ref[...] = both.T.astype(LOW)
    gains = pltpu.make_async_copy(gains_ref, lhs_out.at[layer, 4], local_sem.at[2])
    gains.start()
    result = (grad_middle_ref[...] + grad_norm).astype(LOW)
    result_ref[...] = result
    turned = jnp.dot(result, natural_ref[...], preferred_element_type=jnp.float32)
    natural_out_ref[...] = turned.astype(LOW)
    for copy in crossed + passed:
        copy.wait_send()
    tiles.wait()
    gains.wait()
    if layer == 0:
        finish()


def first_crossed(lhs_all, ahead, section, place, over_core, over_y):
    mlp_all, given_out, lhs_ref, rhs_ref, given_ref, local_sem, near_sem, peer_sem, far_sem = ahead
    other = 1 - section
    core = lax.rem(place, 2)
    tokens = lhs_all.shape[3]
    piece = lhs_all.shape[2] // 8

    def remote(send_sem, recv_sem, source, target, device):
        copy = pltpu.make_async_remote_copy(
            src_ref=source,
            dst_ref=target,
            send_sem=send_sem,
            recv_sem=recv_sem,
            device_id=device,
            device_id_type=MESH_ID,
        )
        copy.start()
        return copy

    pairs, peers = [], []
    for p in range(4):
        mine = lhs_all.at[other, 2, pl.ds((2 * p + core) * piece, piece), :]
        theirs = lhs_all.at[other, 2, pl.ds((2 * p + 1 - core) * piece, piece), :]
        pairs.append((mine, lhs_ref.at[pl.ds(p * piece, piece), pl.ds(0, tokens)]))
        target = lhs_ref.at[pl.ds((p ^ 1) * piece, piece), pl.ds(tokens, tokens)]
        peers.append(remote(near_sem.at[p], peer_sem.at[p], theirs, target, over_core))
    for t in range(2):
        pairs.append((mlp_all.at[other, t], rhs_ref.at[t, pl.ds(0, tokens)]))
        target = rhs_ref.at[t, pl.ds(tokens, tokens)]
        sems = (near_sem.at[4 + t], peer_sem.at[4 + t])
        peers.append(remote(*sems, mlp_all.at[other, t], target, over_core))
    copies = copies_of(local_sem, pairs)
    for copy in copies:
        copy.wait()
    for copy in peers:
        copy.wait_recv()
    sent = []
    for t in range(2):
        value = jnp.dot(lhs_ref[...], rhs_ref[t], preferred_element_type=jnp.float32)
        given_ref[t] = value.astype(LOW)
        sems = (far_sem.at[0, t], far_sem.at[1, t])
        sent.append(remote(*sems, given_ref.at[t], given_out.at[t], over_y))

    def finish():
        for copy in peers:
            copy.wait_send()
        for copy in sent:
            copy.wait()

    return finish


def call_mixed_backward(
    layer, dq_t, dk_t, dv_t, hidden, grad_middle, grad_gain, shared, angles, stores
):
    weights, gain_rows, natural = shared
    rows = hidden.shape[0]
    steps = QKV // TILE + 1
    mixed, mixed_shape = stored(stores, "mixed", (2, steps, rows, TILE))
    extra = [stores["lhs"]] if mixed is None else [stores["lhs"], mixed]
    aliases = {11: 1} if mixed is None else {11: 1, 12: 0}
    ahead = [stores["mlp"]] if layer == 0 else []
    half = D // 2
    ahead_shape = [jax.ShapeDtypeStruct((2, half, TILE), LOW)] if layer == 0 else []
    ahead_scratch = [
        pltpu.VMEM((half, 2 * rows), LOW),
        pltpu.VMEM((2, 2 * rows, TILE), LOW),
        pltpu.VMEM((2, half, TILE), LOW),
        pltpu.SemaphoreType.DMA((6,)),
        pltpu.SemaphoreType.DMA((6,)),
        pltpu.SemaphoreType.DMA((6,)),
        pltpu.SemaphoreType.DMA((2, 2)),
    ]
    in_vmem = pl.BlockSpec(memory_space=pltpu.VMEM)
    dma = pltpu.SemaphoreType.DMA
    part = (2, KV, HD, rows)
    mixed, lhs, result, turned, *given = pl.pallas_call(
        functools.partial(mixed_backward_kernel, layer),
        in_specs=[in_vmem] * 6 + [ANYWHERE] * (5 + len(extra) + len(ahead)),
        out_specs=[ANYWHERE, ANYWHERE, in_vmem, in_vmem] + [ANYWHERE] * len(ahead),
        out_shape=[
            mixed_shape,
            jax.ShapeDtypeStruct(stores["lhs"].shape, LOW),
            jax.ShapeDtypeStruct((rows, D), LOW),
            jax.ShapeDtypeStruct((rows, D), LOW),
            *ahead_shape,
        ],
        scratch_shapes=[
            pltpu.VMEM((D, weights[0].shape[2]), LOW),
            pltpu.VMEM((D, rows), jnp.float32),
            pltpu.VMEM((steps, rows, TILE), LOW),
            pltpu.VMEM((D, rows), LOW),
            pltpu.VMEM((2, *part), LOW),
            pltpu.VMEM(part, LOW),
            pltpu.VMEM(part, LOW),
            pltpu.VMEM((QD, rows), jnp.float32),
            pltpu.VMEM((rows, D), LOW),
            pltpu.VMEM((rows, D), jnp.float32),
            pltpu.VMEM((D, D), LOW),
            dma((6,)),
            dma((6,)),
            dma((3,)),
            dma((5,)),
        ]
        + ahead_scratch * len(ahead),
        input_output_aliases=aliases,
        compiler_params=pltpu.CompilerParams(
            collective_id=4 + layer, has_side_effects=True, vmem_limit_bytes=62 * 2**20
        ),
        cost_estimate=long_cost(30),
    )(
        dk_t,
        dv_t,
        gain_rows,
        grad_gain,
        *angles,
        dq_t,
        hidden,
        grad_middle,
        natural,
        weights[0],
        *extra,
        *ahead,
    )
    stores.update(lhs=lhs, mixed=mixed)
    if given:
        stores["given"] = given[0]
    return result, turned


def pair_backward(layer, grad_low, shared, saved, info, angles, stores, beside):
    grad_middle, do_t, grad_gain = call_mlp_backward(
        layer, grad_low, saved, shared[0], shared[1], stores
    )
    dq_t, dk_t, dv_t = pair_attention_backward(
        info, saved["q_t"], do_t, saved["o_t"], saved["lse"], saved["kv_t"]
    )
    dq_t, beside = lax.optimization_barrier((dq_t, beside))
    result, turned = call_mixed_backward(
        layer, dq_t, dk_t, dv_t, saved["hidden"], grad_middle, grad_gain, shared, angles, stores
    )
    return result, turned, beside


TILE = 384
CROSSED = 22
PLANE = 11


def spread_kernel(
    lhs_all,
    mlp_all,
    mixed_all,
    units_all,
    attended_all,
    grad_ref,
    given_all,
    in_out,
    head_out,
    mlp_out,
    down_out,
    gains_out,
    grad_out,
    mlp_peer,
    mixed_peer,
    units_peer,
    attended_peer,
    lhs_ref,
    rhs_ref,
    given_ref,
    sum_ref,
    side_ref,
    block_ref,
    last_given,
    last_ref,
    hold_ref,
    kept_ref,
    grad_sem,
    early_sem,
    lhs_sem,
    peer_send,
    peer_recv,
    load_sem,
    given_send,
    given_recv,
    side_send,
    side_recv,
    block_send,
    block_recv,
    last_send,
    last_recv,
):
    section = lax.axis_index(SECTION)
    column = lax.axis_index(CTX)
    place = lax.axis_index(WSH)
    other = 1 - section
    over_x = (section, column, lax.rem(place + 2, 4))
    over_y = (other, column, place)
    over_core = (section, column, place + 1 - 2 * lax.rem(place, 2))
    flip_low = column + 1 - 2 * lax.rem(column, 2)
    flip_high = lax.rem(column + 2, 4)
    flip_both = lax.rem(flip_low + 2, 4)
    over_z = [(section, c, place) for c in (flip_low, flip_high, flip_both)]
    origin = place ^ column

    barrier = pltpu.get_barrier_semaphore()
    for target in (over_x, over_y, over_core, *over_z):
        pl.semaphore_signal(barrier, inc=1, device_id=target, device_id_type=MESH_ID)
    moving, partner_column, partner_place = stream_partner(column, place)
    staying = jnp.logical_not(moving)

    @pl.when(moving)
    def _():
        for target in (section, other):
            pl.semaphore_signal(
                barrier,
                inc=1,
                device_id=(target, partner_column, partner_place),
                device_id_type=MESH_ID,
            )
        pl.semaphore_wait(barrier, 8)

    @pl.when(staying)
    def _():
        pl.semaphore_wait(barrier, 6)

    half = lhs_all.shape[2] // 2
    tokens = lhs_all.shape[3]
    quarter = half // 2
    share = quarter // 4
    layers = (section, other)

    def remote(source, target, send_sem, recv_sem, device):
        return pltpu.make_async_remote_copy(
            src_ref=source,
            dst_ref=target,
            send_sem=send_sem,
            recv_sem=recv_sem,
            device_id=device,
            device_id_type=MESH_ID,
        )

    core = lax.rem(place, 2)
    side = place // 2
    piece = half // 4

    def grad_copy(slot, device):
        return remote(
            grad_ref, grad_out.at[slot], grad_sem.at[0], grad_sem.at[1 + slot], device
        )

    hold_in = pltpu.make_async_copy(grad_ref, hold_ref, grad_sem.at[3])
    hold_out = pltpu.make_async_copy(hold_ref, grad_out.at[0], grad_sem.at[3])

    def grad_start():
        @pl.when(moving & (section == 0))
        def _():
            grad_copy(0, (0, partner_column, partner_place)).start()

        @pl.when(staying & (section == 0))
        def _():
            hold_in.start()
            hold_in.wait()
            hold_out.start()

    def grad_cross():
        @pl.when(moving & (section == 1))
        def _():
            grad_copy(1, (0, partner_column, partner_place)).start()

        @pl.when(staying & (section == 1))
        def _():
            grad_copy(1, over_y).start()

    def grad_finish():
        @pl.when(section == 0)
        def _():
            grad_copy(1, over_y).wait_recv()

        @pl.when(moving & (section == 0))
        def _():
            grad_copy(0, over_y).wait_recv()

        @pl.when(moving | (section == 1))
        def _():
            grad_copy(0, over_y).wait_send()

        @pl.when(staying & (section == 0))
        def _():
            hold_out.wait()

    def lhs_copies(group):
        kinds = (pl.ds(2, 1), pl.ds(0, 1), pl.ds(1, 1), pl.ds(3, 2))[group]
        copies = []
        for which in (1, 0):
            for p in range(4):
                index = which * 4 + p
                copies.append(
                    pltpu.make_async_copy(
                        lhs_all.at[layers[which], kinds, pl.ds((2 * p + core) * piece, piece), :],
                        lhs_ref.at[which, kinds, pl.ds(p * piece, piece), pl.ds(0, tokens)],
                        lhs_sem.at[group, 0, index],
                    )
                )
                span = pl.ds((2 * p + 1 - core) * piece, piece)
                copies.append(
                    remote(
                        lhs_all.at[layers[which], kinds, span, :],
                        lhs_ref.at[
                            which, kinds, pl.ds((p ^ 1) * piece, piece), pl.ds(tokens, tokens)
                        ],
                        lhs_sem.at[group, 1, index],
                        lhs_sem.at[group, 2, index],
                        over_core,
                    )
                )
        return copies

    sources = (
        (mlp_all, mlp_peer, lambda tile: tile),
        (mixed_all, mixed_peer, lambda tile: tile - 16),
        (units_all, units_peer, lambda tile: tile - CROSSED),
        (attended_all, attended_peer, lambda tile: tile - CROSSED - 8),
    )

    def peer_copy(which, tile, source):
        mine, theirs, place_of = sources[source]
        return remote(
            mine.at[layers[which], place_of(tile)],
            theirs.at[layers[which], place_of(tile)],
            peer_send.at[which, tile],
            peer_recv.at[which, tile],
            over_core,
        )

    def peer_wait(which, tile):
        return remote(
            mlp_all.at[layers[which], 0],
            mlp_peer.at[layers[which], 0],
            peer_send.at[which, tile],
            peer_recv.at[which, tile],
            over_core,
        )

    def peer_starts(crossed, which, i):
        for early in (True, False):

            @pl.when(((i < 8) == early) & (i < PLANE))
            def _():
                late = 1 - early
                if crossed:
                    peer_copy(which, 2 * i, late).start()
                    peer_copy(which, 2 * i + 1, late).start()
                else:
                    peer_copy(1, CROSSED + i, 2 + late).start()
                    peer_copy(0, CROSSED + i, 2 + late).start()

    def loads(slot, which, tile, source):
        mine, theirs, place_of = sources[source]
        return (
            pltpu.make_async_copy(
                mine.at[layers[which], place_of(tile)],
                rhs_ref.at[slot, pl.ds(0, tokens)],
                load_sem.at[slot, 0],
            ),
            pltpu.make_async_copy(
                theirs.at[layers[which], place_of(tile)],
                rhs_ref.at[slot, pl.ds(tokens, tokens)],
                load_sem.at[slot, 1],
            ),
        )

    def load_start(slot, which, tile, source, early):
        peer_wait(which, tile).wait_recv()
        for flag in (True, False):

            @pl.when(early == flag)
            def _():
                for copy in loads(slot, which, tile, source + 1 - flag):
                    copy.start()

    def product(slot, which, tile, kind):
        for copy in loads(slot, which, 0, 0):
            copy.wait()
        return jnp.dot(
            lhs_ref[which, kind], rhs_ref[slot], preferred_element_type=jnp.float32
        )

    def crossed_kind(tile):
        return jnp.where(tile < 16, 2, jnp.where(tile < 21, 3, 4))

    def plane_kind(i):
        return jnp.where(i < 8, 0, 1)

    def sorted_sides(value):
        blocks = value.reshape(4, 2, share, TILE)
        first, second = blocks[:, 0], blocks[:, 1]
        low = jnp.broadcast_to(side == 0, first.shape)
        away = jnp.where(low, second, first).reshape(quarter, TILE)
        kept = jnp.where(low, first, second).reshape(quarter, TILE)
        return jnp.concatenate([away, kept], axis=0).astype(LOW)

    def given_copy(tile):
        slot = lax.rem(tile, 4)
        return remote(
            given_ref.at[slot],
            sum_ref.at[tile],
            given_send.at[slot],
            given_recv.at[tile],
            over_y,
        )

    def side_copy(unit):
        return remote(
            sum_ref.at[unit, pl.ds(0, quarter)],
            side_ref.at[unit // 2, pl.ds(lax.rem(unit, 2) * quarter, quarter)],
            side_send.at[unit],
            side_recv.at[unit],
            over_x,
        )

    def block_span(k):
        return pl.ds(pl.multiple_of((origin ^ k) * 2 * share, 2 * share), 2 * share)

    def block_copy(pair, k):
        return remote(
            side_ref.at[pair, block_span(k + 1)],
            block_ref.at[pair, k],
            block_send.at[pair, k],
            block_recv.at[pair, k],
            over_z[1 if k == 1 else 0],
        )

    def last_copy(i):
        return remote(
            last_given.at[i], last_ref.at[i], last_send.at[i], last_recv.at[i], over_y
        )

    def combine(pair):
        parts = []
        for e in range(2):
            unit = 2 * pair + e
            side_copy(unit).wait_recv()
            kept = sum_ref[unit, pl.ds(quarter, quarter)].astype(jnp.float32)
            got = side_ref[pair, pl.ds(e * quarter, quarter)].astype(jnp.float32)
            got = jnp.concatenate([got[quarter // 2 :], got[: quarter // 2]], axis=0)
            parts.append((kept + got).reshape(4, share, TILE))
        both = jnp.concatenate(parts, axis=1).reshape(8 * share, TILE)
        side_ref[pair] = both.astype(LOW)
        block_copy(pair, 2).start()
        block_copy(pair, 0).start()

    def relay(pair):
        for k, block in ((2, 2), (0, 0)):
            block_copy(pair, k).wait_recv()
            span = block_span(block)
            total = side_ref[pair, span].astype(jnp.float32)
            total = total + block_ref[pair, k].astype(jnp.float32)
            side_ref[pair, span] = total.astype(LOW)
            if k == 2:
                block_copy(pair, 1).start()

    def settle(pair):
        block_copy(pair, 1).wait_recv()
        total = side_ref[pair, block_span(0)].astype(jnp.float32)
        total = total + block_ref[pair, 1].astype(jnp.float32)
        return total[:share], total[share:]

    early_copies = copies_of(early_sem, [(given_all.at[t], sum_ref.at[t]) for t in range(2)])
    for copy in lhs_copies(0):
        copy.start()
    peer_starts(True, 1, 1)
    peer_starts(False, 0, 0)
    peer_starts(True, 0, 0)
    for group in (1, 2, 3):
        for copy in lhs_copies(group):
            copy.start()
    grad_start()
    for copy in lhs_copies(0):
        copy.wait()
    for copy in early_copies:
        copy.wait()

    def within(i, low=0):
        return (i >= low) & (i < low + PLANE)

    def step(i, carry):
        peer_starts(True, 1, i + 2)
        peer_starts(False, 0, i + 1)
        peer_starts(True, 0, i + 1)

        for group, when in ((1, 0), (2, 6), (3, 6)):

            @pl.when(i == when)
            def _():
                for copy in lhs_copies(group):
                    copy.wait()

        @pl.when(i + 1 < PLANE)
        def _():
            j = i + 1
            load_start(0, 1, 2 * j, 0, j < 8)
            load_start(1, 1, 2 * j + 1, 0, j < 8)
            for e in range(2):
                tile = 2 * j + e
                value = product(e, 1, tile, crossed_kind(tile))

                @pl.when(j >= 3)
                def _():
                    given_copy(tile - 4).wait_send()

                given_ref[lax.rem(tile, 4)] = value.astype(LOW)
                given_copy(tile).start()

        @pl.when(i < PLANE)
        def _():
            load_start(2, 1, CROSSED + i, 2, i < 8)
            load_start(0, 0, CROSSED + i, 2, i < 8)
            for e in range(2):
                unit = CROSSED + 2 * i + e
                value = product(2 - 2 * e, 1 - e, CROSSED + i, plane_kind(i))
                sum_ref[unit] = sorted_sides(value)
                side_copy(unit).start()

        @pl.when(within(i, 1))
        def _():
            combine(PLANE + i - 1)

        @pl.when(i < PLANE)
        def _():
            load_start(1, 0, 2 * i, 0, i < 8)
            load_start(2, 0, 2 * i + 1, 0, i < 8)
            for e in range(2):
                tile = 2 * i + e
                value = product(1 + e, 0, tile, crossed_kind(tile))

                @pl.when(i > 0)
                def _():
                    given_copy(tile).wait_recv()

                sum_ref[tile] = sorted_sides(value + sum_ref[tile].astype(jnp.float32))
                side_copy(tile).start()

        @pl.when(i == PLANE - 1)
        def _():
            grad_cross()

        @pl.when(within(i, 2))
        def _():
            j = i - 2
            given, kept = settle(PLANE + j)
            kept_ref[j] = kept
            last_given[j] = jnp.concatenate(
                [given, jnp.zeros((last_given.shape[1] - share, TILE), jnp.float32)], axis=0
            ).astype(LOW)
            last_copy(j).start()

        @pl.when(within(i, 1))
        def _():
            combine(i - 1)
            relay(PLANE + i - 1)
            relay(i - 1)

        @pl.when(within(i, 2))
        def _():
            j = i - 2
            tiles = settle(j)

            def columns(base):
                return pl.ds(pl.multiple_of(base * TILE, TILE), TILE)

            @pl.when(j < 8)
            def _():
                for e in range(2):
                    mlp_out[:, columns(8 * e + j)] = tiles[e]

            @pl.when(j >= 8)
            def _():
                in_out[:, columns(2 * (j - 8))] = tiles[0]

            @pl.when((j >= 8) & (j < 10))
            def _():
                in_out[:, columns(2 * (j - 8) + 1)] = tiles[1]

            @pl.when(j == 10)
            def _():
                gains_out[...] = tiles[1][:, :SIDE].T[:8]

        @pl.when(within(i, 3))
        def _():
            j = i - 3

            def columns(base):
                return pl.ds(pl.multiple_of(base * TILE, TILE), TILE)

            last_copy(j).wait_recv()
            total = (kept_ref[j] + last_ref[j].astype(jnp.float32)[:share]).T

            @pl.when(j < 8)
            def _():
                down_out[columns(j), :] = total

            @pl.when(j >= 8)
            def _():
                head_out[columns(j - 8), :] = total

        return carry

    lax.fori_loop(0, PLANE + 3, step, 0)

    def drain(i, carry):
        for e in range(4):
            side_copy(4 * i + e).wait_send()
        for e in range(2):
            for k in range(3):
                block_copy(2 * i + e, k).wait_send()
        last_copy(i).wait_send()
        for tile in (2 * i, 2 * i + 1, CROSSED + i):
            peer_wait(0, tile).wait_send()

        @pl.when(i > 0)
        def _():
            for tile in (2 * i, 2 * i + 1):
                peer_wait(1, tile).wait_send()

        peer_wait(1, CROSSED + i).wait_send()
        return carry

    lax.fori_loop(0, PLANE, drain, 0)
    grad_finish()
    for e in range(4):
        given_copy(2 * PLANE - 4 + e).wait_send()


def spread_all(lhs, mlp, mixed, units, attended, given, grad):
    tiles = 3 * PLANE
    half = lhs.shape[2] // 2
    share = half // 8
    tokens = lhs.shape[3]
    sources = (mlp, mixed, units, attended)
    dma = pltpu.SemaphoreType.DMA
    anywhere = pl.BlockSpec(memory_space=pl.ANY)
    return pl.pallas_call(
        spread_kernel,
        out_shape=[
            jax.ShapeDtypeStruct((share, QKV), jnp.float32),
            jax.ShapeDtypeStruct((QD, share), jnp.float32),
            jax.ShapeDtypeStruct((share, 2 * FF), jnp.float32),
            jax.ShapeDtypeStruct((FF, share), jnp.float32),
            jax.ShapeDtypeStruct((8, share), jnp.float32),
            jax.ShapeDtypeStruct((2, *grad.shape), LOW),
            *[jax.ShapeDtypeStruct(v.shape, LOW) for v in sources],
        ],
        in_specs=[anywhere] * 7,
        out_specs=[pl.BlockSpec(memory_space=pltpu.VMEM)] * 5 + [anywhere] * 5,
        scratch_shapes=[
            pltpu.VMEM((2, lhs.shape[1], half, 2 * tokens), LOW),
            pltpu.VMEM((3, 2 * tokens, TILE), LOW),
            pltpu.VMEM((4, half, TILE), LOW),
            pltpu.VMEM((4 * PLANE, half, TILE), LOW),
            pltpu.VMEM((2 * PLANE, half, TILE), LOW),
            pltpu.VMEM((2 * PLANE, 3, 2 * share, TILE), LOW),
            pltpu.VMEM((PLANE, share + 8, TILE), LOW),
            pltpu.VMEM((PLANE, share + 8, TILE), LOW),
            pltpu.VMEM(grad.shape, LOW),
            pltpu.VMEM((PLANE, share, TILE), jnp.float32),
            dma((4,)),
            dma((2,)),
            dma((4, 3, 8)),
            dma((2, tiles)),
            dma((2, tiles)),
            dma((3, 2)),
            dma((4,)),
            dma((CROSSED,)),
            dma((4 * PLANE,)),
            dma((4 * PLANE,)),
            dma((2 * PLANE, 3)),
            dma((2 * PLANE, 3)),
            dma((PLANE,)),
            dma((PLANE,)),
        ],
        compiler_params=pltpu.CompilerParams(
            collective_id=2, has_side_effects=True, vmem_limit_bytes=62 * 2**20
        ),
        cost_estimate=long_cost(250),
    )(lhs, *sources, grad, given)[:6]


def on_device_pairs(
    x_in, cotangent, w_qkv, w_out, w_gate_up, w_down, gains, order, visible, seq_ids
):
    section = lax.axis_index(SECTION)
    column = lax.axis_index(CTX)
    place = lax.axis_index(WSH)
    core = place % 2
    side = place // 2
    rows = x_in.shape[2]
    quarter = D // 4
    share = quarter // 4
    slot = column % 2 + 2 * core
    first_section = section == 0

    def partner(index):
        z, w = index // 4, index % 4
        if (z < 2) == (w % 2 == 1):
            return ((z + 2) % 4) * 4 + (w ^ 1)
        return index

    pairs = [(i, partner(i)) for i in range(16)]
    moving = (column < 2) == (core == 1)

    def placed(value, layer):
        crossing = [((1 - layer) * 16 + i, layer * 16 + j) for i, j in pairs]
        other = lax.ppermute(value, (SECTION, CTX, WSH), crossing)
        inside = [(layer * 16 + i, layer * 16 + j) for i, j in pairs if i != j]
        return lax.ppermute(value, (SECTION, CTX, WSH), inside), value, other

    def chosen(first, second):
        return jnp.where(first_section, first, second)

    def sorted_rows(value):
        blocks = value.reshape(2, 2, share, value.shape[1])
        return blocks.transpose(1, 0, 2, 3).reshape(value.shape)

    gain_columns = jnp.concatenate(
        [gains[0].T, jnp.zeros((quarter, SIDE - gains.shape[1]), LOW)], axis=1
    )
    shards = [
        sorted_rows(jnp.concatenate([w_qkv[0], gain_columns], axis=1)),
        sorted_rows(w_out[0].T),
        sorted_rows(w_gate_up[0]),
        sorted_rows(w_down[0].T),
    ]
    angles = pair_angles(order[section, slot], rows)
    weights, saved_one, ahead, stores, info, gain_rows, early, natural = first_layer(
        x_in, shards, seq_ids, angles, order, visible
    )
    upstream = cotangent[section, 0]
    crossing = [(i, j) for i, j in pairs if i != j]
    upstream, early = lax.optimization_barrier((upstream, early))
    upstream = jnp.where(moving, lax.ppermute(upstream, (CTX, WSH), crossing), upstream)
    grad_low = contract(upstream, natural, 1, 1).astype(LOW)
    saved_two = pair_forward(1, ahead, weights, gain_rows, info, stores)
    late = contract(saved_two["result"], natural, 1, 0).astype(LOW)

    own, away = chosen(early, late), chosen(late, early)
    swaps = [(s * 16 + i, (1 - s) * 16 + j) for s in range(2) for i, j in pairs]
    other = lax.ppermute(away, (SECTION, CTX, WSH), swaps)
    mine = lax.ppermute(own, (CTX, WSH), crossing)
    shared = (weights, gain_rows, natural)
    grad_two, turned, unused = pair_backward(
        1, grad_low, shared, saved_two, info, angles, stores, early
    )
    grad_two, turned, mine, other = lax.optimization_barrier((grad_two, turned, mine, other))
    mine = jnp.where(moving, mine, own)
    activations = jnp.stack([chosen(mine, other), chosen(other, mine)])
    later = placed(turned, 1)
    grad_one, turned, later = pair_backward(
        0, grad_two, shared, saved_one, info, angles, stores, later
    )
    names = ("lhs", "mlp", "mixed", "units", "attended", "given")
    *shares, earlier = spread_all(*[stores[k] for k in names], turned)
    later = (later[2], jnp.where(moving, later[0], later[1]))
    input_grads = jnp.stack([chosen(earlier[m], later[m]).astype(jnp.float32) for m in range(2)])

    share_in, share_head, share_mlp, share_down, share_gains = shares
    return (
        activations[None, :, None],
        input_grads[None, :, None],
        share_in[None],
        share_head[None],
        share_mlp[None],
        share_down[None],
        share_gains[None, :2],
    )


def solution(mesh):
    in_specs = (
        P(None, "wsh", "ctx", None),
        P(None, "wsh", "ctx", None),
        P("section", "wsh", None),
        P("section", None, "wsh"),
        P("section", "wsh", None),
        P("section", None, "wsh"),
        P("section", None, "wsh"),
        P(),
        P(),
        P(None, "wsh", None),
    )
    out_specs = (
        P("section", None, "wsh", "ctx", None),
        P("section", None, "wsh", "ctx", None),
        P("section", ("ctx", "wsh"), None),
        P("section", None, ("ctx", "wsh")),
        P("section", ("ctx", "wsh"), None),
        P("section", None, ("ctx", "wsh")),
        P("section", None, ("ctx", "wsh")),
    )
    body = on_device_pairs if fits_pairs(mesh) else on_device_general
    return jax.shard_map(
        body, mesh=mesh, in_specs=in_specs, out_specs=out_specs, check_vma=False
    )
```

```python
import functools

import jax
import jax.numpy as jnp
from jax import lax
from jax.experimental import pallas as pl
from jax.experimental.pallas import tpu as pltpu
from jax.sharding import PartitionSpec as P

D = 1152
H = 18
KV = 6
HD = 64
FF = 3072
SECTION, CTX, WSH = "section", "ctx", "wsh"


NEG = -1e30
EPS = 1e-05


def shifted(value, axis, by):
    devices = lax.axis_size(axis)
    pairs = [(i, i + by) for i in range(devices) if 0 <= i + by < devices]
    return lax.ppermute(value, axis, pairs)


def rms_forward(hidden, gain_row):
    inverse = lax.rsqrt(jnp.mean(hidden * hidden, axis=-1, keepdims=True) + EPS)
    unit_rows = hidden * inverse
    return (unit_rows * gain_row, unit_rows, inverse)


def rms_backward(grad_rows, unit_rows, inverse, gain_row):
    grad_unit = grad_rows * gain_row
    grad_gain = jnp.sum(grad_rows * unit_rows, axis=0)
    inner = jnp.mean(grad_unit * unit_rows, axis=-1, keepdims=True)
    return (inverse * (grad_unit - unit_rows * inner), grad_gain)


def rotation(positions):
    frequency = 10000.0 ** (-(jnp.arange(HD // 2, dtype=jnp.float32) * 2.0 / HD))
    angles = positions.astype(jnp.float32)[:, None] * frequency[None, :]
    return (jnp.cos(angles), jnp.sin(angles))


def rotate(vectors, cosine, sine):
    half_width = vectors.shape[-1] // 2
    first_half = vectors[..., :half_width]
    second_half = vectors[..., half_width:]
    cos_rows = cosine[:, None, :]
    sin_rows = sine[:, None, :]
    return jnp.concatenate(
        [
            first_half * cos_rows - second_half * sin_rows,
            first_half * sin_rows + second_half * cos_rows,
        ],
        axis=-1,
    )


def stretch_width(rows, n_ctx):
    per_stretch = min(n_ctx, max(1, 512 // rows))
    while n_ctx % per_stretch:
        per_stretch -= 1
    return per_stretch


def sweep(step_fn, init, items, alive):

    def guarded(state, packed):
        item, live = packed
        return step_fn(state, item)

    return lax.scan(guarded, init, (items, alive))


def tables(order, visible, seq_ids, batch_index, column, rows, n_ctx):
    order_row = order[batch_index]
    own_block = order_row[column]
    seq_row = seq_ids[batch_index, 0]
    own_seq = lax.dynamic_slice_in_dim(seq_row, column * rows, rows)
    device_vis = visible[own_block][order_row]
    key_vis = jnp.broadcast_to(device_vis[:, None], (n_ctx, rows)).reshape(n_ctx * rows)
    positions = own_block * rows + jnp.arange(rows, dtype=jnp.int32)
    return ((own_seq, seq_row, key_vis, device_vis), positions)


def key_items(key_rows, value_rows, info, per_stretch, rows):
    own_seq, seq_row, key_vis, device_vis = info
    length = key_rows.shape[0]
    size = per_stretch * rows
    count = length // size
    items = (
        key_rows.reshape(count, size, KV, HD),
        value_rows.reshape(count, size, KV, HD),
        key_vis.reshape(count, size),
        seq_row.reshape(count, size),
    )
    alive = jnp.sum(device_vis.reshape(count, per_stretch), axis=-1) > 0
    return (items, alive, size)


def masked_scores(queries, key_part, vis_part, seq_part, own_seq):
    scores = jnp.einsum(
        "nkgd,mkd->kgnm", queries, key_part, preferred_element_type=jnp.float32
    ) * HD ** (-0.5)
    allowed = (vis_part[None, :] == 1) & (own_seq[:, None] == seq_part[None, :])
    return (jnp.where(allowed[None, None], scores, NEG), allowed)


def attention_forward(queries, key_rows, value_rows, info, per_stretch, rows):
    own_seq = info[0]
    items, alive, size = key_items(key_rows, value_rows, info, per_stretch, rows)
    group = H // KV

    def lse_step(state, item):
        high, total = state
        key_part, value_part, vis_part, seq_part = item
        masked, allowed = masked_scores(queries, key_part, vis_part, seq_part, own_seq)
        top = jnp.maximum(high, jnp.max(masked, axis=-1))
        terms = jnp.where(allowed[None, None], jnp.exp(masked - top[..., None]), 0.0)
        return ((top, total * jnp.exp(high - top) + jnp.sum(terms, axis=-1)), None)

    start_state = (
        jnp.full((KV, group, rows), NEG, jnp.float32),
        jnp.zeros((KV, group, rows), jnp.float32),
    )
    (high, total), unused = sweep(lse_step, start_state, items, alive)
    log_total = high + jnp.log(total)

    def out_step(acc, item):
        key_part, value_part, vis_part, seq_part = item
        masked, allowed = masked_scores(queries, key_part, vis_part, seq_part, own_seq)
        probs = jnp.where(allowed[None, None], jnp.exp(masked - log_total[..., None]), 0.0).astype(
            jnp.bfloat16
        )
        return (
            acc
            + jnp.einsum("kgnm,mkd->nkgd", probs, value_part, preferred_element_type=jnp.float32),
            None,
        )

    attended, unused_two = sweep(
        out_step, jnp.zeros((rows, KV, group, HD), jnp.float32), items, alive
    )
    return (attended, log_total)


def attention_backward(
    queries, key_rows, value_rows, info, per_stretch, rows, log_total, grad_att, delta
):
    own_seq = info[0]
    items, alive, size = key_items(key_rows, value_rows, info, per_stretch, rows)
    group = H // KV

    def back_step(grad_query, item):
        key_part, value_part, vis_part, seq_part = item
        masked, allowed = masked_scores(queries, key_part, vis_part, seq_part, own_seq)
        probs = jnp.where(allowed[None, None], jnp.exp(masked - log_total[..., None]), 0.0)
        probs_low = probs.astype(jnp.bfloat16)
        grad_probs = jnp.einsum(
            "nkgd,mkd->kgnm", grad_att, value_part, preferred_element_type=jnp.float32
        )
        grad_scores = (probs * (grad_probs - delta[..., None])).astype(jnp.bfloat16)
        grad_query = grad_query + jnp.einsum(
            "kgnm,mkd->nkgd", grad_scores, key_part, preferred_element_type=jnp.float32
        ) * HD ** (-0.5)
        grad_keys = jnp.einsum(
            "kgnm,nkgd->mkd", grad_scores, queries, preferred_element_type=jnp.float32
        ) * HD ** (-0.5)
        grad_values = jnp.einsum(
            "kgnm,nkgd->mkd", probs_low, grad_att, preferred_element_type=jnp.float32
        )
        return (grad_query, (grad_keys, grad_values))

    grad_query, (grad_keys, grad_values) = sweep(
        back_step, jnp.zeros((rows, KV, group, HD), jnp.float32), items, alive
    )
    length = key_rows.shape[0]
    return (grad_query, grad_keys.reshape(length, KV, HD), grad_values.reshape(length, KV, HD))


def layer_forward(hidden, weights, info, positions, per_stretch, rows):
    w_qkv, w_out, w_gate_up, w_down, gains = weights
    query_width = H * HD
    key_width = KV * HD
    gain_attn = gains[0].astype(jnp.float32)
    gain_ffn = gains[1].astype(jnp.float32)
    normed, unit_one, inverse_one = rms_forward(hidden, gain_attn)
    normed_low = normed.astype(jnp.bfloat16)
    mixed = jnp.dot(normed_low, w_qkv, preferred_element_type=jnp.float32)
    cosine, sine = rotation(positions)
    queries = (
        rotate(mixed[:, :query_width].reshape(rows, H, HD), cosine, sine)
        .astype(jnp.bfloat16)
        .reshape(rows, KV, H // KV, HD)
    )
    key_own = rotate(
        mixed[:, query_width : query_width + key_width].reshape(rows, KV, HD), cosine, sine
    ).astype(jnp.bfloat16)
    value_own = mixed[:, query_width + key_width :].reshape(rows, KV, HD).astype(jnp.bfloat16)
    key_rows, value_rows = (
        lax.all_gather(key_own, "ctx", axis=0, tiled=True),
        lax.all_gather(value_own, "ctx", axis=0, tiled=True),
    )
    attended, log_total = attention_forward(queries, key_rows, value_rows, info, per_stretch, rows)
    attended_low = attended.reshape(rows, query_width).astype(jnp.bfloat16)
    middle = hidden + jnp.dot(attended_low, w_out, preferred_element_type=jnp.float32)
    normed_two, unit_two, inverse_two = rms_forward(middle, gain_ffn)
    normed_two_low = normed_two.astype(jnp.bfloat16)
    gate_up = jnp.dot(normed_two_low, w_gate_up, preferred_element_type=jnp.float32)
    gate_part = gate_up[:, :FF]
    up_part = gate_up[:, FF:]
    units_low = (jax.nn.silu(gate_part) * up_part).astype(jnp.bfloat16)
    result = middle + jnp.dot(units_low, w_down, preferred_element_type=jnp.float32)
    saved = {
        "unit_one": unit_one,
        "inverse_one": inverse_one,
        "normed_low": normed_low,
        "cosine": cosine,
        "sine": sine,
        "queries": queries,
        "key_rows": key_rows,
        "value_rows": value_rows,
        "attended": attended,
        "log_total": log_total,
        "attended_low": attended_low,
        "unit_two": unit_two,
        "inverse_two": inverse_two,
        "normed_two_low": normed_two_low,
        "gate_part": gate_part,
        "up_part": up_part,
        "units_low": units_low,
    }
    return (result, saved)


def layer_backward(grad_rows, weights, saved, info, per_stretch, rows):
    w_qkv, w_out, w_gate_up, w_down, gains = weights
    query_width = H * HD
    gain_attn = gains[0].astype(jnp.float32)
    gain_ffn = gains[1].astype(jnp.float32)
    gate_part = saved["gate_part"]
    grad_low = grad_rows.astype(jnp.bfloat16)
    grad_units = jnp.dot(grad_low, w_down.T, preferred_element_type=jnp.float32)
    sigmoid = jax.nn.sigmoid(gate_part)
    grad_gate = grad_units * saved["up_part"] * sigmoid * (1.0 + gate_part * (1.0 - sigmoid))
    grad_up = grad_units * gate_part * sigmoid
    grad_mix_low = jnp.concatenate([grad_gate, grad_up], axis=-1).astype(jnp.bfloat16)
    grad_normed_two = jnp.dot(grad_mix_low, w_gate_up.T, preferred_element_type=jnp.float32)
    grad_mid_norm, grad_gain_two = rms_backward(
        grad_normed_two, saved["unit_two"], saved["inverse_two"], gain_ffn
    )
    grad_middle = grad_rows + grad_mid_norm
    grad_branch_low = grad_middle.astype(jnp.bfloat16)
    grad_att = (
        jnp.dot(grad_branch_low, w_out.T, preferred_element_type=jnp.float32)
        .astype(jnp.bfloat16)
        .reshape(rows, KV, H // KV, HD)
    )
    delta = jnp.einsum("nkgd,nkgd->kgn", grad_att.astype(jnp.float32), saved["attended"])
    grad_query, grad_keys, grad_values = attention_backward(
        saved["queries"],
        saved["key_rows"],
        saved["value_rows"],
        info,
        per_stretch,
        rows,
        saved["log_total"],
        grad_att,
        delta,
    )
    key_total, value_total = (
        lax.psum_scatter(
            grad_keys.astype(jnp.bfloat16), "ctx", scatter_dimension=0, tiled=True
        ).astype(jnp.float32),
        lax.psum_scatter(
            grad_values.astype(jnp.bfloat16), "ctx", scatter_dimension=0, tiled=True
        ).astype(jnp.float32),
    )
    cosine = saved["cosine"]
    back_sine = -saved["sine"]
    grad_q = rotate(grad_query.reshape(rows, H, HD), cosine, back_sine).reshape(rows, query_width)
    grad_k = rotate(key_total, cosine, back_sine).reshape(rows, KV * HD)
    grad_v = value_total.reshape(rows, KV * HD)
    grad_qkv_low = jnp.concatenate([grad_q, grad_k, grad_v], axis=-1).astype(jnp.bfloat16)
    grad_normed = jnp.dot(grad_qkv_low, w_qkv.T, preferred_element_type=jnp.float32)
    grad_in_norm, grad_gain_one = rms_backward(
        grad_normed, saved["unit_one"], saved["inverse_one"], gain_attn
    )
    grad_hidden = grad_middle + grad_in_norm
    pairs = (
        saved["normed_low"],
        grad_qkv_low,
        saved["attended_low"],
        grad_branch_low,
        saved["normed_two_low"],
        grad_mix_low,
        saved["units_low"],
        grad_low,
        grad_gain_one,
        grad_gain_two,
    )
    return (grad_hidden, pairs)


def weight_terms(pairs):
    (
        normed_low,
        grad_qkv_low,
        attended_low,
        grad_branch_low,
        normed_two_low,
        grad_mix_low,
        units_low,
        grad_low,
        grad_gain_one,
        grad_gain_two,
    ) = pairs
    return (
        jnp.dot(normed_low.T, grad_qkv_low, preferred_element_type=jnp.float32),
        jnp.dot(attended_low.T, grad_branch_low, preferred_element_type=jnp.float32),
        jnp.dot(normed_two_low.T, grad_mix_low, preferred_element_type=jnp.float32),
        jnp.dot(units_low.T, grad_low, preferred_element_type=jnp.float32),
        jnp.stack([grad_gain_one, grad_gain_two]),
    )


def on_device_general(x_in, cotangent, w_qkv, w_out, w_gate_up, w_down, gains, order, visible, seq_ids):
    section = lax.axis_index("section")
    column = lax.axis_index("ctx")
    n_ctx = lax.axis_size("ctx")
    batches = x_in.shape[0]
    rows = x_in.shape[2]
    per_stretch = stretch_width(rows, n_ctx)
    first_section = section == 0
    weights = (
        lax.all_gather(w_qkv[0], "wsh", axis=0, tiled=True),
        lax.all_gather(w_out[0], "wsh", axis=1, tiled=True),
        lax.all_gather(w_gate_up[0], "wsh", axis=0, tiled=True),
        lax.all_gather(w_down[0], "wsh", axis=1, tiled=True),
        lax.all_gather(gains[0], "wsh", axis=1, tiled=True),
    )
    incoming = jnp.zeros((rows, D), jnp.bfloat16)
    section_inputs = []
    section_outputs = []
    for tick_now in range(batches + 1):
        batch_index = jnp.clip(tick_now - section, 0, batches - 1)
        info, positions = tables(order, visible, seq_ids, batch_index, column, rows, n_ctx)
        source = jnp.where(first_section, x_in[batch_index, 0], incoming)
        result, unused = layer_forward(
            source.astype(jnp.float32), weights, info, positions, per_stretch, rows
        )
        result_low = result.astype(jnp.bfloat16)
        section_inputs.append(source)
        section_outputs.append(result_low)
        if tick_now < batches:
            incoming = shifted(result_low, "section", 1)
    activations = jnp.stack(
        [
            jnp.where(first_section, section_outputs[batch], section_outputs[batch + 1])
            for batch in range(batches)
        ]
    )
    back_weights = (
        lax.all_gather(w_qkv[0], "wsh", axis=0, tiled=True),
        lax.all_gather(w_out[0], "wsh", axis=1, tiled=True),
        lax.all_gather(w_gate_up[0], "wsh", axis=0, tiled=True),
        lax.all_gather(w_down[0], "wsh", axis=1, tiled=True),
        lax.all_gather(gains[0], "wsh", axis=1, tiled=True),
    )
    returned = jnp.zeros((rows, D), jnp.bfloat16)
    grad_list = []
    totals = None
    for tick_now in range(batches + 1):
        raw_index = tick_now - 1 + section
        valid = (raw_index >= 0) & (raw_index < batches)
        batch_index = jnp.clip(raw_index, 0, batches - 1)
        info, positions = tables(order, visible, seq_ids, batch_index, column, rows, n_ctx)
        source = jnp.where(
            first_section,
            section_inputs[max(tick_now - 1, 0)],
            section_inputs[min(tick_now + 1, batches)],
        )
        unused, saved = layer_forward(
            source.astype(jnp.float32), back_weights, info, positions, per_stretch, rows
        )
        grad_rows = jnp.where(first_section, returned, cotangent[batch_index, 0]).astype(
            jnp.float32
        ) * valid.astype(jnp.float32)
        grad_hidden, pairs = layer_backward(grad_rows, back_weights, saved, info, per_stretch, rows)
        grad_hidden_low = grad_hidden.astype(jnp.bfloat16)
        grad_list.append((grad_hidden, grad_hidden_low))
        if tick_now < batches:
            returned = shifted(grad_hidden_low, "section", -1)
        terms = weight_terms(pairs)
        totals = terms if totals is None else jax.tree.map(jnp.add, totals, terms)
    input_grads = jnp.stack(
        [
            jnp.where(
                first_section, grad_list[batch + 1][0], grad_list[batch][1].astype(jnp.float32)
            )
            for batch in range(batches)
        ]
    )
    term_qkv, term_out, term_gate_up, term_down, term_gains = totals
    shares = (
        lax.psum_scatter(term_qkv, ("ctx", "wsh"), scatter_dimension=0, tiled=True),
        lax.psum_scatter(term_out, ("ctx", "wsh"), scatter_dimension=1, tiled=True),
        lax.psum_scatter(term_gate_up, ("ctx", "wsh"), scatter_dimension=0, tiled=True),
        lax.psum_scatter(term_down, ("ctx", "wsh"), scatter_dimension=1, tiled=True),
        lax.psum_scatter(term_gains, ("ctx", "wsh"), scatter_dimension=1, tiled=True),
    )
    return (
        activations[None, :, None],
        input_grads[None, :, None],
        shares[0][None],
        shares[1][None],
        shares[2][None],
        shares[3][None],
        shares[4][None],
    )


GROUP = H // KV
QD = H * HD
KD = KV * HD
QKV = QD + 2 * KD
SIDE = 128
LOW = jnp.bfloat16


def fits_pairs(mesh):
    return mesh.shape[SECTION] == 2 and mesh.shape[CTX] == 4 and mesh.shape[WSH] == 4


def contract(left, right, left_dim, right_dim):
    return lax.dot_general(
        left,
        right,
        (((left_dim,), (right_dim,)), ((), ())),
        preferred_element_type=jnp.float32,
    )


def swap(value, axis, bit):
    return lax.ppermute(value, axis, [(i, i ^ bit) for i in range(lax.axis_size(axis))])


def after(value, *others):
    return lax.optimization_barrier((value, *others))[0]


def masked_pair(first, second):
    return jnp.concatenate([first, second], axis=0)


def attend(queries, masks, keys_of, values_of, key_mask_of, first, last, slot_of):
    rows = masks.shape[1]
    query = masked_pair(
        jnp.concatenate(queries, axis=1), jnp.concatenate([masks] * GROUP, axis=1)
    )

    def step(i, state):
        high, acc = state
        slot = slot_of(i)
        value_t = values_of(slot)
        ones = jnp.ones((1, value_t.shape[1]), jnp.float32)
        ones = jnp.concatenate([ones, jnp.zeros((15, value_t.shape[1]), jnp.float32)], axis=0)
        scores = contract(masked_pair(keys_of(slot), key_mask_of(slot)), query, 0, 0)
        top = jnp.maximum(high, jnp.max(scores, axis=0, keepdims=True))
        terms = jnp.exp(scores - top).astype(LOW)
        fresh = contract(masked_pair(value_t, ones.astype(LOW)), terms, 1, 0)
        return top, acc * jnp.exp(high - top) + fresh

    start = (
        jnp.full((1, GROUP * rows), NEG, jnp.float32),
        jnp.zeros((HD + 16, GROUP * rows), jnp.float32),
    )
    high, acc = lax.fori_loop(first, last, step, start)
    total = acc[HD : HD + 1]
    out = (acc[:HD] / total).astype(LOW)
    log_total = high + jnp.log(total)
    cuts = [slice(j * rows, (j + 1) * rows) for j in range(GROUP)]
    return [out[:, c] for c in cuts], [log_total[:, c] for c in cuts]


def forward_kernel(live_ref, q_ref, k_ref, v_ref, key_mask_ref, mask_ref, o_ref, lse_ref):
    out, log_total = attend(
        [q_ref[pl.ds(j * HD, HD), :] for j in range(GROUP)],
        mask_ref[...],
        lambda slot: k_ref[slot, 0],
        lambda slot: v_ref[slot, 0],
        lambda slot: key_mask_ref[slot],
        0,
        live_ref[0],
        lambda i: live_ref[1 + i],
    )
    for j in range(GROUP):
        o_ref[pl.ds(j * HD, HD), :] = out[j]
        lse_ref[0, pl.ds(j, 1), :] = log_total[j]


def backward_kernel(
    live_ref,
    q_ref,
    do_ref,
    o_ref,
    lse_ref,
    k_ref,
    v_ref,
    key_mask_ref,
    mask_ref,
    dq_ref,
    dk_ref,
    dv_ref,
    acc_ref,
):
    rows = q_ref.shape[1]
    acc_ref[...] = jnp.zeros_like(acc_ref)
    dk_ref[...] = jnp.zeros_like(dk_ref)
    dv_ref[...] = jnp.zeros_like(dv_ref)
    parts = [pl.ds(j * HD, HD) for j in range(GROUP)]
    query_t = jnp.concatenate([q_ref[part, :] for part in parts], axis=1)
    grad_t = jnp.concatenate([do_ref[part, :] for part in parts], axis=1)
    out_t = jnp.concatenate([o_ref[part, :] for part in parts], axis=1)
    log_total = jnp.concatenate([lse_ref[0, pl.ds(j, 1), :] for j in range(GROUP)], axis=1)
    both = grad_t.astype(jnp.float32) * out_t.astype(jnp.float32)
    delta = jnp.sum(both, axis=0, keepdims=True)
    query = masked_pair(query_t, jnp.concatenate([mask_ref[...]] * GROUP, axis=1))

    def step(i, carry):
        slot = live_ref[1 + i]
        key_t = k_ref[slot, 0]
        scores = contract(masked_pair(key_t, key_mask_ref[slot]), query, 0, 0)
        probs = jnp.exp(scores - log_total)
        grad_probs = contract(v_ref[slot, 0], grad_t, 0, 0)
        grad_scores = (probs * (grad_probs - delta)).astype(LOW)
        grad_v = contract(probs.astype(LOW), grad_t, 1, 1)
        grad_k = contract(grad_scores, query_t, 1, 1)
        acc_ref[...] += contract(key_t, grad_scores, 1, 0)
        dk_ref[slot, 0] = jnp.transpose(grad_k).astype(LOW)
        dv_ref[slot, 0] = jnp.transpose(grad_v).astype(LOW)
        return carry

    lax.fori_loop(0, live_ref[0], step, 0)
    for j in range(GROUP):
        cut = slice(j * rows, (j + 1) * rows)
        dq_ref[parts[j], :] = acc_ref[:, cut] * HD ** (-0.5)


def long_cost(microseconds):
    return pl.CostEstimate(
        flops=microseconds * 10**9, bytes_accessed=2**20, transcendentals=0
    )


def kernel_cost(scores, matmuls):
    return pl.CostEstimate(
        flops=scores * matmuls * HD * 2 * 4, bytes_accessed=12 * 2**20, transcendentals=scores
    )


def pair_attention_forward(info, q_t, kv_t):
    live, key_masks, masks = info
    slots, keys = kv_t.shape[0], kv_t.shape[3]
    rows = q_t.shape[1]
    return pl.pallas_call(
        forward_kernel,
        grid_spec=pltpu.PrefetchScalarGridSpec(
            num_scalar_prefetch=1,
            grid=(KV,),
            in_specs=[
                pl.BlockSpec((GROUP * HD, rows), lambda g, l: (g, 0)),
                pl.BlockSpec((slots, 1, HD, keys), lambda g, l: (0, g, 0, 0)),
                pl.BlockSpec((slots, 1, HD, keys), lambda g, l: (0, KV + g, 0, 0)),
                pl.BlockSpec((slots, 16, keys), lambda g, l: (0, 0, 0)),
                pl.BlockSpec((16, rows), lambda g, l: (0, 0)),
            ],
            out_specs=[
                pl.BlockSpec((GROUP * HD, rows), lambda g, l: (g, 0)),
                pl.BlockSpec((1, GROUP, rows), lambda g, l: (g, 0, 0)),
            ],
        ),
        out_shape=[
            jax.ShapeDtypeStruct(q_t.shape, LOW),
            jax.ShapeDtypeStruct((KV, GROUP, rows), jnp.float32),
        ],
        compiler_params=pltpu.CompilerParams(vmem_limit_bytes=62 * 2**20),
        cost_estimate=kernel_cost(H * rows * slots * keys, 2),
    )(live, q_t, kv_t, kv_t, key_masks, masks)


def pair_attention_backward(info, q_t, do_t, o_t, lse, kv_t):
    live, key_masks, masks = info
    slots, keys = kv_t.shape[0], kv_t.shape[3]
    rows = q_t.shape[1]
    q_spec = pl.BlockSpec((GROUP * HD, rows), lambda g, l: (g, 0))
    part_spec = pl.BlockSpec((slots, 1, HD, keys), lambda g, l: (0, g, 0, 0))
    part_shape = jax.ShapeDtypeStruct((slots, KV, HD, keys), LOW)
    return pl.pallas_call(
        backward_kernel,
        grid_spec=pltpu.PrefetchScalarGridSpec(
            num_scalar_prefetch=1,
            grid=(KV,),
            in_specs=[
                q_spec,
                q_spec,
                q_spec,
                pl.BlockSpec((1, GROUP, rows), lambda g, l: (g, 0, 0)),
                part_spec,
                pl.BlockSpec((slots, 1, HD, keys), lambda g, l: (0, KV + g, 0, 0)),
                pl.BlockSpec((slots, 16, keys), lambda g, l: (0, 0, 0)),
                pl.BlockSpec((16, rows), lambda g, l: (0, 0)),
            ],
            out_specs=[q_spec, part_spec, part_spec],
            scratch_shapes=[pltpu.VMEM((HD, GROUP * rows), jnp.float32)],
        ),
        out_shape=[jax.ShapeDtypeStruct(q_t.shape, jnp.float32), part_shape, part_shape],
        compiler_params=pltpu.CompilerParams(vmem_limit_bytes=62 * 2**20),
        cost_estimate=kernel_cost(H * rows * slots * keys, 5),
    )(live, q_t, do_t, o_t, lse, kv_t, kv_t, key_masks, masks)


def turn(heads, cosine, sine):
    half = HD // 2
    first, second = heads[:, :half], heads[:, half:]
    return jnp.concatenate(
        [first * cosine - second * sine, first * sine + second * cosine], axis=1
    )


def pair_angles(own_block, rows):
    positions = own_block * rows + jnp.arange(rows, dtype=jnp.int32)
    frequency = 10000.0 ** (-(jnp.arange(HD // 2, dtype=jnp.float32) * 2.0 / HD))
    angles = frequency[:, None] * positions.astype(jnp.float32)[None, :]
    return jnp.cos(angles), jnp.sin(angles)


MESH_ID = pl.DeviceIdType.MESH


def stream_partner(column, place):
    core = place % 2
    moving = (column < 2) == (core == 1)
    return moving, lax.rem(column + 2, 4), place + 1 - 2 * core


def first_kernel(*refs):
    x_ref, shard_refs = refs[0], refs[1:5]
    seq_all_ref, cos_ref, sin_ref, order_ref, visible_ref = refs[5:10]
    full_refs = refs[10:15]
    (
        hidden_ref,
        q_ref,
        kv_out,
        o_ref,
        lse_ref,
        result_ref,
        middle_ref,
        lhs_out,
        attended_out,
        units_out,
        gate_out,
        up_out,
        stream_ref,
        gains_ref,
        next_q_ref,
        next_kv_out,
        natural_out_ref,
        key_mask_out,
        mask_out,
        live_ref,
        natural_ref,
    ) = refs[15:36]
    (
        send_sem,
        recv_sem,
        store_sem,
        hold_sem,
        local_sem,
        ring_ref,
        rows_ref,
        w_in_ref,
        w_out_ref,
        w_mlp_ref,
        w_down_ref,
        units_ref,
        gate_ref,
        up_ref,
        normed_ref,
        turned_ref,
        attended_ref,
        acc_ref,
        kv_ref,
        seq_peer_ref,
        key_mask_ref,
        mask_ref,
        gain_ref,
        next_kv_ref,
        seq_ref,
    ) = refs[36:]
    section = lax.axis_index(SECTION)
    column = lax.axis_index(CTX)
    place = lax.axis_index(WSH)
    half = lax.rem(column, 2)
    core = lax.rem(place, 2)
    other = 1 - section
    over_x = (section, column, lax.rem(place + 2, 4))
    over_y = (other, column, place)
    over_z = (section, column + 1 - 2 * half, place)
    over_core = (section, column, place + 1 - 2 * core)
    moving, partner_column, partner_place = stream_partner(column, place)
    partner = (section, partner_column, partner_place)

    barrier = pltpu.get_barrier_semaphore()
    for target in (over_x, over_y, over_z, over_core):
        pl.semaphore_signal(barrier, inc=1, device_id=target, device_id_type=MESH_ID)

    @pl.when(moving)
    def _():
        pl.semaphore_signal(barrier, inc=1, device_id=partner, device_id_type=MESH_ID)
        pl.semaphore_wait(barrier, 5)

    @pl.when(jnp.logical_not(moving))
    def _():
        pl.semaphore_wait(barrier, 4)

    seq_ref[...] = seq_all_ref[section].astype(jnp.float32)
    in_shard, out_shard, gate_up_shard, down_shard = shard_refs
    sources = [
        (in_shard, 0, full_refs[0], 1024),
        (out_shard, 0, full_refs[1], QD),
        (gate_up_shard, 0, full_refs[2], WIDE),
        (gate_up_shard, FF, full_refs[3], WIDE),
        (down_shard, 0, full_refs[4], WIDE),
    ]
    pieces = []
    for shard_ref, offset, full_ref, step in sources:
        for first in range(0, full_ref.shape[2], step):
            pieces.append((shard_ref, offset + first, full_ref, first, step))
    count = len(pieces)
    direct = (13, 14)
    quarter = in_shard.shape[0]
    mid = quarter // 2
    rows = hidden_ref.shape[0]

    def own(k):
        shard_ref, offset, full_ref, first, step = pieces[k]
        return shard_ref.at[:, pl.ds(offset, step)]

    def own_half(k):
        shard_ref, offset, full_ref, first, step = pieces[k]
        return shard_ref.at[pl.ds(half * mid, mid), pl.ds(offset, step)]

    def full(k, layer, block):
        shard_ref, offset, full_ref, first, step = pieces[k]
        return full_ref.at[layer, pl.ds(block * quarter, quarter), pl.ds(first, step)]

    def full_half(k, layer, block, which):
        shard_ref, offset, full_ref, first, step = pieces[k]
        span = pl.ds(block * quarter + which * mid, mid)
        return full_ref.at[layer, span, pl.ds(first, step)]

    started = {}
    arrived = set()

    def remote(kind, k, source, target, device):
        return pltpu.make_async_remote_copy(
            src_ref=source,
            dst_ref=target,
            send_sem=send_sem.at[kind, k],
            recv_sem=recv_sem.at[kind, k],
            device_id=device,
            device_id_type=MESH_ID,
        )

    def send(kind, k, source, target, device):
        copy = remote(kind, k, source, target, device)
        copy.start()
        started[kind, k] = copy

    def receive(kind, k):
        if (kind, k) not in arrived:
            arrived.add((kind, k))
            started[kind, k].wait_recv()

    def start_near(k):
        if k < count:
            send(0, k, own(k), full(k, section, 2), over_x)

    def start_cross(k):
        if k in direct:
            send(1, k, own(k), full(k, section, 0), over_y)
        elif k < count:
            send(1, k, own_half(k), full_half(k, section, 0, half), over_y)

    def ring(k):
        return ring_ref.at[k % 2, :, pl.ds(0, pieces[k][4])]

    def hold(k):
        return pltpu.make_async_copy(own(k), ring(k), hold_sem.at[k % 2])

    def store(k):
        return pltpu.make_async_copy(ring(k), full(k, section, 0), store_sem.at[k])

    stored_pieces = set()

    def need(k):
        for kind in range(5, 10 if k in direct else 11):
            receive(kind, k)
        if k not in stored_pieces:
            stored_pieces.add(k)
            store(k).wait()

    local_copies = {}

    def begin(name, source, target):
        copy = pltpu.make_async_copy(source, target, local_sem.at[len(local_copies)])
        local_copies[name] = copy
        copy.start()

    def finish(name):
        local_copies[name].wait()

    row_source = x_ref.at[section, 0]
    row_move = remote(11, 0, row_source, rows_ref, partner)
    row_copy = pltpu.make_async_copy(row_source, rows_ref, hold_sem.at[2])

    def move_rows():
        @pl.when(moving)
        def _():
            row_move.wait()

        @pl.when(jnp.logical_not(moving))
        def _():
            row_copy.wait()

        share = quarter // 4
        index = lax.broadcasted_iota(jnp.int32, (D, 1), 0)
        block, inner = index // quarter, index % quarter
        to_core, to_side = inner // (2 * share), inner % (2 * share) // share
        index = (block ^ place) * quarter + (2 * to_side + to_core) * share + inner % share
        lane = lax.broadcasted_iota(jnp.int32, (D, D), 1)
        natural_ref[...] = jnp.where(index == lane, 1.0, 0.0).astype(LOW)
        hidden_ref[...] = contract(rows_ref[...], natural_ref[...], 1, 1).astype(LOW)

    def make_masks():
        receive(11, 1)
        own_stream = jnp.broadcast_to(core == column // 2, seq_ref.shape)
        stream_ref[...] = jnp.where(own_stream, seq_ref[...], seq_peer_ref[...])
        slot = half + 2 * core
        own_block = order_ref[section, slot]
        alive, spans = [], []
        for p, step in enumerate((0, 2, 1, 3)):
            at = slot ^ step
            span = pl.ds(pl.multiple_of(at * rows, rows), rows)
            ids = stream_ref[:, span]
            seen = visible_ref[own_block, order_ref[section, at]].astype(jnp.float32)
            unseen = jnp.full((1, rows), 1.0, jnp.float32) * (1.0 - seen)
            blank = jnp.zeros((13, rows), jnp.float32)
            key_mask = jnp.concatenate([ids, 1.0 - ids, unseen, blank], axis=0) * NEG
            key_mask_ref[p] = key_mask.astype(LOW)
            spans.append((jnp.min(ids), jnp.max(ids)))
            if p == 0:
                ones = jnp.ones((1, rows), jnp.float32)
                mask_ref[...] = jnp.concatenate([1.0 - ids, ids, ones, blank], axis=0).astype(LOW)
                alive.append(jnp.int32(1))
            else:
                shared = (spans[p][0] <= spans[0][1]) & (spans[0][0] <= spans[p][1])
                alive.append(jnp.where(shared & (seen > 0.5), 1, 0).astype(jnp.int32))
        key_mask_out[...] = key_mask_ref[...]
        mask_out[...] = mask_ref[...]
        found = [sum(alive[:p], jnp.int32(0)) for p in range(5)]
        live_ref[0] = found[4]
        for j in range(4):
            live_ref[1 + j] = sum(
                (jnp.where((alive[p] == 1) & (found[p] == j), p, 0) for p in range(1, 4)),
                jnp.int32(0),
            )

    def load_in(layer):
        need(0)
        need(1)
        begin((0, layer), full_refs[0].at[layer], w_in_ref)

    def make_keys(layer, source_ref, keys_ref, first):
        if layer == 0:
            finish((0, 0))
            gain_ref[0] = w_in_ref[:, pl.ds(QKV, SIDE)].astype(jnp.float32).T[:8]
        else:
            finish((1, 0))
        unit_rows, unused = norm_parts(source_ref[...].astype(jnp.float32))
        normed = (unit_rows * gain_ref[layer, :1]).astype(LOW)
        normed_ref[...] = normed
        turned_ref[1] = normed.T
        begin((1, layer), turned_ref.at[1], lhs_out.at[layer, 3])
        for part in range(2):
            cut = pl.ds(QD + part * KD, KD)
            heads = jnp.dot(normed, w_in_ref[:, cut], preferred_element_type=jnp.float32).T
            heads = heads.reshape(KV, HD, rows)
            if part == 0:
                heads = turn(heads, cos_ref[...], sin_ref[...])
            keys_ref[0, pl.ds(part * KV, KV)] = heads.astype(LOW)
        send(11, first, keys_ref.at[0], keys_ref.at[2], over_z)
        send(11, first + 1, keys_ref.at[0], keys_ref.at[1], over_core)

    def make_queries(target_ref):
        normed = normed_ref[...]
        for part in range(QD // KD):
            heads = jnp.dot(
                normed, w_in_ref[:, pl.ds(part * KD, KD)], preferred_element_type=jnp.float32
            ).T
            turned = turn(heads.reshape(KV, HD, rows), cos_ref[...], sin_ref[...])
            turned = turned.astype(LOW).astype(jnp.float32) * HD ** (-0.5)
            target_ref[pl.ds(part * KD, KD), :] = turned.astype(LOW).reshape(KD, rows)

    def take_keys(layer, keys_ref, keys_out, first):
        receive(11, first)
        send(11, first + 2, keys_ref.at[2], keys_ref.at[3], over_core)
        receive(11, first + 1)
        receive(11, first + 2)
        begin((2, layer), keys_ref, keys_out)

    def attention(first, last):
        def one(g, carry):
            spans = [
                pl.ds(pl.multiple_of(g * GROUP * HD + j * HD, HD), HD) for j in range(GROUP)
            ]
            out, log_total = attend(
                [q_ref[span, :] for span in spans],
                mask_ref[...],
                lambda slot: kv_ref[slot, g],
                lambda slot: kv_ref[slot, KV + g],
                lambda slot: key_mask_ref[slot],
                0,
                4,
                lambda i: i,
            )
            for j in range(GROUP):
                o_ref[spans[j], :] = out[j]
            lse_ref[g] = jnp.concatenate(log_total, axis=0)
            return carry

        lax.fori_loop(first, last, one, 0)

    def load_out():
        need(2)
        begin((3, 0), full_refs[1].at[0], w_out_ref)

    def make_middle():
        attended = o_ref[...].T
        for t in range(QD // TILE):
            attended_ref[t] = attended[:, t * TILE : (t + 1) * TILE]
        begin((4, 0), attended_ref, attended_out.at[0])
        finish((3, 0))
        added = jnp.dot(w_out_ref[...], o_ref[...], preferred_element_type=jnp.float32)
        middle = hidden_ref[...].astype(jnp.float32) + added.T
        middle_ref[...] = middle
        acc_ref[...] = jnp.zeros_like(acc_ref)
        unit_rows, unused = norm_parts(middle)
        normed = (unit_rows * gain_ref[0, 1:2]).astype(LOW)
        normed_ref[...] = normed
        turned_ref[0] = normed.T
        begin((5, 0), turned_ref.at[0], lhs_out.at[0, 2])

    per = WIDE // TILE

    def load_mlp(t):
        need(3 + t)
        need(7 + t)
        span = pl.ds(t * WIDE, WIDE)
        begin((6, t), full_refs[2].at[0, :, span], w_mlp_ref.at[t % 2, 0])
        begin((7, t), full_refs[3].at[0, :, span], w_mlp_ref.at[t % 2, 1])

    def make_units(t):
        finish((6, t))
        finish((7, t))
        normed = normed_ref[...]
        gate = jnp.dot(normed, w_mlp_ref[t % 2, 0], preferred_element_type=jnp.float32)
        up = jnp.dot(normed, w_mlp_ref[t % 2, 1], preferred_element_type=jnp.float32)
        units = (gate * sigmoid_of(gate) * up).astype(LOW)
        gate_low, up_low = gate.astype(LOW), up.astype(LOW)
        for i in range(per):
            cut = slice(i * TILE, (i + 1) * TILE)
            gate_ref[per * t + i] = gate_low[:, cut]
            up_ref[per * t + i] = up_low[:, cut]
            units_ref[per * t + i] = units[:, cut]
        span = pl.ds(per * t, per)
        begin((8, t), units_ref.at[span], units_out.at[0, span])
        begin((9, t), gate_ref.at[span], gate_out.at[span])
        begin((10, t), up_ref.at[span], up_out.at[span])

    def load_down(t):
        need(11 + t)
        span = pl.ds(t * WIDE, WIDE)
        begin((11, t), full_refs[4].at[0, :, span], w_down_ref.at[t % 2])

    def add_down(t):
        finish((11, t))
        units = jnp.concatenate([units_ref[per * t + i] for i in range(per)], axis=1)
        acc_ref[...] += jnp.dot(w_down_ref[t % 2], units.T, preferred_element_type=jnp.float32)

    def make_late_gains():
        finish((0, 1))
        gain_ref[1] = w_in_ref[:, pl.ds(QKV, SIDE)].astype(jnp.float32).T[:8]
        gains_ref[...] = gain_ref[...]

    tasks = {
        1: [make_masks],
        2: [move_rows],
        3: [lambda: load_in(0)],
        4: [lambda: make_keys(0, hidden_ref, kv_ref, 2), lambda: make_queries(q_ref)],
        6: [lambda: take_keys(0, kv_ref, kv_out, 2), lambda: attention(0, 1), load_out],
        7: [lambda: attention(1, 2)],
        8: [lambda: attention(2, 3)],
        9: [lambda: attention(3, 4)],
        10: [lambda: attention(4, 5)],
        11: [lambda: attention(5, 6), make_middle, lambda: load_mlp(0), lambda: load_in(1)],
        12: [lambda: load_mlp(1), lambda: make_units(0), make_late_gains],
        13: [lambda: load_mlp(2), lambda: make_units(1)],
        14: [lambda: load_mlp(3), lambda: make_units(2), lambda: load_down(0)],
        15: [lambda: make_units(3)],
        16: [lambda: load_down(1), lambda: add_down(0), lambda: load_down(2), lambda: add_down(1)],
    }

    ahead = 3
    for k in range(ahead):
        start_near(k)
        start_cross(k)

    @pl.when(moving)
    def _():
        row_move.start()

    @pl.when(jnp.logical_not(moving))
    def _():
        row_copy.start()

    send(11, 1, seq_ref, seq_peer_ref, over_core)
    hold(0).start()
    for k in range(count):
        send(5, k, own(k), full(k, section, 1), over_core)

    for k in range(count + 2):
        if k < count:
            hold(k).wait()
            store(k).start()
            if k + 1 < count:
                if k >= 1 and k - 1 not in stored_pieces:
                    stored_pieces.add(k - 1)
                    store(k - 1).wait()
                hold(k + 1).start()
            receive(0, k)
            send(6, k, full(k, section, 2), full(k, section, 3), over_core)
            which = 1 if k in direct else half
            mine = full_half(k, section, 2, which)
            send(2, k, mine, mine, over_y)
            start_near(k + ahead)
            receive(1, k)
            if k in direct:
                send(3, k, full_half(k, other, 0, 0), full_half(k, other, 2, 0), over_x)
                send(7, k, full(k, other, 0), full(k, other, 1), over_core)
            else:
                crossed = full_half(k, other, 0, half)
                send(3, k, crossed, crossed, over_z)
                send(7, k, crossed, full_half(k, other, 1, half), over_core)
            start_cross(k + ahead)
        j = k - 1
        if 0 <= j < count:
            receive(2, j)
            if j in direct:
                send(8, j, full_half(j, other, 2, 1), full_half(j, other, 3, 1), over_core)
                receive(3, j)
                send(9, j, full_half(j, other, 2, 0), full_half(j, other, 3, 0), over_core)
            else:
                crossed = full_half(j, other, 2, half)
                send(4, j, crossed, crossed, over_z)
                send(8, j, crossed, full_half(j, other, 3, half), over_core)
                receive(3, j)
                passed = full_half(j, other, 0, 1 - half)
                send(9, j, passed, full_half(j, other, 1, 1 - half), over_core)
        j = k - 2
        if 0 <= j < count and j not in direct:
            receive(4, j)
            passed = full_half(j, other, 2, 1 - half)
            send(10, j, passed, full_half(j, other, 3, 1 - half), over_core)
        for task in tasks.get(k, []):
            task()
    load_down(3)
    add_down(2)
    add_down(3)
    result_ref[...] = (middle_ref[...] + acc_ref[...].T).astype(LOW)
    make_keys(1, result_ref, next_kv_ref, 5)
    make_queries(next_q_ref)
    turned = jnp.dot(result_ref[...], natural_ref[...], preferred_element_type=jnp.float32)
    natural_out_ref[...] = turned.astype(LOW)
    for k in range(count):
        need(k)
    take_keys(1, next_kv_ref, next_kv_out, 5)
    for copy in started.values():
        copy.wait_send()
    for name in ((1, 1), (2, 0), (2, 1), (4, 0), (5, 0)):
        finish(name)
    for t in range(FF // WIDE):
        for name in (8, 9, 10):
            finish((name, t))


def first_layer(x_in, shards, seq_ids, angles, order, visible):
    rows = x_in.shape[2]
    quarter = shards[0].shape[0]
    widths = [shards[0].shape[1], QD, FF, FF, FF]
    pieces = 15
    tiles, head_tiles = FF // TILE, QD // TILE
    in_vmem = pl.BlockSpec(memory_space=pltpu.VMEM)
    in_smem = pl.BlockSpec(memory_space=pltpu.SMEM)

    def low(*shape):
        return jax.ShapeDtypeStruct(shape, LOW)

    def wide(*shape):
        return jax.ShapeDtypeStruct(shape, jnp.float32)

    dma = pltpu.SemaphoreType.DMA
    outs = pl.pallas_call(
        first_kernel,
        out_shape=[low(2, 4 * quarter, w) for w in widths]
        + [
            low(rows, D),
            low(QD, rows),
            low(4, 2 * KV, HD, rows),
            low(QD, rows),
            wide(KV, GROUP, rows),
            low(rows, D),
            wide(rows, D),
            low(2, 5, D, rows),
            low(2, head_tiles, rows, TILE),
            low(2, tiles, rows, TILE),
            low(tiles, rows, TILE),
            low(tiles, rows, TILE),
            wide(*seq_ids.shape[1:]),
            wide(2, 8, D),
            low(QD, rows),
            low(4, 2 * KV, HD, rows),
            low(rows, D),
            low(4, 16, rows),
            low(16, rows),
            jax.ShapeDtypeStruct((8,), jnp.int32),
            low(D, D),
        ],
        in_specs=[ANYWHERE] * 5 + [in_vmem] * 3 + [in_smem] * 2,
        out_specs=[ANYWHERE] * 5
        + [in_vmem, in_vmem, ANYWHERE, in_vmem, in_vmem, in_vmem, in_vmem]
        + [ANYWHERE] * 5
        + [in_vmem, in_vmem, in_vmem, ANYWHERE, in_vmem, in_vmem, in_vmem, in_smem, in_vmem],
        scratch_shapes=[
            dma((12, pieces)),
            dma((12, pieces)),
            dma((pieces,)),
            dma((3,)),
            dma((40,)),
            pltpu.VMEM((2, quarter, QD), LOW),
            pltpu.VMEM((rows, D), LOW),
            pltpu.VMEM((D, widths[0]), LOW),
            pltpu.VMEM((D, QD), LOW),
            pltpu.VMEM((2, 2, D, WIDE), LOW),
            pltpu.VMEM((2, D, WIDE), LOW),
            pltpu.VMEM((tiles, rows, TILE), LOW),
            pltpu.VMEM((tiles, rows, TILE), LOW),
            pltpu.VMEM((tiles, rows, TILE), LOW),
            pltpu.VMEM((rows, D), LOW),
            pltpu.VMEM((2, D, rows), LOW),
            pltpu.VMEM((head_tiles, rows, TILE), LOW),
            pltpu.VMEM((D, rows), jnp.float32),
            pltpu.VMEM((4, 2 * KV, HD, rows), LOW),
            pltpu.VMEM(seq_ids.shape[1:], jnp.float32),
            pltpu.VMEM((4, 16, rows), LOW),
            pltpu.VMEM((16, rows), LOW),
            pltpu.VMEM((2, 8, D), jnp.float32),
            pltpu.VMEM((4, 2 * KV, HD, rows), LOW),
            pltpu.VMEM(seq_ids.shape[1:], jnp.float32),
        ],
        compiler_params=pltpu.CompilerParams(
            collective_id=1, has_side_effects=True, vmem_limit_bytes=62 * 2**20
        ),
        cost_estimate=long_cost(230),
    )(x_in, *shards, seq_ids, *angles, order, visible)
    names = ("hidden", "q_t", "kv_t", "o_t", "lse", "result", "middle")
    saved = dict(zip(names, outs[5:12]))
    saved.update(gate=outs[15], up=outs[16])
    stores = dict(lhs=outs[12], attended=outs[13], units=outs[14])
    ahead = dict(hidden=outs[10], q_t=outs[19], kv_t=outs[20])
    info = (outs[24], outs[22], outs[23])
    return outs[:5], saved, ahead, stores, info, outs[18], outs[21], outs[25]


ANYWHERE = pl.BlockSpec(memory_space=pl.ANY)
WIDE = 768


def whole(shape, *index):
    return pl.BlockSpec(shape, lambda s: index + (0,) * (len(shape) - len(index)))


def sigmoid_of(value):
    return 0.5 * jnp.tanh(0.5 * value) + 0.5


def norm_parts(value):
    inverse = lax.rsqrt(jnp.mean(value * value, axis=-1, keepdims=True) + EPS)
    return value * inverse, inverse


def norm_back(grad_rows, value, gain_row):
    unit_rows, inverse = norm_parts(value)
    grad_unit = grad_rows * gain_row
    grad_gain = jnp.sum(grad_rows * unit_rows, axis=0, keepdims=True)
    inner = jnp.mean(grad_unit * unit_rows, axis=-1, keepdims=True)
    return inverse * (grad_unit - unit_rows * inner), grad_gain


def stored(stores, name, shape):
    return stores.get(name), jax.ShapeDtypeStruct(shape, LOW)


def copies_of(sem, pairs):
    copies = [pltpu.make_async_copy(x, y, sem.at[i]) for i, (x, y) in enumerate(pairs)]
    for copy in copies:
        copy.start()
    return copies


def mlp_forward_kernel(
    h_ref, o_ref, w_out_ref, w_gate_ref, w_up_ref, w_down_ref, gain_ref, *refs
):
    (
        result_ref,
        middle_ref,
        normed_t_ref,
        attended_ref,
        units_ref,
        gate_ref,
        up_ref,
        acc_ref,
        normed_ref,
    ) = refs[-9:]
    step = pl.program_id(0)

    @pl.when(step == 0)
    def _():
        attended = o_ref[...].T
        for t in range(attended_ref.shape[1]):
            attended_ref[0, t] = attended[:, t * TILE : (t + 1) * TILE]
        added = jnp.dot(w_out_ref[0], o_ref[...], preferred_element_type=jnp.float32)
        middle = h_ref[...].astype(jnp.float32) + added.T
        middle_ref[...] = middle
        acc_ref[...] = jnp.zeros_like(acc_ref)
        unit_rows, unused = norm_parts(middle)
        normed = (unit_rows * gain_ref[0, 1:2]).astype(LOW)
        normed_ref[...] = normed
        normed_t_ref[0, 0] = normed.T

    @pl.when(step > 0)
    def _():
        normed = normed_ref[...]
        gate = jnp.dot(normed, w_gate_ref[0], preferred_element_type=jnp.float32)
        up = jnp.dot(normed, w_up_ref[0], preferred_element_type=jnp.float32)
        units = (gate * sigmoid_of(gate) * up).astype(LOW)
        gate_low, up_low = gate.astype(LOW), up.astype(LOW)
        for t in range(WIDE // TILE):
            cut = slice(t * TILE, (t + 1) * TILE)
            gate_ref[t] = gate_low[:, cut]
            up_ref[t] = up_low[:, cut]
            units_ref[0, t] = units[:, cut]
        acc_ref[...] += jnp.dot(w_down_ref[0], units.T, preferred_element_type=jnp.float32)

    @pl.when(step == pl.num_programs(0) - 1)
    def _():
        result_ref[...] = (middle_ref[...] + acc_ref[...].T).astype(LOW)


def call_mlp_forward(layer, hidden, o_t, weights, gain_rows, stores):
    w_in, w_out_t, w_gate, w_up, w_down_t = weights
    rows = hidden.shape[0]
    steps, per = FF // WIDE, WIDE // TILE
    tiles, head_tiles = FF // TILE, QD // TILE
    names = ("lhs", "attended", "units")
    shapes = ((2, 5, D, rows), (2, head_tiles, rows, TILE), (2, tiles, rows, TILE))
    extra, aliases, store_shapes = [], {}, []
    for place, (name, shape) in enumerate(zip(names, shapes)):
        value, shape = stored(stores, name, shape)
        store_shapes.append(shape)
        if value is not None:
            aliases[7 + len(extra)] = 2 + place
            extra.append(value)

    def behind(s):
        return jnp.maximum(s - 1, 0)

    column = pl.BlockSpec((1, D, WIDE), lambda s: (layer, 0, behind(s)))
    kept = pl.BlockSpec((per, rows, TILE), lambda s: (behind(s), 0, 0))
    result, middle, lhs, attended, units, gate, up = pl.pallas_call(
        mlp_forward_kernel,
        grid=(steps + 1,),
        in_specs=[
            whole((rows, D)),
            whole((QD, rows)),
            whole((1, D, QD), layer),
            column,
            column,
            column,
            whole((1, 8, D), layer),
        ]
        + [ANYWHERE] * len(extra),
        out_specs=[
            whole((rows, D)),
            whole((rows, D)),
            whole((1, 1, D, rows), layer, 2),
            whole((1, head_tiles, rows, TILE), layer),
            pl.BlockSpec((1, per, rows, TILE), lambda s: (layer, behind(s), 0, 0)),
            kept,
            kept,
        ],
        out_shape=[
            jax.ShapeDtypeStruct((rows, D), LOW),
            jax.ShapeDtypeStruct((rows, D), jnp.float32),
            *store_shapes,
            jax.ShapeDtypeStruct((tiles, rows, TILE), LOW),
            jax.ShapeDtypeStruct((tiles, rows, TILE), LOW),
        ],
        scratch_shapes=[pltpu.VMEM((D, rows), jnp.float32), pltpu.VMEM((rows, D), LOW)],
        input_output_aliases=aliases,
        compiler_params=pltpu.CompilerParams(vmem_limit_bytes=62 * 2**20),
        cost_estimate=long_cost(25),
    )(hidden, o_t, w_out_t, w_gate, w_up, w_down_t, gain_rows, *extra)
    stores.update(lhs=lhs, attended=attended, units=units)
    return result, middle, gate, up


def pair_forward(layer, saved, weights, gain_rows, info, stores):
    o_t, lse = pair_attention_forward(info, saved["q_t"], saved["kv_t"])
    result, middle, gate, up = call_mlp_forward(
        layer, saved["hidden"], o_t, weights, gain_rows, stores
    )
    return dict(saved, o_t=o_t, lse=lse, middle=middle, gate=gate, up=up, result=result)


def mlp_backward_kernel(
    layer,
    grad_ref,
    gate_ref,
    up_ref,
    w_gate_ref,
    w_up_ref,
    w_down_ref,
    middle_ref,
    gain_ref,
    w_out_ref,
    *refs,
):
    (
        mlp_ref,
        pair_ref,
        grad_middle_ref,
        do_ref,
        gain_grad_ref,
        acc_ref,
        late_middle,
        late_out,
        late_sem,
    ) = refs[-9:]
    step = pl.program_id(0)
    per = gate_ref.shape[0]
    late = [
        pltpu.make_async_copy(middle_ref, late_middle, late_sem.at[0]),
        pltpu.make_async_copy(w_out_ref.at[layer], late_out, late_sem.at[1]),
    ]

    @pl.when(step == 0)
    def _():
        for copy in late:
            copy.start()

    gate = jnp.concatenate([gate_ref[t] for t in range(per)], axis=1).astype(jnp.float32)
    up = jnp.concatenate([up_ref[t] for t in range(per)], axis=1).astype(jnp.float32)
    grad_units = jnp.dot(grad_ref[...], w_down_ref[0], preferred_element_type=jnp.float32)
    sigmoid = sigmoid_of(gate)
    slope = grad_units * sigmoid
    tilted = slope * gate
    grad_gate = (up * (slope + tilted * (1.0 - sigmoid))).astype(LOW)
    grad_up = tilted.astype(LOW)
    for t in range(per):
        cut = slice(t * TILE, (t + 1) * TILE)
        mlp_ref[0, 2 * t] = grad_gate[:, cut]
        mlp_ref[0, 2 * t + 1] = grad_up[:, cut]
    part = jnp.dot(w_gate_ref[0], grad_gate.T, preferred_element_type=jnp.float32)
    part = part + jnp.dot(w_up_ref[0], grad_up.T, preferred_element_type=jnp.float32)

    @pl.when(step == 0)
    def _():
        acc_ref[...] = part
        pair_ref[0, 0] = grad_ref[...].T

    @pl.when(step > 0)
    def _():
        acc_ref[...] += part

    @pl.when(step == pl.num_programs(0) - 1)
    def _():
        for copy in late:
            copy.wait()
        grad_norm, grad_gain = norm_back(acc_ref[...].T, late_middle[...], gain_ref[0, 1:2])
        gain_grad_ref[...] = jnp.broadcast_to(grad_gain, gain_grad_ref.shape)
        grad_middle = grad_ref[...].astype(jnp.float32) + grad_norm
        grad_middle_ref[...] = grad_middle
        grad_branch = grad_middle.astype(LOW)
        pair_ref[0, 1] = grad_branch.T
        grad_attended = jnp.dot(grad_branch, late_out[...], preferred_element_type=jnp.float32)
        do_ref[...] = grad_attended.astype(LOW).T


def call_mlp_backward(layer, grad_low, saved, weights, gain_rows, stores):
    w_in, w_out_t, w_gate, w_up, w_down_t = weights
    rows = grad_low.shape[0]
    steps, per = FF // WIDE, WIDE // TILE
    mlp, mlp_shape = stored(stores, "mlp", (2, 2 * FF // TILE, rows, TILE))
    extra = [stores["lhs"]] if mlp is None else [stores["lhs"], mlp]
    aliases = {9: 1} if mlp is None else {9: 1, 10: 0}
    column = pl.BlockSpec((1, D, WIDE), lambda s: (layer, 0, s))
    kept = pl.BlockSpec((per, rows, TILE), lambda s: (s, 0, 0))
    mlp, lhs, grad_middle, do_t, grad_gain = pl.pallas_call(
        functools.partial(mlp_backward_kernel, layer),
        grid=(steps,),
        in_specs=[
            whole((rows, D)),
            kept,
            kept,
            column,
            column,
            column,
            ANYWHERE,
            whole((1, 8, D), layer),
            ANYWHERE,
        ]
        + [ANYWHERE] * len(extra),
        out_specs=[
            pl.BlockSpec((1, 2 * per, rows, TILE), lambda s: (layer, s, 0, 0)),
            whole((1, 2, D, rows), layer),
            whole((rows, D)),
            whole((QD, rows)),
            whole((8, D)),
        ],
        out_shape=[
            mlp_shape,
            jax.ShapeDtypeStruct(stores["lhs"].shape, LOW),
            jax.ShapeDtypeStruct((rows, D), jnp.float32),
            jax.ShapeDtypeStruct((QD, rows), LOW),
            jax.ShapeDtypeStruct((8, D), jnp.float32),
        ],
        scratch_shapes=[
            pltpu.VMEM((D, rows), jnp.float32),
            pltpu.VMEM((rows, D), jnp.float32),
            pltpu.VMEM((D, QD), LOW),
            pltpu.SemaphoreType.DMA((2,)),
        ],
        input_output_aliases=aliases,
        compiler_params=pltpu.CompilerParams(vmem_limit_bytes=62 * 2**20),
        cost_estimate=long_cost(25),
    )(
        grad_low,
        saved["gate"],
        saved["up"],
        w_gate,
        w_up,
        w_down_t,
        saved["middle"],
        gain_rows,
        w_out_t,
        *extra,
    )
    stores.update(lhs=lhs, mlp=mlp)
    return grad_middle, do_t, grad_gain


def mixed_backward_kernel(
    layer,
    dk_ref,
    dv_ref,
    gain_ref,
    gain_grad_ref,
    cos_ref,
    sin_ref,
    dq_all,
    h_all,
    grad_middle_all,
    natural_all,
    w_all,
    *refs,
):
    if layer == 0:
        outs = len(refs) - 27
        ahead = (refs[outs - 1], refs[outs + 4], *refs[-7:])
        refs = refs[: outs + 4] + refs[outs + 5 : -7]
    (
        mixed_out,
        lhs_out,
        result_ref,
        natural_out_ref,
        w_ref,
        acc_ref,
        tile_ref,
        gains_ref,
        near_ref,
        far_ref,
        passed_ref,
        dq_ref,
        h_ref,
        grad_middle_ref,
        natural_ref,
        send_sem,
        recv_sem,
        local_sem,
        load_sem,
    ) = refs[-19:]
    section = lax.axis_index(SECTION)
    column = lax.axis_index(CTX)
    place = lax.axis_index(WSH)
    over_z = (section, column + 1 - 2 * lax.rem(column, 2), place)
    over_core = (section, column, place + 1 - 2 * lax.rem(place, 2))
    rows = result_ref.shape[0]
    steps = QKV // TILE
    barrier = pltpu.get_barrier_semaphore()
    over_y = (1 - section, column, place)
    targets = (over_z, over_core, over_y) if layer == 0 else (over_z, over_core)
    for target in targets:
        pl.semaphore_signal(barrier, inc=1, device_id=target, device_id_type=MESH_ID)
    pl.semaphore_wait(barrier, len(targets))

    def remote(index, source, target, device):
        copy = pltpu.make_async_remote_copy(
            src_ref=source,
            dst_ref=target,
            send_sem=send_sem.at[index],
            recv_sem=recv_sem.at[index],
            device_id=device,
            device_id_type=MESH_ID,
        )
        copy.start()
        return copy

    crossed = [
        remote(2 * slot + part, source.at[2 * slot + 1], near_ref.at[slot, part], over_core)
        for slot in (1, 0)
        for part, source in enumerate((dk_ref, dv_ref))
    ]
    loads = copies_of(
        load_sem,
        [
            (w_all.at[layer], w_ref),
            (dq_all, dq_ref),
            (h_all, h_ref),
            (grad_middle_all, grad_middle_ref),
            (natural_all, natural_ref),
        ],
    )
    for copy in crossed[:2]:
        copy.wait_recv()
    for part, source in enumerate((dk_ref, dv_ref)):
        both = source[2].astype(jnp.float32) + near_ref[1, part].astype(jnp.float32)
        far_ref[part] = both.astype(LOW)
    passed = [remote(4 + part, far_ref.at[part], passed_ref.at[part], over_z) for part in range(2)]
    if layer == 0:
        finish = first_crossed(refs[0], ahead, section, place, over_core, over_y)
    for copy in loads:
        copy.wait()

    def add(t, grad_t):
        grad_t = grad_t.astype(LOW)
        tile_ref[t] = grad_t.T
        part = jnp.dot(
            w_ref[:, pl.ds(t * TILE, TILE)], grad_t, preferred_element_type=jnp.float32
        )
        if t == 0:
            acc_ref[...] = part
        else:
            acc_ref[...] += part

    def back(heads):
        return turn(heads, cos_ref[...], -sin_ref[...]).reshape(KD, rows)

    for t in range(QD // KD):
        add(t, back(dq_ref[pl.ds(t * KD, KD), :].reshape(KV, HD, rows)))
    row = lax.broadcasted_iota(jnp.int32, (rows, TILE), 0)
    lane = lax.broadcasted_iota(jnp.int32, (rows, TILE), 1)
    tile_ref[steps] = jnp.where(row == lane, 1.0, 0.0).astype(LOW)
    for copy in crossed[2:]:
        copy.wait_recv()
    for part, source in enumerate((dk_ref, dv_ref)):
        passed[part].wait_recv()
        own = source[0].astype(jnp.float32) + near_ref[0, part].astype(jnp.float32)
        own = own + passed_ref[part].astype(jnp.float32)
        add(QD // KD + part, back(own) if part == 0 else own.reshape(KD, rows))
    tiles = pltpu.make_async_copy(tile_ref, mixed_out.at[layer], local_sem.at[1])
    tiles.start()
    grad_norm, grad_gain = norm_back(
        acc_ref[...].T, h_ref[...].astype(jnp.float32), gain_ref[layer, :1]
    )
    both = jnp.concatenate(
        [grad_gain, gain_grad_ref[:1], jnp.zeros((rows - 2, D), jnp.float32)], axis=0
    )
    gains_ref[...] = both.T.astype(LOW)
    gains = pltpu.make_async_copy(gains_ref, lhs_out.at[layer, 4], local_sem.at[2])
    gains.start()
    result = (grad_middle_ref[...] + grad_norm).astype(LOW)
    result_ref[...] = result
    turned = jnp.dot(result, natural_ref[...], preferred_element_type=jnp.float32)
    natural_out_ref[...] = turned.astype(LOW)
    for copy in crossed + passed:
        copy.wait_send()
    tiles.wait()
    gains.wait()
    if layer == 0:
        finish()


def first_crossed(lhs_all, ahead, section, place, over_core, over_y):
    mlp_all, given_out, lhs_ref, rhs_ref, given_ref, local_sem, near_sem, peer_sem, far_sem = ahead
    other = 1 - section
    core = lax.rem(place, 2)
    tokens = lhs_all.shape[3]
    piece = lhs_all.shape[2] // 8

    def remote(send_sem, recv_sem, source, target, device):
        copy = pltpu.make_async_remote_copy(
            src_ref=source,
            dst_ref=target,
            send_sem=send_sem,
            recv_sem=recv_sem,
            device_id=device,
            device_id_type=MESH_ID,
        )
        copy.start()
        return copy

    pairs, peers = [], []
    for p in range(4):
        mine = lhs_all.at[other, 2, pl.ds((2 * p + core) * piece, piece), :]
        theirs = lhs_all.at[other, 2, pl.ds((2 * p + 1 - core) * piece, piece), :]
        pairs.append((mine, lhs_ref.at[pl.ds(p * piece, piece), pl.ds(0, tokens)]))
        target = lhs_ref.at[pl.ds((p ^ 1) * piece, piece), pl.ds(tokens, tokens)]
        peers.append(remote(near_sem.at[p], peer_sem.at[p], theirs, target, over_core))
    for t in range(2):
        pairs.append((mlp_all.at[other, t], rhs_ref.at[t, pl.ds(0, tokens)]))
        target = rhs_ref.at[t, pl.ds(tokens, tokens)]
        sems = (near_sem.at[4 + t], peer_sem.at[4 + t])
        peers.append(remote(*sems, mlp_all.at[other, t], target, over_core))
    copies = copies_of(local_sem, pairs)
    for copy in copies:
        copy.wait()
    for copy in peers:
        copy.wait_recv()
    sent = []
    for t in range(2):
        value = jnp.dot(lhs_ref[...], rhs_ref[t], preferred_element_type=jnp.float32)
        given_ref[t] = value.astype(LOW)
        sems = (far_sem.at[0, t], far_sem.at[1, t])
        sent.append(remote(*sems, given_ref.at[t], given_out.at[t], over_y))

    def finish():
        for copy in peers:
            copy.wait_send()
        for copy in sent:
            copy.wait()

    return finish


def call_mixed_backward(
    layer, dq_t, dk_t, dv_t, hidden, grad_middle, grad_gain, shared, angles, stores
):
    weights, gain_rows, natural = shared
    rows = hidden.shape[0]
    steps = QKV // TILE + 1
    mixed, mixed_shape = stored(stores, "mixed", (2, steps, rows, TILE))
    extra = [stores["lhs"]] if mixed is None else [stores["lhs"], mixed]
    aliases = {11: 1} if mixed is None else {11: 1, 12: 0}
    ahead = [stores["mlp"]] if layer == 0 else []
    half = D // 2
    ahead_shape = [jax.ShapeDtypeStruct((2, half, TILE), LOW)] if layer == 0 else []
    ahead_scratch = [
        pltpu.VMEM((half, 2 * rows), LOW),
        pltpu.VMEM((2, 2 * rows, TILE), LOW),
        pltpu.VMEM((2, half, TILE), LOW),
        pltpu.SemaphoreType.DMA((6,)),
        pltpu.SemaphoreType.DMA((6,)),
        pltpu.SemaphoreType.DMA((6,)),
        pltpu.SemaphoreType.DMA((2, 2)),
    ]
    in_vmem = pl.BlockSpec(memory_space=pltpu.VMEM)
    dma = pltpu.SemaphoreType.DMA
    part = (2, KV, HD, rows)
    mixed, lhs, result, turned, *given = pl.pallas_call(
        functools.partial(mixed_backward_kernel, layer),
        in_specs=[in_vmem] * 6 + [ANYWHERE] * (5 + len(extra) + len(ahead)),
        out_specs=[ANYWHERE, ANYWHERE, in_vmem, in_vmem] + [ANYWHERE] * len(ahead),
        out_shape=[
            mixed_shape,
            jax.ShapeDtypeStruct(stores["lhs"].shape, LOW),
            jax.ShapeDtypeStruct((rows, D), LOW),
            jax.ShapeDtypeStruct((rows, D), LOW),
            *ahead_shape,
        ],
        scratch_shapes=[
            pltpu.VMEM((D, weights[0].shape[2]), LOW),
            pltpu.VMEM((D, rows), jnp.float32),
            pltpu.VMEM((steps, rows, TILE), LOW),
            pltpu.VMEM((D, rows), LOW),
            pltpu.VMEM((2, *part), LOW),
            pltpu.VMEM(part, LOW),
            pltpu.VMEM(part, LOW),
            pltpu.VMEM((QD, rows), jnp.float32),
            pltpu.VMEM((rows, D), LOW),
            pltpu.VMEM((rows, D), jnp.float32),
            pltpu.VMEM((D, D), LOW),
            dma((6,)),
            dma((6,)),
            dma((3,)),
            dma((5,)),
        ]
        + ahead_scratch * len(ahead),
        input_output_aliases=aliases,
        compiler_params=pltpu.CompilerParams(
            collective_id=4 + layer, has_side_effects=True, vmem_limit_bytes=62 * 2**20
        ),
        cost_estimate=long_cost(30),
    )(
        dk_t,
        dv_t,
        gain_rows,
        grad_gain,
        *angles,
        dq_t,
        hidden,
        grad_middle,
        natural,
        weights[0],
        *extra,
        *ahead,
    )
    stores.update(lhs=lhs, mixed=mixed)
    if given:
        stores["given"] = given[0]
    return result, turned


def pair_backward(layer, grad_low, shared, saved, info, angles, stores, beside):
    grad_middle, do_t, grad_gain = call_mlp_backward(
        layer, grad_low, saved, shared[0], shared[1], stores
    )
    dq_t, dk_t, dv_t = pair_attention_backward(
        info, saved["q_t"], do_t, saved["o_t"], saved["lse"], saved["kv_t"]
    )
    dq_t, beside = lax.optimization_barrier((dq_t, beside))
    result, turned = call_mixed_backward(
        layer, dq_t, dk_t, dv_t, saved["hidden"], grad_middle, grad_gain, shared, angles, stores
    )
    return result, turned, beside


TILE = 384
CROSSED = 22
PLANE = 11


def spread_kernel(
    lhs_all,
    mlp_all,
    mixed_all,
    units_all,
    attended_all,
    grad_ref,
    given_all,
    in_out,
    head_out,
    mlp_out,
    down_out,
    gains_out,
    grad_out,
    mlp_peer,
    mixed_peer,
    units_peer,
    attended_peer,
    lhs_ref,
    rhs_ref,
    given_ref,
    sum_ref,
    side_ref,
    block_ref,
    last_given,
    last_ref,
    hold_ref,
    kept_ref,
    grad_sem,
    early_sem,
    lhs_sem,
    peer_send,
    peer_recv,
    load_sem,
    given_send,
    given_recv,
    side_send,
    side_recv,
    block_send,
    block_recv,
    last_send,
    last_recv,
):
    section = lax.axis_index(SECTION)
    column = lax.axis_index(CTX)
    place = lax.axis_index(WSH)
    other = 1 - section
    over_x = (section, column, lax.rem(place + 2, 4))
    over_y = (other, column, place)
    over_core = (section, column, place + 1 - 2 * lax.rem(place, 2))
    flip_low = column + 1 - 2 * lax.rem(column, 2)
    flip_high = lax.rem(column + 2, 4)
    flip_both = lax.rem(flip_low + 2, 4)
    over_z = [(section, c, place) for c in (flip_low, flip_high, flip_both)]
    origin = place ^ column

    barrier = pltpu.get_barrier_semaphore()
    for target in (over_x, over_y, over_core, *over_z):
        pl.semaphore_signal(barrier, inc=1, device_id=target, device_id_type=MESH_ID)
    moving, partner_column, partner_place = stream_partner(column, place)
    staying = jnp.logical_not(moving)

    @pl.when(moving)
    def _():
        for target in (section, other):
            pl.semaphore_signal(
                barrier,
                inc=1,
                device_id=(target, partner_column, partner_place),
                device_id_type=MESH_ID,
            )
        pl.semaphore_wait(barrier, 8)

    @pl.when(staying)
    def _():
        pl.semaphore_wait(barrier, 6)

    half = lhs_all.shape[2] // 2
    tokens = lhs_all.shape[3]
    quarter = half // 2
    share = quarter // 4
    layers = (section, other)

    def remote(source, target, send_sem, recv_sem, device):
        return pltpu.make_async_remote_copy(
            src_ref=source,
            dst_ref=target,
            send_sem=send_sem,
            recv_sem=recv_sem,
            device_id=device,
            device_id_type=MESH_ID,
        )

    core = lax.rem(place, 2)
    side = place // 2
    piece = half // 4

    def grad_copy(slot, device):
        return remote(
            grad_ref, grad_out.at[slot], grad_sem.at[0], grad_sem.at[1 + slot], device
        )

    hold_in = pltpu.make_async_copy(grad_ref, hold_ref, grad_sem.at[3])
    hold_out = pltpu.make_async_copy(hold_ref, grad_out.at[0], grad_sem.at[3])

    def grad_start():
        @pl.when(moving & (section == 0))
        def _():
            grad_copy(0, (0, partner_column, partner_place)).start()

        @pl.when(staying & (section == 0))
        def _():
            hold_in.start()
            hold_in.wait()
            hold_out.start()

    def grad_cross():
        @pl.when(moving & (section == 1))
        def _():
            grad_copy(1, (0, partner_column, partner_place)).start()

        @pl.when(staying & (section == 1))
        def _():
            grad_copy(1, over_y).start()

    def grad_finish():
        @pl.when(section == 0)
        def _():
            grad_copy(1, over_y).wait_recv()

        @pl.when(moving & (section == 0))
        def _():
            grad_copy(0, over_y).wait_recv()

        @pl.when(moving | (section == 1))
        def _():
            grad_copy(0, over_y).wait_send()

        @pl.when(staying & (section == 0))
        def _():
            hold_out.wait()

    def lhs_copies(group):
        kinds = (pl.ds(2, 1), pl.ds(0, 1), pl.ds(1, 1), pl.ds(3, 2))[group]
        copies = []
        for which in (1, 0):
            for p in range(4):
                index = which * 4 + p
                copies.append(
                    pltpu.make_async_copy(
                        lhs_all.at[layers[which], kinds, pl.ds((2 * p + core) * piece, piece), :],
                        lhs_ref.at[which, kinds, pl.ds(p * piece, piece), pl.ds(0, tokens)],
                        lhs_sem.at[group, 0, index],
                    )
                )
                span = pl.ds((2 * p + 1 - core) * piece, piece)
                copies.append(
                    remote(
                        lhs_all.at[layers[which], kinds, span, :],
                        lhs_ref.at[
                            which, kinds, pl.ds((p ^ 1) * piece, piece), pl.ds(tokens, tokens)
                        ],
                        lhs_sem.at[group, 1, index],
                        lhs_sem.at[group, 2, index],
                        over_core,
                    )
                )
        return copies

    sources = (
        (mlp_all, mlp_peer, lambda tile: tile),
        (mixed_all, mixed_peer, lambda tile: tile - 16),
        (units_all, units_peer, lambda tile: tile - CROSSED),
        (attended_all, attended_peer, lambda tile: tile - CROSSED - 8),
    )

    def peer_copy(which, tile, source):
        mine, theirs, place_of = sources[source]
        return remote(
            mine.at[layers[which], place_of(tile)],
            theirs.at[layers[which], place_of(tile)],
            peer_send.at[which, tile],
            peer_recv.at[which, tile],
            over_core,
        )

    def peer_wait(which, tile):
        return remote(
            mlp_all.at[layers[which], 0],
            mlp_peer.at[layers[which], 0],
            peer_send.at[which, tile],
            peer_recv.at[which, tile],
            over_core,
        )

    def peer_starts(crossed, which, i):
        for early in (True, False):

            @pl.when(((i < 8) == early) & (i < PLANE))
            def _():
                late = 1 - early
                if crossed:
                    peer_copy(which, 2 * i, late).start()
                    peer_copy(which, 2 * i + 1, late).start()
                else:
                    peer_copy(1, CROSSED + i, 2 + late).start()
                    peer_copy(0, CROSSED + i, 2 + late).start()

    def loads(slot, which, tile, source):
        mine, theirs, place_of = sources[source]
        return (
            pltpu.make_async_copy(
                mine.at[layers[which], place_of(tile)],
                rhs_ref.at[slot, pl.ds(0, tokens)],
                load_sem.at[slot, 0],
            ),
            pltpu.make_async_copy(
                theirs.at[layers[which], place_of(tile)],
                rhs_ref.at[slot, pl.ds(tokens, tokens)],
                load_sem.at[slot, 1],
            ),
        )

    def load_start(slot, which, tile, source, early):
        peer_wait(which, tile).wait_recv()
        for flag in (True, False):

            @pl.when(early == flag)
            def _():
                for copy in loads(slot, which, tile, source + 1 - flag):
                    copy.start()

    def product(slot, which, tile, kind):
        for copy in loads(slot, which, 0, 0):
            copy.wait()
        return jnp.dot(
            lhs_ref[which, kind], rhs_ref[slot], preferred_element_type=jnp.float32
        )

    def crossed_kind(tile):
        return jnp.where(tile < 16, 2, jnp.where(tile < 21, 3, 4))

    def plane_kind(i):
        return jnp.where(i < 8, 0, 1)

    def sorted_sides(value):
        blocks = value.reshape(4, 2, share, TILE)
        first, second = blocks[:, 0], blocks[:, 1]
        low = jnp.broadcast_to(side == 0, first.shape)
        away = jnp.where(low, second, first).reshape(quarter, TILE)
        kept = jnp.where(low, first, second).reshape(quarter, TILE)
        return jnp.concatenate([away, kept], axis=0).astype(LOW)

    def given_copy(tile):
        slot = lax.rem(tile, 4)
        return remote(
            given_ref.at[slot],
            sum_ref.at[tile],
            given_send.at[slot],
            given_recv.at[tile],
            over_y,
        )

    def side_copy(unit):
        return remote(
            sum_ref.at[unit, pl.ds(0, quarter)],
            side_ref.at[unit // 2, pl.ds(lax.rem(unit, 2) * quarter, quarter)],
            side_send.at[unit],
            side_recv.at[unit],
            over_x,
        )

    def block_span(k):
        return pl.ds(pl.multiple_of((origin ^ k) * 2 * share, 2 * share), 2 * share)

    def block_copy(pair, k):
        return remote(
            side_ref.at[pair, block_span(k + 1)],
            block_ref.at[pair, k],
            block_send.at[pair, k],
            block_recv.at[pair, k],
            over_z[1 if k == 1 else 0],
        )

    def last_copy(i):
        return remote(
            last_given.at[i], last_ref.at[i], last_send.at[i], last_recv.at[i], over_y
        )

    def combine(pair):
        parts = []
        for e in range(2):
            unit = 2 * pair + e
            side_copy(unit).wait_recv()
            kept = sum_ref[unit, pl.ds(quarter, quarter)].astype(jnp.float32)
            got = side_ref[pair, pl.ds(e * quarter, quarter)].astype(jnp.float32)
            got = jnp.concatenate([got[quarter // 2 :], got[: quarter // 2]], axis=0)
            parts.append((kept + got).reshape(4, share, TILE))
        both = jnp.concatenate(parts, axis=1).reshape(8 * share, TILE)
        side_ref[pair] = both.astype(LOW)
        block_copy(pair, 2).start()
        block_copy(pair, 0).start()

    def relay(pair):
        for k, block in ((2, 2), (0, 0)):
            block_copy(pair, k).wait_recv()
            span = block_span(block)
            total = side_ref[pair, span].astype(jnp.float32)
            total = total + block_ref[pair, k].astype(jnp.float32)
            side_ref[pair, span] = total.astype(LOW)
            if k == 2:
                block_copy(pair, 1).start()

    def settle(pair):
        block_copy(pair, 1).wait_recv()
        total = side_ref[pair, block_span(0)].astype(jnp.float32)
        total = total + block_ref[pair, 1].astype(jnp.float32)
        return total[:share], total[share:]

    early_copies = copies_of(early_sem, [(given_all.at[t], sum_ref.at[t]) for t in range(2)])
    for copy in lhs_copies(0):
        copy.start()
    peer_starts(True, 1, 1)
    peer_starts(False, 0, 0)
    peer_starts(True, 0, 0)
    for group in (1, 2, 3):
        for copy in lhs_copies(group):
            copy.start()
    grad_start()
    for copy in lhs_copies(0):
        copy.wait()
    for copy in early_copies:
        copy.wait()

    def within(i, low=0):
        return (i >= low) & (i < low + PLANE)

    def step(i, carry):
        peer_starts(True, 1, i + 2)
        peer_starts(False, 0, i + 1)
        peer_starts(True, 0, i + 1)

        for group, when in ((1, 0), (2, 6), (3, 6)):

            @pl.when(i == when)
            def _():
                for copy in lhs_copies(group):
                    copy.wait()

        @pl.when(i + 1 < PLANE)
        def _():
            j = i + 1
            load_start(0, 1, 2 * j, 0, j < 8)
            load_start(1, 1, 2 * j + 1, 0, j < 8)
            for e in range(2):
                tile = 2 * j + e
                value = product(e, 1, tile, crossed_kind(tile))

                @pl.when(j >= 3)
                def _():
                    given_copy(tile - 4).wait_send()

                given_ref[lax.rem(tile, 4)] = value.astype(LOW)
                given_copy(tile).start()

        @pl.when(i < PLANE)
        def _():
            load_start(2, 1, CROSSED + i, 2, i < 8)
            load_start(0, 0, CROSSED + i, 2, i < 8)
            for e in range(2):
                unit = CROSSED + 2 * i + e
                value = product(2 - 2 * e, 1 - e, CROSSED + i, plane_kind(i))
                sum_ref[unit] = sorted_sides(value)
                side_copy(unit).start()

        @pl.when(within(i, 1))
        def _():
            combine(PLANE + i - 1)

        @pl.when(i < PLANE)
        def _():
            load_start(1, 0, 2 * i, 0, i < 8)
            load_start(2, 0, 2 * i + 1, 0, i < 8)
            for e in range(2):
                tile = 2 * i + e
                value = product(1 + e, 0, tile, crossed_kind(tile))

                @pl.when(i > 0)
                def _():
                    given_copy(tile).wait_recv()

                sum_ref[tile] = sorted_sides(value + sum_ref[tile].astype(jnp.float32))
                side_copy(tile).start()

        @pl.when(i == PLANE - 3)
        def _():
            grad_cross()

        @pl.when(within(i, 2))
        def _():
            j = i - 2
            given, kept = settle(PLANE + j)
            kept_ref[j] = kept
            last_given[j] = jnp.concatenate(
                [given, jnp.zeros((last_given.shape[1] - share, TILE), jnp.float32)], axis=0
            ).astype(LOW)
            last_copy(j).start()

        @pl.when(within(i, 1))
        def _():
            combine(i - 1)
            relay(PLANE + i - 1)
            relay(i - 1)

        @pl.when(within(i, 2))
        def _():
            j = i - 2
            tiles = settle(j)

            def columns(base):
                return pl.ds(pl.multiple_of(base * TILE, TILE), TILE)

            @pl.when(j < 8)
            def _():
                for e in range(2):
                    mlp_out[:, columns(8 * e + j)] = tiles[e]

            @pl.when(j >= 8)
            def _():
                in_out[:, columns(2 * (j - 8))] = tiles[0]

            @pl.when((j >= 8) & (j < 10))
            def _():
                in_out[:, columns(2 * (j - 8) + 1)] = tiles[1]

            @pl.when(j == 10)
            def _():
                gains_out[...] = tiles[1][:, :SIDE].T[:8]

        @pl.when(within(i, 3))
        def _():
            j = i - 3

            def columns(base):
                return pl.ds(pl.multiple_of(base * TILE, TILE), TILE)

            last_copy(j).wait_recv()
            total = (kept_ref[j] + last_ref[j].astype(jnp.float32)[:share]).T

            @pl.when(j < 8)
            def _():
                down_out[columns(j), :] = total

            @pl.when(j >= 8)
            def _():
                head_out[columns(j - 8), :] = total

        return carry

    lax.fori_loop(0, PLANE + 3, step, 0)

    def drain(i, carry):
        for e in range(4):
            side_copy(4 * i + e).wait_send()
        for e in range(2):
            for k in range(3):
                block_copy(2 * i + e, k).wait_send()
        last_copy(i).wait_send()
        for tile in (2 * i, 2 * i + 1, CROSSED + i):
            peer_wait(0, tile).wait_send()

        @pl.when(i > 0)
        def _():
            for tile in (2 * i, 2 * i + 1):
                peer_wait(1, tile).wait_send()

        peer_wait(1, CROSSED + i).wait_send()
        return carry

    lax.fori_loop(0, PLANE, drain, 0)
    grad_finish()
    for e in range(4):
        given_copy(2 * PLANE - 4 + e).wait_send()


def spread_all(lhs, mlp, mixed, units, attended, given, grad):
    tiles = 3 * PLANE
    half = lhs.shape[2] // 2
    share = half // 8
    tokens = lhs.shape[3]
    sources = (mlp, mixed, units, attended)
    dma = pltpu.SemaphoreType.DMA
    anywhere = pl.BlockSpec(memory_space=pl.ANY)
    return pl.pallas_call(
        spread_kernel,
        out_shape=[
            jax.ShapeDtypeStruct((share, QKV), jnp.float32),
            jax.ShapeDtypeStruct((QD, share), jnp.float32),
            jax.ShapeDtypeStruct((share, 2 * FF), jnp.float32),
            jax.ShapeDtypeStruct((FF, share), jnp.float32),
            jax.ShapeDtypeStruct((8, share), jnp.float32),
            jax.ShapeDtypeStruct((2, *grad.shape), LOW),
            *[jax.ShapeDtypeStruct(v.shape, LOW) for v in sources],
        ],
        in_specs=[anywhere] * 7,
        out_specs=[pl.BlockSpec(memory_space=pltpu.VMEM)] * 5 + [anywhere] * 5,
        scratch_shapes=[
            pltpu.VMEM((2, lhs.shape[1], half, 2 * tokens), LOW),
            pltpu.VMEM((3, 2 * tokens, TILE), LOW),
            pltpu.VMEM((4, half, TILE), LOW),
            pltpu.VMEM((4 * PLANE, half, TILE), LOW),
            pltpu.VMEM((2 * PLANE, half, TILE), LOW),
            pltpu.VMEM((2 * PLANE, 3, 2 * share, TILE), LOW),
            pltpu.VMEM((PLANE, share + 8, TILE), LOW),
            pltpu.VMEM((PLANE, share + 8, TILE), LOW),
            pltpu.VMEM(grad.shape, LOW),
            pltpu.VMEM((PLANE, share, TILE), jnp.float32),
            dma((4,)),
            dma((2,)),
            dma((4, 3, 8)),
            dma((2, tiles)),
            dma((2, tiles)),
            dma((3, 2)),
            dma((4,)),
            dma((CROSSED,)),
            dma((4 * PLANE,)),
            dma((4 * PLANE,)),
            dma((2 * PLANE, 3)),
            dma((2 * PLANE, 3)),
            dma((PLANE,)),
            dma((PLANE,)),
        ],
        compiler_params=pltpu.CompilerParams(
            collective_id=2, has_side_effects=True, vmem_limit_bytes=62 * 2**20
        ),
        cost_estimate=long_cost(250),
    )(lhs, *sources, grad, given)[:6]


def on_device_pairs(
    x_in, cotangent, w_qkv, w_out, w_gate_up, w_down, gains, order, visible, seq_ids
):
    section = lax.axis_index(SECTION)
    column = lax.axis_index(CTX)
    place = lax.axis_index(WSH)
    core = place % 2
    side = place // 2
    rows = x_in.shape[2]
    quarter = D // 4
    share = quarter // 4
    slot = column % 2 + 2 * core
    first_section = section == 0

    def partner(index):
        z, w = index // 4, index % 4
        if (z < 2) == (w % 2 == 1):
            return ((z + 2) % 4) * 4 + (w ^ 1)
        return index

    pairs = [(i, partner(i)) for i in range(16)]
    moving = (column < 2) == (core == 1)

    def placed(value, layer):
        crossing = [((1 - layer) * 16 + i, layer * 16 + j) for i, j in pairs]
        other = lax.ppermute(value, (SECTION, CTX, WSH), crossing)
        inside = [(layer * 16 + i, layer * 16 + j) for i, j in pairs if i != j]
        return lax.ppermute(value, (SECTION, CTX, WSH), inside), value, other

    def chosen(first, second):
        return jnp.where(first_section, first, second)

    def sorted_rows(value):
        blocks = value.reshape(2, 2, share, value.shape[1])
        return blocks.transpose(1, 0, 2, 3).reshape(value.shape)

    gain_columns = jnp.concatenate(
        [gains[0].T, jnp.zeros((quarter, SIDE - gains.shape[1]), LOW)], axis=1
    )
    shards = [
        sorted_rows(jnp.concatenate([w_qkv[0], gain_columns], axis=1)),
        sorted_rows(w_out[0].T),
        sorted_rows(w_gate_up[0]),
        sorted_rows(w_down[0].T),
    ]
    angles = pair_angles(order[section, slot], rows)
    weights, saved_one, ahead, stores, info, gain_rows, early, natural = first_layer(
        x_in, shards, seq_ids, angles, order, visible
    )
    upstream = cotangent[section, 0]
    crossing = [(i, j) for i, j in pairs if i != j]
    upstream, early = lax.optimization_barrier((upstream, early))
    upstream = jnp.where(moving, lax.ppermute(upstream, (CTX, WSH), crossing), upstream)
    grad_low = contract(upstream, natural, 1, 1).astype(LOW)
    saved_two = pair_forward(1, ahead, weights, gain_rows, info, stores)
    late = contract(saved_two["result"], natural, 1, 0).astype(LOW)

    own, away = chosen(early, late), chosen(late, early)
    swaps = [(s * 16 + i, (1 - s) * 16 + j) for s in range(2) for i, j in pairs]
    other = lax.ppermute(away, (SECTION, CTX, WSH), swaps)
    mine = lax.ppermute(own, (CTX, WSH), crossing)
    shared = (weights, gain_rows, natural)
    grad_two, turned, unused = pair_backward(
        1, grad_low, shared, saved_two, info, angles, stores, early
    )
    grad_two, turned, mine, other = lax.optimization_barrier((grad_two, turned, mine, other))
    mine = jnp.where(moving, mine, own)
    activations = jnp.stack([chosen(mine, other), chosen(other, mine)])
    later = placed(turned, 1)
    grad_one, turned, later = pair_backward(
        0, grad_two, shared, saved_one, info, angles, stores, later
    )
    names = ("lhs", "mlp", "mixed", "units", "attended", "given")
    *shares, earlier = spread_all(*[stores[k] for k in names], turned)
    later = (later[2], jnp.where(moving, later[0], later[1]))
    input_grads = jnp.stack([chosen(earlier[m], later[m]).astype(jnp.float32) for m in range(2)])

    share_in, share_head, share_mlp, share_down, share_gains = shares
    return (
        activations[None, :, None],
        input_grads[None, :, None],
        share_in[None],
        share_head[None],
        share_mlp[None],
        share_down[None],
        share_gains[None, :2],
    )


def solution(mesh):
    in_specs = (
        P(None, "wsh", "ctx", None),
        P(None, "wsh", "ctx", None),
        P("section", "wsh", None),
        P("section", None, "wsh"),
        P("section", "wsh", None),
        P("section", None, "wsh"),
        P("section", None, "wsh"),
        P(),
        P(),
        P(None, "wsh", None),
    )
    out_specs = (
        P("section", None, "wsh", "ctx", None),
        P("section", None, "wsh", "ctx", None),
        P("section", ("ctx", "wsh"), None),
        P("section", None, ("ctx", "wsh")),
        P("section", ("ctx", "wsh"), None),
        P("section", None, ("ctx", "wsh")),
        P("section", None, ("ctx", "wsh")),
    )
    body = on_device_pairs if fits_pairs(mesh) else on_device_general
    return jax.shard_map(
        body, mesh=mesh, in_specs=in_specs, out_specs=out_specs, check_vma=False
    )
```
